32 devices in a mesh: frame: 16 (over z, x, core), space: 2 (over y).
Axes of the slice: x: 2, y: 2, z: 4, core: 2. Of those that a mesh axis runs over, the one named last changes fastest.
Arguments:
- queries: bfloat16 [2560, 3072], P('frame', 'space'), may hold values from -24 to 24
- keys: bfloat16 [2560, 3072], P('frame', 'space'), may hold values from -24 to 24
- values: bfloat16 [2560, 3072], P('frame', 'space'), may hold values from -6 to 6
- grad_out: bfloat16 [2560, 3072], P('frame', 'space'), may hold values from -24 to 24
- proj_weight: bfloat16 [3072, 3072], P('space', 'frame'), may hold values from -0.109375 to 0.109375
Outputs:
- grad_queries: bfloat16 [2560, 3072], P('frame', 'space')
- grad_keys: bfloat16 [2560, 3072], P('frame', 'space')
- grad_values: bfloat16 [2560, 3072], P('frame', 'space')
- grad_proj: float32 [3072, 3072], P('space', 'frame')
The draws below stay inside these ranges and needn't reach their ends.
All inputs are finite; a program needn't handle non-finite values.
Results may differ from the reference program's by a relative error of at most 0.03.
Values may be sent and summed in bfloat16 or wider, within the bound.
No kernel may reach another device: no remote copies, remote signals or barrier semaphores. Data moves between devices by JAX's collectives and lax.ppermute only.
A program may use at most 128 MiB of HBM per device.

```python
import jax
import jax.numpy as jnp
from jax import lax

D = 3072
H = 24
HD = 128
L = 2560
N_FRAME = 16


def query_key_pair(key):
    key_q, key_k = jax.random.split(jax.random.fold_in(key, 7177), 2)
    shape = (L, H * HD)
    query_draw = 1.5 * jax.random.truncated_normal(key_q, -6.0, 6.0, shape, jnp.float32)
    key_draw = 1.5 * jax.random.truncated_normal(key_k, -6.0, 6.0, shape, jnp.float32)
    return (query_draw, key_draw)


def draw_queries(key, part):
    return query_key_pair(key)[0].astype(jnp.bfloat16)


def draw_keys(key, part):
    return query_key_pair(key)[1].astype(jnp.bfloat16)


def level_of(stream_key, dims, cuts, low, top_value):
    factor_of = 1.0
    for position, shards_of in cuts:
        heights = jax.random.uniform(jax.random.fold_in(jax.random.fold_in(stream_key, 6), position), (shards_of,), jnp.float32, low / len(cuts), top_value / len(cuts))
        factor_of = factor_of * jnp.repeat(jnp.exp(heights), dims[position] // shards_of).reshape((-1,) + (1,) * (len(dims) - 1 - position))
    return factor_of


def centred(own_key, dims, deviation, reach, cuts=(), held_as=jnp.bfloat16):
    result = jax.random.normal(own_key, dims, jnp.float32) * deviation
    if len(cuts) > 0:
        result = level_of(own_key, dims, cuts, -0.22, 0.18) * result
    return jnp.clip(result, min=-reach, max=reach).astype(held_as)


def setup_inputs(seed: int = 0) -> dict:
    seeds = jax.random.split(jax.random.key(seed), 6)
    queries = draw_queries(jax.random.fold_in(seeds[5], 71), 0)
    keys = draw_keys(jax.random.fold_in(seeds[5], 71), 0)
    values = centred(seeds[2], (L, H * HD), 1.0, 6.0, ((0, 16), (1, 2)))
    grad_out = centred(seeds[3], (L, D), 4.0, 24.0, ((0, 16), (1, 2)))
    proj_weight = centred(seeds[4], (H * HD, D), (H * HD) ** -0.5, 0.109375, ((0, 2), (1, 16)))
    return {"queries": queries, "keys": keys, "values": values, "grad_out": grad_out, "proj_weight": proj_weight}


def head_grads(inputs):
    query_h, key_h, value_h, grad_h = inputs
    factor = 1.0 / jnp.sqrt(jnp.float32(HD))
    seq_len = query_h.shape[0]
    group_rows = seq_len // N_FRAME
    logits = jnp.dot(query_h, key_h.T, preferred_element_type=jnp.float32) * factor
    row_max = lax.optimization_barrier(jnp.max(logits, axis=1, keepdims=True))
    log_norm = row_max + jnp.log(lax.optimization_barrier(jnp.sum(jnp.exp(logits - row_max), axis=1, keepdims=True)))
    probs = jnp.exp(logits - log_norm)
    probs_low = probs.astype(jnp.bfloat16)
    attn_out = jnp.dot(probs_low, value_h, preferred_element_type=jnp.float32).astype(jnp.bfloat16)
    row_delta = lax.optimization_barrier(jnp.sum(grad_h.astype(jnp.float32) * attn_out.astype(jnp.float32), axis=1, keepdims=True))
    grad_probs = jnp.dot(grad_h, value_h.T, preferred_element_type=jnp.float32)
    grad_logits = (probs * (grad_probs - row_delta)).astype(jnp.bfloat16)
    grad_query = (factor * jnp.dot(grad_logits, key_h, preferred_element_type=jnp.float32)).astype(jnp.bfloat16)
    grouped_logits = grad_logits.reshape(N_FRAME, group_rows, seq_len).astype(jnp.float32)
    grouped_probs = probs_low.reshape(N_FRAME, group_rows, seq_len).astype(jnp.float32)
    grouped_query = query_h.reshape(N_FRAME, group_rows, HD).astype(jnp.float32)
    grouped_grad = grad_h.reshape(N_FRAME, group_rows, HD).astype(jnp.float32)
    key_part = (factor * jnp.einsum('gqk,gqd->gkd', grouped_logits, grouped_query)).astype(jnp.bfloat16)
    value_part = jnp.einsum('gqk,gqd->gkd', grouped_probs, grouped_grad).astype(jnp.bfloat16)
    key_part = lax.optimization_barrier(key_part)
    value_part = lax.optimization_barrier(value_part)
    grad_key = lax.optimization_barrier(jnp.sum(key_part.astype(jnp.float32), axis=0)).astype(jnp.bfloat16)
    grad_value = lax.optimization_barrier(jnp.sum(value_part.astype(jnp.float32), axis=0)).astype(jnp.bfloat16)
    return (attn_out, grad_query, grad_key, grad_value)

def by_heads(matrix):
    return matrix.reshape(matrix.shape[0], H, HD).transpose(1, 0, 2)

def to_rows(stacked):
    return stacked.transpose(1, 0, 2).reshape(stacked.shape[1], H * HD)

def reference(queries, keys, values, grad_out, proj_weight):
    grad_attn = jnp.dot(grad_out, proj_weight.T, preferred_element_type=jnp.float32).astype(jnp.bfloat16)
    attn_out, grad_query, grad_key, grad_value = lax.map(head_grads, (by_heads(queries), by_heads(keys), by_heads(values), by_heads(grad_attn)))
    attn_rows = to_rows(attn_out)
    grad_proj = jnp.dot(attn_rows.T, grad_out, preferred_element_type=jnp.float32)
    return (to_rows(grad_query), to_rows(grad_key), to_rows(grad_value), grad_proj)
```

```python
import functools
import math

import jax
import jax.numpy as jnp
from jax import lax
from jax.experimental import pallas as pl
from jax.experimental.pallas import tpu as pltpu
from jax.sharding import PartitionSpec as P

HD = 128
VMEM_BYTES = 50 * 1024 * 1024
BF16 = jnp.bfloat16
F32 = jnp.float32


def bits_of(count):
    found = []
    bit = 1
    while bit < count:
        found.append(bit)
        bit *= 2
    return found


def relative_of(position, bits):
    total = 0
    for place, bit in enumerate(reversed(bits)):
        if position >> place & 1:
            total |= bit
    return total


def shift_pairs(n_groups, n_tok, step):
    return [
        (g * n_tok + t, (g + step) % n_groups * n_tok + t)
        for g in range(n_groups)
        for t in range(n_tok)
    ]


def xor_pairs(count, bit):
    return [(i, i ^ bit) for i in range(count)]


def gather_bits(block, axis, count, bits):
    for bit in reversed(bits):
        other = lax.ppermute(block, axis, xor_pairs(count, bit))
        block = jnp.concatenate([block, other], axis=0)
    return block


def scatter_bits(block, axis, count, bits):
    for bit in bits:
        half = block.shape[0] // 2
        other = lax.ppermute(block[half:], axis, xor_pairs(count, bit))
        block = (block[:half].astype(F32) + other.astype(F32)).astype(BF16)
    return block


def params():
    return pltpu.CompilerParams(vmem_limit_bytes=VMEM_BYTES)


def smem():
    return pl.BlockSpec(memory_space=pltpu.SMEM)


def vmem():
    return pl.BlockSpec(memory_space=pltpu.VMEM)


def aligned(value, unit):
    return pl.multiple_of(value, unit)


def dot(a, b, dims):
    return lax.dot_general(a, b, (dims, ((), ())), preferred_element_type=F32)


def pack_kernel(n_groups, ids, q, k, v, w, *outs):
    group_width = q.shape[1] // n_groups
    for s in range(n_groups):
        dest = lax.rem(ids[0] + s, n_groups)
        start = dest * group_width
        cols = pl.ds(aligned(start, HD), group_width)
        outs[s][...] = q[:, cols]
        for h in range(group_width // HD):
            head = pl.ds(aligned(start + h * HD, HD), HD)
            outs[n_groups + s][:, 2 * h * HD : (2 * h + 1) * HD] = k[:, head]
            outs[n_groups + s][:, (2 * h + 1) * HD : (2 * h + 2) * HD] = v[:, head]
        outs[2 * n_groups + s][...] = w[:, cols]


def pack(ids, q, k, v, w, n_groups):
    rows, width = q.shape
    gw = width // n_groups
    shapes = (
        [jax.ShapeDtypeStruct((rows, gw), BF16)] * n_groups
        + [jax.ShapeDtypeStruct((rows, 2 * gw), BF16)] * n_groups
        + [jax.ShapeDtypeStruct((w.shape[0], gw), BF16)] * n_groups
    )
    outs = pl.pallas_call(
        functools.partial(pack_kernel, n_groups),
        out_shape=shapes,
        in_specs=[smem()] + [vmem()] * 4,
        out_specs=[vmem()] * len(shapes),
        compiler_params=params(),
        name="pack",
    )(ids, q, k, v, w)
    return outs[:n_groups], outs[n_groups : 2 * n_groups], outs[2 * n_groups :]


def place_queries(n_groups, ids, pieces, scratch):
    rows = pieces[0].shape[0]
    for s in range(n_groups):
        src = lax.rem(ids[0] - s + n_groups, n_groups)
        scratch[pl.ds(aligned(src * rows, 16), rows), :] = pieces[s][...]


def forward_kernel(n_groups, chunk, scale, ids, *refs):
    pieces, (kv, p_out, o_out, il_out, q_all, logits) = refs[:n_groups], refs[n_groups:]
    seq_len = kv.shape[0]
    place_queries(n_groups, ids, pieces, q_all)
    q = q_all[...]
    top = None
    for c in range(0, seq_len, chunk):
        block = dot(kv[c : c + chunk, :HD], q, ((1,), (1,)))
        logits[c : c + chunk, :] = block
        here = jnp.max(block, axis=0, keepdims=True)
        top = here if top is None else jnp.maximum(top, here)
    top = top * scale
    total = jnp.zeros_like(top)
    out = jnp.zeros((HD, q.shape[0]), F32)
    for c in range(0, seq_len, chunk):
        prob = jnp.exp2(logits[c : c + chunk, :] * scale - top)
        total = total + jnp.sum(prob, axis=0, keepdims=True)
        low = prob.astype(BF16)
        p_out[0, c : c + chunk, :] = low
        out = out + dot(kv[c : c + chunk, HD:], low, ((0,), (0,)))
    inverse = 1.0 / total
    il_out[0] = inverse
    o_out[...] = (out * inverse).T.astype(BF16)


def forward(ids, pieces, kv, n_groups):
    rows, gw = pieces[0].shape
    heads = gw // HD
    n_q = rows * n_groups
    seq_len = kv.shape[0]
    chunk = math.gcd(seq_len, 512)
    scale = math.log2(math.e) / math.sqrt(HD)
    return pl.pallas_call(
        functools.partial(forward_kernel, n_groups, chunk, scale),
        grid=(heads,),
        out_shape=[
            jax.ShapeDtypeStruct((heads, seq_len, n_q), BF16),
            jax.ShapeDtypeStruct((n_q, gw), BF16),
            jax.ShapeDtypeStruct((heads, 1, n_q), F32),
        ],
        in_specs=[smem()]
        + [pl.BlockSpec((rows, HD), lambda h: (0, h))] * n_groups
        + [pl.BlockSpec((seq_len, 2 * HD), lambda h: (0, h))],
        out_specs=[
            pl.BlockSpec((1, seq_len, n_q), lambda h: (h, 0, 0)),
            pl.BlockSpec((n_q, HD), lambda h: (0, h)),
            pl.BlockSpec((1, 1, n_q), lambda h: (h, 0, 0)),
        ],
        scratch_shapes=[pltpu.VMEM((n_q, HD), BF16), pltpu.VMEM((seq_len, n_q), F32)],
        compiler_params=params(),
        cost_estimate=pl.CostEstimate(
            flops=4 * heads * seq_len * n_q * HD,
            bytes_accessed=2 * heads * seq_len * n_q,
            transcendentals=heads * seq_len * n_q,
        ),
        name="forward",
    )(ids, *pieces, kv)


def backward_kernel(n_groups, chunk, factor, ids, *refs):
    pieces = refs[:n_groups]
    kv, p_in, o_in, il_in, da_in = refs[n_groups : n_groups + 5]
    dq_outs = refs[n_groups + 5 : 2 * n_groups + 5]
    dkv_out, q_all, dq_all = refs[2 * n_groups + 5 :]
    seq_len = kv.shape[0]
    rows = pieces[0].shape[0]
    place_queries(n_groups, ids, pieces, q_all)
    q = q_all[...]
    n_q = q.shape[0]
    inverse = jnp.broadcast_to(il_in[0], (HD, n_q)).T
    da = (da_in[...].astype(F32) * inverse).astype(BF16)
    delta = jnp.sum((da.astype(F32) * o_in[...].astype(F32)).T, axis=0, keepdims=True)
    dq = jnp.zeros((HD, n_q), F32)
    for c in range(0, seq_len, chunk):
        low = p_in[0, c : c + chunk, :]
        dp = dot(kv[c : c + chunk, HD:], da, ((1,), (1,)))
        ds = (low.astype(F32) * (dp - delta)).astype(BF16)
        dkv_out[c : c + chunk, :HD] = (factor * dot(ds, q, ((1,), (0,)))).astype(BF16)
        dkv_out[c : c + chunk, HD:] = dot(low, da, ((1,), (0,))).astype(BF16)
        dq = dq + dot(kv[c : c + chunk, :HD], ds, ((0,), (0,)))
    dq_all[...] = (factor * dq).T.astype(BF16)
    for s in range(n_groups):
        src = lax.rem(ids[0] - s + n_groups, n_groups)
        dq_outs[s][...] = dq_all[pl.ds(aligned(src * rows, 16), rows), :]


def backward(ids, pieces, kv, probs, out, inverse, grad_attn, n_groups):
    rows, gw = pieces[0].shape
    heads = gw // HD
    n_q = rows * n_groups
    seq_len = kv.shape[0]
    chunk = math.gcd(seq_len, 512)
    outs = pl.pallas_call(
        functools.partial(backward_kernel, n_groups, chunk, 1.0 / math.sqrt(HD)),
        grid=(heads,),
        out_shape=[jax.ShapeDtypeStruct((rows, gw), BF16)] * n_groups
        + [jax.ShapeDtypeStruct((seq_len, 2 * gw), BF16)],
        in_specs=[smem()]
        + [pl.BlockSpec((rows, HD), lambda h: (0, h))] * n_groups
        + [
            pl.BlockSpec((seq_len, 2 * HD), lambda h: (0, h)),
            pl.BlockSpec((1, seq_len, n_q), lambda h: (h, 0, 0)),
            pl.BlockSpec((n_q, HD), lambda h: (0, h)),
            pl.BlockSpec((1, 1, n_q), lambda h: (h, 0, 0)),
            pl.BlockSpec((n_q, HD), lambda h: (0, h)),
        ],
        out_specs=[pl.BlockSpec((rows, HD), lambda h: (0, h))] * n_groups
        + [pl.BlockSpec((seq_len, 2 * HD), lambda h: (0, h))],
        scratch_shapes=[pltpu.VMEM((n_q, HD), BF16), pltpu.VMEM((n_q, HD), BF16)],
        compiler_params=params(),
        cost_estimate=pl.CostEstimate(
            flops=8 * heads * seq_len * n_q * HD,
            bytes_accessed=2 * heads * seq_len * n_q,
            transcendentals=0,
        ),
        name="backward",
    )(ids, *pieces, kv, probs, out, inverse, grad_attn)
    return outs[:n_groups], outs[n_groups]


def frame_block(ids, sign, s, position, n_groups, n_tok):
    group = lax.rem(ids[0] + sign * s + n_groups, n_groups)
    return group * n_tok + jnp.bitwise_xor(ids[1], relative_of(position, bits_of(n_tok)))


def attn_kernel(n_groups, n_tok, n_space, ids, *refs):
    grads, (w_rel, out, weight) = refs[:n_space], refs[n_space:]
    depth = w_rel.shape[0] // (n_groups * n_tok)
    for j in range(n_tok):
        for s in range(n_groups):
            place = frame_block(ids, -1, s, j, n_groups, n_tok) * depth
            at = (j * n_groups + s) * depth
            weight[pl.ds(aligned(place, 16), depth), :] = w_rel[at : at + depth, :]
    part = grads[0].shape[1]
    total = None
    for r in range(n_space):
        start = jnp.bitwise_xor(ids[2], relative_of(r, bits_of(n_space))) * part
        term = dot(grads[r][...], weight[pl.ds(aligned(start, 16), part), :], ((1,), (0,)))
        total = term if total is None else total + term
    out[...] = total.astype(BF16)


def attn_gradient(ids, grads, w_rel, n_groups, n_tok, n_space):
    n_q = grads[0].shape[0]
    depth, gw = w_rel.shape
    return pl.pallas_call(
        functools.partial(attn_kernel, n_groups, n_tok, n_space),
        out_shape=jax.ShapeDtypeStruct((n_q, gw), BF16),
        in_specs=[smem()] + [vmem()] * (n_space + 1),
        out_specs=vmem(),
        scratch_shapes=[pltpu.VMEM((depth, gw), BF16)],
        compiler_params=params(),
        cost_estimate=pl.CostEstimate(
            flops=2 * n_q * depth * gw,
            bytes_accessed=2 * (n_q * depth + depth * gw + n_q * gw),
            transcendentals=0,
        ),
        name="attn_gradient",
    )(ids, *grads, w_rel)


def proj_kernel(n_groups, n_tok, n_space, ids, *refs):
    grads, (attn, out, whole) = refs[:n_space], refs[n_space:]
    part = grads[0].shape[1]
    for r in range(n_space):
        start = jnp.bitwise_xor(ids[2], relative_of(r, bits_of(n_space))) * part
        term = dot(grads[r][...], attn[...], ((0,), (0,)))
        whole[pl.ds(aligned(start, 16), part), :] = term.astype(BF16)
    depth = out.shape[0] // (n_groups * n_tok)
    for j in range(n_tok):
        for s in range(n_groups):
            place = frame_block(ids, 1, s, j, n_groups, n_tok) * depth
            at = (j * n_groups + s) * depth
            out[at : at + depth, :] = whole[pl.ds(aligned(place, 16), depth), :]


def proj_gradient(ids, grads, attn, n_groups, n_tok, n_space):
    n_q, part = grads[0].shape
    depth = part * n_space
    gw = attn.shape[1]
    return pl.pallas_call(
        functools.partial(proj_kernel, n_groups, n_tok, n_space),
        out_shape=jax.ShapeDtypeStruct((depth, gw), BF16),
        in_specs=[smem()] + [vmem()] * (n_space + 1),
        out_specs=vmem(),
        scratch_shapes=[pltpu.VMEM((depth, gw), BF16)],
        compiler_params=params(),
        cost_estimate=pl.CostEstimate(
            flops=2 * n_q * depth * gw,
            bytes_accessed=2 * (n_q * depth + depth * gw + n_q * gw),
            transcendentals=0,
        ),
        name="proj_gradient",
    )(ids, *grads, attn)


def unpack_kernel(n_groups, ids, *refs):
    dq_in, dkv_in, (dq, dk, dv) = refs[:n_groups], refs[n_groups : 2 * n_groups], refs[2 * n_groups :]
    gw = dq_in[0].shape[1]
    for s in range(n_groups):
        start = lax.rem(ids[0] + s, n_groups) * gw
        dq[:, pl.ds(aligned(start, HD), gw)] = dq_in[s][...]
        for h in range(gw // HD):
            head = pl.ds(aligned(start + h * HD, HD), HD)
            dk[:, head] = dkv_in[s][:, 2 * h * HD : (2 * h + 1) * HD]
            dv[:, head] = dkv_in[s][:, (2 * h + 1) * HD : (2 * h + 2) * HD]


def unpack(ids, dq_in, dkv_in, n_groups):
    rows, gw = dq_in[0].shape
    return pl.pallas_call(
        functools.partial(unpack_kernel, n_groups),
        out_shape=[jax.ShapeDtypeStruct((rows, gw * n_groups), BF16)] * 3,
        in_specs=[smem()] + [vmem()] * (2 * n_groups),
        out_specs=[vmem()] * 3,
        compiler_params=params(),
        name="unpack",
    )(ids, *dq_in, *dkv_in)


def join_kernel(n_groups, ids, *refs):
    pieces, out = refs[:n_groups], refs[n_groups]
    gw = pieces[0].shape[1]
    for s in range(n_groups):
        start = lax.rem(ids[0] - s + n_groups, n_groups) * gw
        out[:, pl.ds(aligned(start, HD), gw)] = pieces[s][...].astype(F32)


def join(ids, pieces, n_groups):
    rows, gw = pieces[0].shape
    return pl.pallas_call(
        functools.partial(join_kernel, n_groups),
        out_shape=jax.ShapeDtypeStruct((rows, gw * n_groups), F32),
        in_specs=[smem()] + [vmem()] * n_groups,
        out_specs=vmem(),
        compiler_params=params(),
        name="join",
    )(ids, *pieces)


def exchange(pieces, n_groups, n_tok, sign):
    return [pieces[0]] + [
        lax.ppermute(pieces[s], "frame", shift_pairs(n_groups, n_tok, sign * s))
        for s in range(1, n_groups)
    ]


def local(queries, keys, values, grad_out, proj_weight):
    n_frame = lax.axis_size("frame")
    n_space = lax.axis_size("space")
    rows, width = queries.shape
    n_groups = math.gcd(width // HD, n_frame)
    n_tok = n_frame // n_groups
    tok_bits = bits_of(n_tok)
    gw = width // n_groups
    frame = lax.axis_index("frame")
    ids = jnp.stack([frame // n_tok, frame % n_tok, lax.axis_index("space")]).astype(jnp.int32)

    q_send, kv_send, w_send = pack(ids, queries, keys, values, proj_weight.T, n_groups)
    q_pieces = exchange(q_send, n_groups, n_tok, 1)
    kv = jnp.concatenate(exchange(kv_send, n_groups, n_tok, 1), axis=0)
    kv = gather_bits(kv, "frame", n_frame, tok_bits)
    weight = jnp.concatenate(exchange(w_send, n_groups, n_tok, 1), axis=0)
    weight = gather_bits(weight, "frame", n_frame, tok_bits)

    own = grad_out
    if n_groups > 1:
        groups = [[g * n_tok + t for g in range(n_groups)] for t in range(n_tok)]
        own = lax.all_gather(grad_out, "frame", axis=0, tiled=True, axis_index_groups=groups)
    grads = [own]
    for bit in reversed(bits_of(n_space)):
        grads = grads + [lax.ppermute(g, "space", xor_pairs(n_space, bit)) for g in grads]

    probs, out, inverse = forward(ids, q_pieces, kv, n_groups)
    proj = proj_gradient(ids, grads, out, n_groups, n_tok, n_space)
    grad_attn = attn_gradient(ids, grads, weight, n_groups, n_tok, n_space)
    dq_send, dkv = backward(ids, q_pieces, kv, probs, out, inverse, grad_attn, n_groups)

    proj = scatter_bits(proj, "frame", n_frame, tok_bits)
    depth = proj.shape[0] // n_groups
    proj_pieces = exchange(
        [proj[s * depth : (s + 1) * depth] for s in range(n_groups)], n_groups, n_tok, 1
    )
    grad_proj = join(ids, proj_pieces, n_groups).T

    dq_pieces = exchange(dq_send, n_groups, n_tok, -1)
    dkv = scatter_bits(dkv, "frame", n_frame, tok_bits)
    dkv_pieces = exchange(
        [dkv[s * rows : (s + 1) * rows] for s in range(n_groups)], n_groups, n_tok, -1
    )
    grad_queries, grad_keys, grad_values = unpack(ids, dq_pieces, dkv_pieces, n_groups)
    return (grad_queries, grad_keys, grad_values, grad_proj)


def solution(mesh):
    in_specs = (
        P("frame", "space"),
        P("frame", "space"),
        P("frame", "space"),
        P("frame", "space"),
        P("space", "frame"),
    )
    out_specs = (P("frame", "space"), P("frame", "space"), P("frame", "space"), P("space", "frame"))
    return jax.shard_map(local, mesh=mesh, in_specs=in_specs, out_specs=out_specs, check_vma=False)
```

```python
import functools
import math

import jax
import jax.numpy as jnp
from jax import lax
from jax.experimental import pallas as pl
from jax.experimental.pallas import tpu as pltpu
from jax.sharding import PartitionSpec as P

HD = 128
VMEM_BYTES = 40 * 1024 * 1024
GRAD_CHUNKS = 2
BF16 = jnp.bfloat16
F32 = jnp.float32


def bits_of(count):
    found = []
    bit = 1
    while bit < count:
        found.append(bit)
        bit *= 2
    return found


def relative_of(position, bits):
    total = 0
    for place, bit in enumerate(reversed(bits)):
        if position >> place & 1:
            total |= bit
    return total


def shift_pairs(n_groups, n_tok, step):
    return [
        (g * n_tok + t, (g + step) % n_groups * n_tok + t)
        for g in range(n_groups)
        for t in range(n_tok)
    ]


def xor_pairs(count, bit):
    return [(i, i ^ bit) for i in range(count)]


def gather_blocks(block, axis, count, bits):
    blocks = [block]
    for bit in reversed(bits):
        blocks = blocks + [lax.ppermute(b, axis, xor_pairs(count, bit)) for b in blocks]
    return blocks


def params():
    return pltpu.CompilerParams(vmem_limit_bytes=VMEM_BYTES)


def smem():
    return pl.BlockSpec(memory_space=pltpu.SMEM)


def vmem():
    return pl.BlockSpec(memory_space=pltpu.VMEM)


def aligned(value, unit):
    return pl.multiple_of(value, unit)


def dot(a, b, dims):
    return lax.dot_general(a, b, (dims, ((), ())), preferred_element_type=F32)


def whole_call(body, out_shape, args, name, scratch=(), cost=None):
    single = not isinstance(out_shape, list)
    return pl.pallas_call(
        body,
        out_shape=out_shape,
        in_specs=[smem()] + [vmem()] * (len(args) - 1),
        out_specs=vmem() if single else [vmem()] * len(out_shape),
        scratch_shapes=list(scratch),
        compiler_params=params(),
        cost_estimate=cost,
        name=name,
    )(*args)


def pack_kernel(n_groups, ids, q, k, v, *outs):
    rows = q.shape[0]
    gw = q.shape[1] // n_groups
    for s in range(n_groups):
        cols = pl.ds(aligned(lax.rem(ids[0] + s, n_groups) * gw, HD), gw)
        for i, source in enumerate((q, k, v)):
            outs[s][i * rows : (i + 1) * rows, :] = source[:, cols]


def pack(ids, q, k, v, n_groups):
    rows, width = q.shape
    shape = jax.ShapeDtypeStruct((3 * rows, width // n_groups), BF16)
    return whole_call(
        functools.partial(pack_kernel, n_groups), [shape] * n_groups, (ids, q, k, v), "pack"
    )


def cut_kernel(n_groups, ids, w, *outs):
    gw = w.shape[1] // n_groups
    for s in range(n_groups):
        outs[s][...] = w[:, pl.ds(aligned(lax.rem(ids[0] + s, n_groups) * gw, HD), gw)]


def cut(ids, w, n_groups):
    depth, width = w.shape
    shape = jax.ShapeDtypeStruct((depth, width // n_groups), BF16)
    return whole_call(functools.partial(cut_kernel, n_groups), [shape] * n_groups, (ids, w), "cut")


def split_kernel(n_groups, ids, *refs):
    pieces, (q_out, kv_out) = refs[:n_groups], refs[n_groups:]
    rows = pieces[0].shape[0] // 3
    half = n_groups * rows
    for s in range(n_groups):
        src = lax.rem(ids[0] - s + n_groups, n_groups)
        q_out[pl.ds(aligned(src * rows, 16), rows), :] = pieces[s][:rows, :]
        kv_out[s * rows : (s + 1) * rows, :] = pieces[s][rows : 2 * rows, :]
        kv_out[half + s * rows : half + (s + 1) * rows, :] = pieces[s][2 * rows :, :]


def split(ids, pieces, n_groups):
    rows, gw = pieces[0].shape[0] // 3, pieces[0].shape[1]
    shapes = [
        jax.ShapeDtypeStruct((n_groups * rows, gw), BF16),
        jax.ShapeDtypeStruct((2 * n_groups * rows, gw), BF16),
    ]
    return whole_call(functools.partial(split_kernel, n_groups), shapes, (ids, *pieces), "split")


def stack_kernel(ids, *refs):
    pieces, out = refs[:-1], refs[-1]
    rows = pieces[0].shape[0]
    for s, piece in enumerate(pieces):
        out[s * rows : (s + 1) * rows, :] = piece[...]


def stack(ids, pieces):
    rows, gw = pieces[0].shape
    shape = jax.ShapeDtypeStruct((rows * len(pieces), gw), BF16)
    return whole_call(stack_kernel, shape, (ids, *pieces), "stack")


def forward_kernel(chunk, scale, q_in, *refs):
    blocks, (p_out, o_out, il_out, logits) = refs[:-4], refs[-4:]
    part = blocks[0].shape[0] // 2
    q = q_in[...]
    top = None
    for j, kv in enumerate(blocks):
        for c in range(0, part, chunk):
            at = j * part + c
            block = dot(kv[c : c + chunk, :], q, ((1,), (1,)))
            logits[at : at + chunk, :] = block
            here = jnp.max(block, axis=0, keepdims=True)
            top = here if top is None else jnp.maximum(top, here)
    top = top * scale
    total = jnp.zeros_like(top)
    out = jnp.zeros((HD, q.shape[0]), F32)
    for j, kv in enumerate(blocks):
        for c in range(0, part, chunk):
            at = j * part + c
            prob = jnp.exp2(logits[at : at + chunk, :] * scale - top)
            total = total + jnp.sum(prob, axis=0, keepdims=True)
            low = prob.astype(BF16)
            p_out[0, at : at + chunk, :] = low
            out = out + dot(kv[part + c : part + c + chunk, :], low, ((0,), (0,)))
    inverse = 1.0 / total
    il_out[0] = inverse
    o_out[...] = (out * inverse).T.astype(BF16)


def forward(q, blocks):
    n_q, gw = q.shape
    heads = gw // HD
    part = blocks[0].shape[0] // 2
    seq_len = part * len(blocks)
    chunk = part if part <= 640 else math.gcd(part, 512)
    scale = math.log2(math.e) / math.sqrt(HD)
    return pl.pallas_call(
        functools.partial(forward_kernel, chunk, scale),
        grid=(heads,),
        out_shape=[
            jax.ShapeDtypeStruct((heads, seq_len, n_q), BF16),
            jax.ShapeDtypeStruct((n_q, gw), BF16),
            jax.ShapeDtypeStruct((heads, 1, n_q), F32),
        ],
        in_specs=[pl.BlockSpec((n_q, HD), lambda h: (0, h))]
        + [pl.BlockSpec((2 * part, HD), lambda h: (0, h))] * len(blocks),
        out_specs=[
            pl.BlockSpec((1, seq_len, n_q), lambda h: (h, 0, 0)),
            pl.BlockSpec((n_q, HD), lambda h: (0, h)),
            pl.BlockSpec((1, 1, n_q), lambda h: (h, 0, 0)),
        ],
        scratch_shapes=[pltpu.VMEM((seq_len, n_q), F32)],
        compiler_params=params(),
        cost_estimate=pl.CostEstimate(
            flops=4 * heads * seq_len * n_q * HD,
            bytes_accessed=2 * heads * seq_len * n_q,
            transcendentals=heads * seq_len * n_q,
        ),
        name="forward",
    )(q, *blocks)


def backward_kernel(n_groups, chunk, factor, ids, *refs):
    q_in, p_in, o_in, il_in, da_in = refs[:5]
    dq_outs, halves, dq_all = refs[-n_groups - 3 : -3], refs[-3:-1], refs[-1]
    blocks = refs[5 : -n_groups - 3]
    part = blocks[0].shape[0] // 2
    rows = dq_outs[0].shape[0]
    q = q_in[...]
    n_q = q.shape[0]
    inverse = jnp.broadcast_to(il_in[0], (HD, n_q)).T
    da = (da_in[...].astype(F32) * inverse).astype(BF16)
    delta = jnp.sum((da.astype(F32) * o_in[...].astype(F32)).T, axis=0, keepdims=True)
    dq = jnp.zeros((HD, n_q), F32)
    per_half = max(1, len(blocks) // 2)
    for j, kv in enumerate(blocks):
        out = halves[j // per_half]
        base = j % per_half * 2 * part
        for c in range(0, part, chunk):
            at = j * part + c
            low = p_in[0, at : at + chunk, :]
            dp = dot(kv[part + c : part + c + chunk, :], da, ((1,), (1,)))
            ds = (low.astype(F32) * (dp - delta)).astype(BF16)
            dk = (factor * dot(ds, q, ((1,), (0,)))).astype(BF16)
            out[base + c : base + c + chunk, :] = dk
            dv = dot(low, da, ((1,), (0,))).astype(BF16)
            out[base + part + c : base + part + c + chunk, :] = dv
            dq = dq + dot(kv[c : c + chunk, :], ds, ((0,), (0,)))
    dq_all[...] = (factor * dq).T.astype(BF16)
    for s in range(n_groups):
        src = lax.rem(ids[0] - s + n_groups, n_groups)
        dq_outs[s][...] = dq_all[pl.ds(aligned(src * rows, 16), rows), :]


def backward(ids, head, q, blocks, probs, out, inverse, grad_attn, n_groups):
    n_q = q.shape[0]
    rows = n_q // n_groups
    part = blocks[0].shape[0] // 2
    seq_len = part * len(blocks)
    chunk = part if part <= 640 else math.gcd(part, 512)
    per_half = max(1, len(blocks) // 2)
    column = pl.BlockSpec((n_q, HD), lambda i: (0, head))
    results = pl.pallas_call(
        functools.partial(backward_kernel, n_groups, chunk, 1.0 / math.sqrt(HD)),
        grid=(1,),
        out_shape=[jax.ShapeDtypeStruct((rows, HD), BF16)] * n_groups
        + [jax.ShapeDtypeStruct((per_half * 2 * part, HD), BF16)] * 2,
        in_specs=[
            smem(),
            column,
            pl.BlockSpec((1, seq_len, n_q), lambda i: (head, 0, 0)),
            column,
            pl.BlockSpec((1, 1, n_q), lambda i: (head, 0, 0)),
            column,
        ]
        + [pl.BlockSpec((2 * part, HD), lambda i: (0, head))] * len(blocks),
        out_specs=[vmem()] * (n_groups + 2),
        scratch_shapes=[pltpu.VMEM((n_q, HD), BF16)],
        compiler_params=params(),
        cost_estimate=pl.CostEstimate(
            flops=8 * seq_len * n_q * HD,
            bytes_accessed=2 * seq_len * n_q,
            transcendentals=0,
        ),
        name="backward",
    )(ids, q, probs, out, inverse, grad_attn, *blocks)
    return results[:n_groups], results[n_groups:]


def frame_block(ids, sign, s, position, n_groups, n_tok):
    group = lax.rem(ids[0] + sign * s + n_groups, n_groups)
    return group * n_tok + jnp.bitwise_xor(ids[1], relative_of(position, bits_of(n_tok)))


def column_starts(ids, grads, n_space):
    part = sum(g.shape[1] for g in grads[0])
    for r in range(n_space):
        start = jnp.bitwise_xor(ids[2], relative_of(r, bits_of(n_space))) * part
        for grad in grads[r]:
            yield grad, aligned(start, 16)
            start = start + grad.shape[1]


def by_space(refs, n_space):
    count = len(refs) // n_space
    return [refs[r * count : (r + 1) * count] for r in range(n_space)]


def attn_kernel(n_groups, n_tok, n_space, ids, *refs):
    weights, (out, weight) = refs[:n_tok], refs[-2:]
    grads = by_space(refs[n_tok:-2], n_space)
    depth = weights[0].shape[0] // n_groups
    for j in range(n_tok):
        for s in range(n_groups):
            place = frame_block(ids, -1, s, j, n_groups, n_tok) * depth
            weight[pl.ds(aligned(place, 16), depth), :] = weights[j][s * depth : (s + 1) * depth, :]
    total = None
    for grad, start in column_starts(ids, grads, n_space):
        term = dot(grad[...], weight[pl.ds(start, grad.shape[1]), :], ((1,), (0,)))
        total = term if total is None else total + term
    out[...] = total.astype(BF16)


def projection_cost(n_q, depth, gw):
    return pl.CostEstimate(
        flops=2 * n_q * depth * gw,
        bytes_accessed=2 * (n_q * depth + depth * gw + n_q * gw),
        transcendentals=0,
    )


def attn_gradient(ids, grads, weights, n_groups, n_tok, n_space):
    n_q = grads[0][0].shape[0]
    depth, gw = n_tok * weights[0].shape[0], weights[0].shape[1]
    return whole_call(
        functools.partial(attn_kernel, n_groups, n_tok, n_space),
        jax.ShapeDtypeStruct((n_q, gw), BF16),
        (ids, *weights, *[g for part in grads for g in part]),
        "attn_gradient",
        [pltpu.VMEM((depth, gw), BF16)],
        projection_cost(n_q, depth, gw),
    )


def proj_kernel(n_groups, n_tok, n_space, ids, *refs):
    attn, halves, whole = refs[0], refs[-3:-1], refs[-1]
    grads = by_space(refs[1:-3], n_space)
    for grad, start in column_starts(ids, grads, n_space):
        term = dot(grad[...], attn[...], ((0,), (0,)))
        whole[pl.ds(start, grad.shape[1]), :] = term.astype(BF16)
    depth = whole.shape[0] // (n_groups * n_tok)
    per_half = max(1, n_tok // 2)
    for j in range(n_tok):
        for s in range(n_groups):
            place = frame_block(ids, 1, s, j, n_groups, n_tok) * depth
            at = (j % per_half * n_groups + s) * depth
            halves[j // per_half][at : at + depth, :] = whole[pl.ds(aligned(place, 16), depth), :]


def proj_gradient(ids, grads, attn, n_groups, n_tok, n_space):
    n_q, gw = attn.shape
    depth = n_space * sum(g.shape[1] for g in grads[0])
    half = depth // n_tok * max(1, n_tok // 2)
    return whole_call(
        functools.partial(proj_kernel, n_groups, n_tok, n_space),
        [jax.ShapeDtypeStruct((half, gw), BF16)] * 2,
        (ids, attn, *[g for part in grads for g in part]),
        "proj_gradient",
        [pltpu.VMEM((depth, gw), BF16)],
        projection_cost(n_q, depth, gw),
    )


def add_kernel(ids, kept, other, *outs):
    rows = outs[0].shape[0]
    for i, out in enumerate(outs):
        total = kept[i * rows : (i + 1) * rows, :].astype(F32)
        total = total + other[i * rows : (i + 1) * rows, :].astype(F32)
        out[...] = total.astype(BF16)


def add_parts(ids, kept, other, count):
    rows, gw = kept.shape
    shape = jax.ShapeDtypeStruct((rows // count, gw), BF16)
    return whole_call(add_kernel, [shape] * count, (ids, kept, other), "add_parts")


def reduce_halves(ids, kept, sent, n_frame, bits):
    for place, bit in enumerate(bits):
        other = lax.ppermute(sent, "frame", xor_pairs(n_frame, bit))
        if place == len(bits) - 1:
            return kept, other
        kept, sent = add_parts(ids, kept, other, 2)


def finish_kernel(n_groups, ids, kept, other, *refs):
    dq, outs = refs[:n_groups], refs[n_groups:]
    rows = dq[0].shape[0]
    for s in range(n_groups):
        outs[s][:rows, :] = dq[s][...]
        for i in range(2):
            at = (i * n_groups + s) * rows
            total = kept[at : at + rows, :].astype(F32) + other[at : at + rows, :].astype(F32)
            outs[s][(i + 1) * rows : (i + 2) * rows, :] = total.astype(BF16)


def finish(ids, kept, other, dq, n_groups):
    rows = dq[0].shape[0]
    return whole_call(
        functools.partial(finish_kernel, n_groups),
        [jax.ShapeDtypeStruct((3 * rows, HD), BF16)] * n_groups,
        (ids, kept, other, *dq),
        "finish",
    )


def unpack_kernel(n_groups, heads, ids, *refs):
    rows = refs[-1].shape[0]
    for h in range(heads):
        for s in range(n_groups):
            start = (lax.rem(ids[0] + s, n_groups) * heads + h) * HD
            for i, out in enumerate(refs[-3:]):
                piece = refs[h * n_groups + s][i * rows : (i + 1) * rows, :]
                out[:, pl.ds(aligned(start, HD), HD)] = piece


def unpack(ids, pieces, n_groups):
    heads = len(pieces)
    rows = pieces[0][0].shape[0] // 3
    shape = jax.ShapeDtypeStruct((rows, HD * heads * n_groups), BF16)
    return whole_call(
        functools.partial(unpack_kernel, n_groups, heads),
        [shape] * 3,
        (ids, *[p for per_head in pieces for p in per_head]),
        "unpack",
    )


def join_kernel(n_groups, ids, *refs):
    pieces, out = refs[:n_groups], refs[n_groups]
    gw = pieces[0].shape[1]
    for s in range(n_groups):
        start = lax.rem(ids[0] - s + n_groups, n_groups) * gw
        out[:, pl.ds(aligned(start, HD), gw)] = pieces[s][...].astype(F32)


def join(ids, pieces, n_groups):
    rows, gw = pieces[0].shape
    return whole_call(
        functools.partial(join_kernel, n_groups),
        jax.ShapeDtypeStruct((rows, gw * n_groups), F32),
        (ids, *pieces),
        "join",
    )


def exchange(pieces, n_groups, n_tok, sign):
    return [pieces[0]] + [
        lax.ppermute(pieces[s], "frame", shift_pairs(n_groups, n_tok, sign * s))
        for s in range(1, n_groups)
    ]


def local(queries, keys, values, grad_out, proj_weight):
    n_frame = lax.axis_size("frame")
    n_space = lax.axis_size("space")
    width = queries.shape[1]
    n_groups = math.gcd(width // HD, n_frame)
    n_tok = n_frame // n_groups
    tok_bits = bits_of(n_tok)
    heads = width // n_groups // HD
    frame = lax.axis_index("frame")
    ids = jnp.stack([frame // n_tok, frame % n_tok, lax.axis_index("space")]).astype(jnp.int32)

    pieces = exchange(pack(ids, queries, keys, values, n_groups), n_groups, n_tok, 1)
    q, kv = split(ids, pieces, n_groups)
    kv = gather_blocks(kv, "frame", n_frame, tok_bits)
    weight = exchange(cut(ids, proj_weight.T, n_groups), n_groups, n_tok, 1)
    weights = gather_blocks(stack(ids, weight), "frame", n_frame, tok_bits)

    n_chunk = math.gcd(grad_out.shape[1] // HD, GRAD_CHUNKS)
    chunk_cols = grad_out.shape[1] // n_chunk
    lines = [[g * n_tok + t for g in range(n_groups)] for t in range(n_tok)]
    grads = [[] for _ in range(n_space)]
    for c in range(n_chunk):
        own = grad_out[:, c * chunk_cols : (c + 1) * chunk_cols]
        if n_groups > 1:
            own = lax.all_gather(own, "frame", axis=0, tiled=True, axis_index_groups=lines)
        gathered = gather_blocks(own, "space", n_space, bits_of(n_space))
        for r in range(n_space):
            grads[r].append(gathered[r])

    probs, out, inverse = forward(q, kv)
    kept, sent = proj_gradient(ids, grads, out, n_groups, n_tok, n_space)
    grad_attn = attn_gradient(ids, grads, weights, n_groups, n_tok, n_space)
    grad_attn, kept, sent = lax.optimization_barrier((grad_attn, kept, sent))
    proj = reduce_halves(ids, kept, sent, n_frame, tok_bits)
    proj = exchange(add_parts(ids, *proj, n_groups), n_groups, n_tok, 1)
    grad_proj = join(ids, proj, n_groups).T

    returned = []
    for h in range(heads):
        dq, halves = backward(ids, h, q, kv, probs, out, inverse, grad_attn, n_groups)
        kept, other = reduce_halves(ids, *halves, n_frame, tok_bits)
        returned.append(exchange(finish(ids, kept, other, dq, n_groups), n_groups, n_tok, -1))
    grad_queries, grad_keys, grad_values = unpack(ids, returned, n_groups)
    return (grad_queries, grad_keys, grad_values, grad_proj)


def solution(mesh):
    in_specs = (
        P("frame", "space"),
        P("frame", "space"),
        P("frame", "space"),
        P("frame", "space"),
        P("space", "frame"),
    )
    out_specs = (P("frame", "space"), P("frame", "space"), P("frame", "space"), P("space", "frame"))
    return jax.shard_map(local, mesh=mesh, in_specs=in_specs, out_specs=out_specs, check_vma=False)
```

```python
import functools
import math

import jax
import jax.numpy as jnp
from jax import lax
from jax.experimental import pallas as pl
from jax.experimental.pallas import tpu as pltpu
from jax.sharding import PartitionSpec as P

HD = 128
VMEM_BYTES = 32 * 1024 * 1024
BF16 = jnp.bfloat16
F32 = jnp.float32


def bits_of(count):
    found = []
    bit = 1
    while bit < count:
        found.append(bit)
        bit *= 2
    return found


def relative_of(position, bits):
    total = 0
    for place, bit in enumerate(reversed(bits)):
        if position >> place & 1:
            total |= bit
    return total


def shift_pairs(n_groups, n_tok, step):
    return [
        (g * n_tok + t, (g + step) % n_groups * n_tok + t)
        for g in range(n_groups)
        for t in range(n_tok)
    ]


def xor_pairs(count, bit):
    return [(i, i ^ bit) for i in range(count)]


def gather_blocks(block, axis, count, bits):
    blocks = [block]
    for bit in reversed(bits):
        blocks = blocks + [lax.ppermute(b, axis, xor_pairs(count, bit)) for b in blocks]
    return blocks


def params():
    return pltpu.CompilerParams(vmem_limit_bytes=VMEM_BYTES)


def smem():
    return pl.BlockSpec(memory_space=pltpu.SMEM)


def vmem():
    return pl.BlockSpec(memory_space=pltpu.VMEM)


def aligned(value, unit):
    return pl.multiple_of(value, unit)


def dot(a, b, dims):
    return lax.dot_general(a, b, (dims, ((), ())), preferred_element_type=F32)


def whole_call(body, out_shape, args, name, scratch=(), cost=None):
    single = not isinstance(out_shape, list)
    return pl.pallas_call(
        body,
        out_shape=out_shape,
        in_specs=[smem()] + [vmem()] * (len(args) - 1),
        out_specs=vmem() if single else [vmem()] * len(out_shape),
        scratch_shapes=list(scratch),
        compiler_params=params(),
        cost_estimate=cost,
        name=name,
    )(*args)


def pack_kernel(n_groups, ids, q, k, v, w, *outs):
    rows, depth = q.shape[0], w.shape[0]
    gw = q.shape[1] // n_groups
    for s in range(n_groups):
        cols = pl.ds(aligned(lax.rem(ids[0] + s, n_groups) * gw, HD), gw)
        outs[s][:rows, :] = k[:, cols]
        outs[s][rows : 2 * rows, :] = v[:, cols]
        outs[s][2 * rows : 2 * rows + depth, :] = w[:, cols]
        if s == 0:
            outs[n_groups][...] = q[:, cols]
        else:
            outs[s][2 * rows + depth :, :] = q[:, cols]


def pack(ids, q, k, v, w, n_groups):
    rows, width = q.shape
    gw = width // n_groups
    shared = 2 * rows + w.shape[0]
    shapes = (
        [jax.ShapeDtypeStruct((shared, gw), BF16)]
        + [jax.ShapeDtypeStruct((shared + rows, gw), BF16)] * (n_groups - 1)
        + [jax.ShapeDtypeStruct((rows, gw), BF16)]
    )
    return whole_call(functools.partial(pack_kernel, n_groups), shapes, (ids, q, k, v, w), "pack")


def stack_kernel(n_groups, rows, ids, *refs):
    pieces, out = refs[:n_groups], refs[n_groups]
    shared = out.shape[0] // n_groups
    depth = shared - 2 * rows
    for s, piece in enumerate(pieces):
        for i in range(2):
            at = (i * n_groups + s) * rows
            out[at : at + rows, :] = piece[i * rows : (i + 1) * rows, :]
        at = 2 * n_groups * rows + s * depth
        out[at : at + depth, :] = piece[2 * rows : shared, :]


def stack(ids, pieces, rows):
    shared, gw = pieces[0].shape
    return whole_call(
        functools.partial(stack_kernel, len(pieces), rows),
        jax.ShapeDtypeStruct((shared * len(pieces), gw), BF16),
        (ids, *pieces),
        "stack",
    )


def stack_queries_kernel(ids, own, *refs):
    pieces, out = refs[:-1], refs[-1]
    rows = own.shape[0]
    out[:rows, :] = own[...]
    for s, piece in enumerate(pieces):
        out[(s + 1) * rows : (s + 2) * rows, :] = piece[piece.shape[0] - rows :, :]


def stack_queries(ids, own, pieces):
    rows, gw = own.shape
    shape = jax.ShapeDtypeStruct((rows * (len(pieces) + 1), gw), BF16)
    return whole_call(stack_queries_kernel, shape, (ids, own, *pieces), "stack_queries")


def forward_kernel(chunk, scale, q_in, *refs):
    blocks, (p_out, o_out, il_out, logits) = refs[:-4], refs[-4:]
    part = blocks[0].shape[0] // 2
    q = q_in[...]
    top = None
    for j, kv in enumerate(blocks):
        for c in range(0, part, chunk):
            at = j * part + c
            block = dot(kv[c : c + chunk, :], q, ((1,), (1,)))
            logits[at : at + chunk, :] = block
            here = jnp.max(block, axis=0, keepdims=True)
            top = here if top is None else jnp.maximum(top, here)
    top = top * scale
    total = jnp.zeros_like(top)
    out = jnp.zeros((HD, q.shape[0]), F32)
    for j, kv in enumerate(blocks):
        for c in range(0, part, chunk):
            at = j * part + c
            prob = jnp.exp2(logits[at : at + chunk, :] * scale - top)
            total = total + jnp.sum(prob, axis=0, keepdims=True)
            low = prob.astype(BF16)
            p_out[0, at : at + chunk, :] = low
            out = out + dot(kv[part + c : part + c + chunk, :], low, ((0,), (0,)))
    inverse = 1.0 / total
    il_out[0] = inverse
    o_out[...] = (out * inverse).T.astype(BF16)


def forward(q, blocks, part):
    n_q, gw = q.shape
    heads = gw // HD
    seq_len = part * len(blocks)
    chunk = part if part <= 640 else math.gcd(part, 512)
    scale = math.log2(math.e) / math.sqrt(HD)
    return pl.pallas_call(
        functools.partial(forward_kernel, chunk, scale),
        grid=(heads,),
        out_shape=[
            jax.ShapeDtypeStruct((heads, seq_len, n_q), BF16),
            jax.ShapeDtypeStruct((n_q, gw), BF16),
            jax.ShapeDtypeStruct((heads, 1, n_q), F32),
        ],
        in_specs=[pl.BlockSpec((n_q, HD), lambda h: (0, h))]
        + [pl.BlockSpec((2 * part, HD), lambda h: (0, h))] * len(blocks),
        out_specs=[
            pl.BlockSpec((1, seq_len, n_q), lambda h: (h, 0, 0)),
            pl.BlockSpec((n_q, HD), lambda h: (0, h)),
            pl.BlockSpec((1, 1, n_q), lambda h: (h, 0, 0)),
        ],
        scratch_shapes=[pltpu.VMEM((seq_len, n_q), F32)],
        compiler_params=params(),
        cost_estimate=pl.CostEstimate(
            flops=4 * heads * seq_len * n_q * HD,
            bytes_accessed=2 * heads * seq_len * n_q,
            transcendentals=heads * seq_len * n_q,
        ),
        name="forward",
    )(q, *blocks)


def backward_kernel(n_groups, chunk, factor, *refs):
    q_in, p_in, o_in, il_in, da_in = refs[:5]
    dq_outs, halves, dq_all = refs[-n_groups - 3 : -3], refs[-3:-1], refs[-1]
    blocks = refs[5 : -n_groups - 3]
    part = blocks[0].shape[0] // 2
    rows = dq_outs[0].shape[0]
    q = q_in[...]
    n_q = q.shape[0]
    inverse = jnp.broadcast_to(il_in[0], (HD, n_q)).T
    da = (da_in[...].astype(F32) * inverse).astype(BF16)
    delta = jnp.sum((da.astype(F32) * o_in[...].astype(F32)).T, axis=0, keepdims=True)
    dq = jnp.zeros((HD, n_q), F32)
    per_half = max(1, len(blocks) // 2)
    for j, kv in enumerate(blocks):
        out = halves[j // per_half]
        base = j % per_half * 2 * part
        for c in range(0, part, chunk):
            at = j * part + c
            low = p_in[0, at : at + chunk, :]
            dp = dot(kv[part + c : part + c + chunk, :], da, ((1,), (1,)))
            ds = (low.astype(F32) * (dp - delta)).astype(BF16)
            dk = (factor * dot(ds, q, ((1,), (0,)))).astype(BF16)
            out[base + c : base + c + chunk, :] = dk
            dv = dot(low, da, ((1,), (0,))).astype(BF16)
            out[base + part + c : base + part + c + chunk, :] = dv
            dq = dq + dot(kv[c : c + chunk, :], ds, ((0,), (0,)))
    dq_all[...] = (factor * dq).T.astype(BF16)
    for s in range(n_groups):
        dq_outs[s][...] = dq_all[s * rows : (s + 1) * rows, :]


def backward(head, q, blocks, part, probs, out, inverse, grad_attn, n_groups):
    n_q = q.shape[0]
    rows = n_q // n_groups
    seq_len = part * len(blocks)
    chunk = part if part <= 640 else math.gcd(part, 512)
    per_half = max(1, len(blocks) // 2)
    column = pl.BlockSpec((n_q, HD), lambda i: (0, head))
    results = pl.pallas_call(
        functools.partial(backward_kernel, n_groups, chunk, 1.0 / math.sqrt(HD)),
        grid=(1,),
        out_shape=[jax.ShapeDtypeStruct((rows, HD), BF16)] * n_groups
        + [jax.ShapeDtypeStruct((per_half * 2 * part, HD), BF16)] * 2,
        in_specs=[
            column,
            pl.BlockSpec((1, seq_len, n_q), lambda i: (head, 0, 0)),
            column,
            pl.BlockSpec((1, 1, n_q), lambda i: (head, 0, 0)),
            column,
        ]
        + [pl.BlockSpec((2 * part, HD), lambda i: (0, head))] * len(blocks),
        out_specs=[vmem()] * (n_groups + 2),
        scratch_shapes=[pltpu.VMEM((n_q, HD), BF16)],
        compiler_params=params(),
        cost_estimate=pl.CostEstimate(
            flops=n_q * HD,
            bytes_accessed=2 * n_q * HD,
            transcendentals=0,
        ),
        name="backward",
    )(q, probs, out, inverse, grad_attn, *blocks)
    return results[:n_groups], results[n_groups:]


def frame_block(ids, sign, s, position, n_groups, n_tok):
    group = lax.rem(ids[0] + sign * s + n_groups, n_groups)
    return group * n_tok + jnp.bitwise_xor(ids[1], relative_of(position, bits_of(n_tok)))


def project_kernel(n_groups, n_tok, n_space, ids, attn, *refs):
    blocks, grads = refs[:n_tok], refs[n_tok : n_tok + n_groups * n_space]
    grad_attn, kept, sent, weight, whole, tokens = refs[n_tok + n_groups * n_space :]
    rows, part = grads[0].shape
    depth = weight.shape[0] // (n_groups * n_tok)
    first = blocks[0].shape[0] - n_groups * depth
    for j in range(n_tok):
        for s in range(n_groups):
            place = frame_block(ids, -1, s, j, n_groups, n_tok) * depth
            at = first + s * depth
            weight[pl.ds(aligned(place, 16), depth), :] = blocks[j][at : at + depth, :]
    total = None
    for r in range(n_space):
        for s in range(n_groups):
            tokens[s * rows : (s + 1) * rows, :] = grads[r * n_groups + s][...]
        start = jnp.bitwise_xor(ids[2], relative_of(r, bits_of(n_space))) * part
        block = tokens[...]
        here = pl.ds(aligned(start, 16), part)
        term = dot(block, weight[here, :], ((1,), (0,)))
        total = term if total is None else total + term
        whole[here, :] = dot(block, attn[...], ((0,), (0,))).astype(BF16)
    grad_attn[...] = total.astype(BF16)
    per_half = max(1, n_tok // 2)
    for j in range(n_tok):
        half = sent if j >= per_half else kept
        for s in range(n_groups):
            place = frame_block(ids, 1, s, j, n_groups, n_tok) * depth
            at = (j % per_half * n_groups + s) * depth
            half[at : at + depth, :] = whole[pl.ds(aligned(place, 16), depth), :]


def project(ids, attn, blocks, grads, depth, n_groups, n_tok, n_space):
    n_q, gw = attn.shape
    part = grads[0].shape[1]
    half = n_groups * depth * max(1, n_tok // 2)
    total = n_groups * n_tok * depth
    return whole_call(
        functools.partial(project_kernel, n_groups, n_tok, n_space),
        [jax.ShapeDtypeStruct((n_q, gw), BF16)] + [jax.ShapeDtypeStruct((half, gw), BF16)] * 2,
        (ids, attn, *blocks, *grads),
        "project",
        [
            pltpu.VMEM((total, gw), BF16),
            pltpu.VMEM((total, gw), BF16),
            pltpu.VMEM((n_q, part), BF16),
        ],
        pl.CostEstimate(
            flops=4 * n_q * total * gw,
            bytes_accessed=2 * (n_q * total + 2 * total * gw + 2 * n_q * gw),
            transcendentals=0,
        ),
    )


def add_kernel(ids, kept, other, *outs):
    rows = outs[0].shape[0]
    for i, out in enumerate(outs):
        total = kept[i * rows : (i + 1) * rows, :].astype(F32)
        total = total + other[i * rows : (i + 1) * rows, :].astype(F32)
        out[...] = total.astype(BF16)


def add_parts(ids, kept, other, count):
    rows, gw = kept.shape
    shape = jax.ShapeDtypeStruct((rows // count, gw), BF16)
    return whole_call(add_kernel, [shape] * count, (ids, kept, other), "add_parts")


def halve(ids, kept, sent, n_frame, bits):
    for bit in bits[:-1]:
        other = lax.ppermute(sent, "frame", xor_pairs(n_frame, bit))
        kept, sent = add_parts(ids, kept, other, 2)
    return kept, sent


def finish_kernel(n_groups, ids, kept, other, *refs):
    dq, outs = refs[:n_groups], refs[n_groups:]
    rows = dq[0].shape[0]
    for s in range(n_groups):
        outs[s][:rows, :] = dq[s][...]
        for i in range(2):
            at = (i * n_groups + s) * rows
            total = kept[at : at + rows, :].astype(F32) + other[at : at + rows, :].astype(F32)
            outs[s][(i + 1) * rows : (i + 2) * rows, :] = total.astype(BF16)


def finish(ids, kept, other, dq, n_groups):
    rows = dq[0].shape[0]
    return whole_call(
        functools.partial(finish_kernel, n_groups),
        [jax.ShapeDtypeStruct((3 * rows, HD), BF16)] * n_groups,
        (ids, kept, other, *dq),
        "finish",
    )


def unpack_kernel(n_groups, heads, ids, *refs):
    rows = refs[-1].shape[0]
    for h in range(heads):
        for s in range(n_groups):
            start = (lax.rem(ids[0] + s, n_groups) * heads + h) * HD
            for i, out in enumerate(refs[-3:]):
                piece = refs[h * n_groups + s][i * rows : (i + 1) * rows, :]
                out[:, pl.ds(aligned(start, HD), HD)] = piece


def unpack(ids, pieces, n_groups):
    heads = len(pieces)
    rows = pieces[0][0].shape[0] // 3
    shape = jax.ShapeDtypeStruct((rows, HD * heads * n_groups), BF16)
    return whole_call(
        functools.partial(unpack_kernel, n_groups, heads),
        [shape] * 3,
        (ids, *[p for per_head in pieces for p in per_head]),
        "unpack",
    )


def join_kernel(n_groups, ids, *refs):
    pieces, out = refs[:n_groups], refs[n_groups]
    gw = pieces[0].shape[1]
    for s in range(n_groups):
        start = lax.rem(ids[0] - s + n_groups, n_groups) * gw
        out[:, pl.ds(aligned(start, HD), gw)] = pieces[s][...].astype(F32)


def join(ids, pieces, n_groups):
    rows, gw = pieces[0].shape
    return whole_call(
        functools.partial(join_kernel, n_groups),
        jax.ShapeDtypeStruct((rows, gw * n_groups), F32),
        (ids, *pieces),
        "join",
    )


def exchange(pieces, n_groups, n_tok, sign):
    return [pieces[0]] + [
        lax.ppermute(pieces[s], "frame", shift_pairs(n_groups, n_tok, sign * s))
        for s in range(1, n_groups)
    ]


def local(queries, keys, values, grad_out, proj_weight):
    n_frame = lax.axis_size("frame")
    n_space = lax.axis_size("space")
    rows, width = queries.shape
    depth = proj_weight.shape[1]
    n_groups = math.gcd(width // HD, n_frame)
    n_tok = n_frame // n_groups
    tok_bits = bits_of(n_tok)
    space_bits = bits_of(n_space)
    heads = width // n_groups // HD
    shared = 2 * rows + depth
    frame = lax.axis_index("frame")
    ids = jnp.stack([frame // n_tok, frame % n_tok, lax.axis_index("space")]).astype(jnp.int32)

    *pieces, own_q = pack(ids, queries, keys, values, proj_weight.T, n_groups)
    pieces = exchange(pieces, n_groups, n_tok, 1)
    q_pieces = pieces[1:]
    first = xor_pairs(n_frame, tok_bits[-1])
    own, others, by_piece = [pieces[0]], [lax.ppermute(pieces[0], "frame", first)], []
    ring = grad_out
    for s in range(n_groups):
        across = gather_blocks(ring, "space", n_space, space_bits)
        if s + 1 < n_groups:
            ring = lax.ppermute(ring, "frame", shift_pairs(n_groups, n_tok, 1))
            ring, piece, *across = lax.optimization_barrier((ring, pieces[s + 1][:shared], *across))
            own.append(piece)
            others.append(lax.ppermute(piece, "frame", first))
        by_piece.append(across)
    grads = [by_piece[s][r] for r in range(n_space) for s in range(n_groups)]

    q = stack_queries(ids, own_q, q_pieces)
    blocks = [stack(ids, own, rows), stack(ids, others, rows)]
    for bit in reversed(tok_bits[:-1]):
        blocks = blocks + [lax.ppermute(b, "frame", xor_pairs(n_frame, bit)) for b in blocks]

    part = n_groups * rows
    probs, out, inverse = forward(q, blocks, part)
    grad_attn, kept, sent = project(ids, out, blocks, grads, depth, n_groups, n_tok, n_space)
    last = xor_pairs(n_frame, tok_bits[-1])
    proj_kept, proj_sent = halve(ids, kept, sent, n_frame, tok_bits)
    here, sums, finished = q, (), []
    for h in range(heads):
        if h > 0:
            here, kept, sent, *sums = lax.optimization_barrier((q, kept, sent, *sums))
        if h > 1:
            finished[-1] = sums
        if h > 0:
            other = lax.ppermute(sent, "frame", last)
            kept_dq = (kept, other, dq)
        dq, halves = backward(h, here, blocks, part, probs, out, inverse, grad_attn, n_groups)
        if h > 0:
            sums = finish(ids, *kept_dq, n_groups)
            finished.append(sums)
        kept, sent = halve(ids, *halves, n_frame, tok_bits)
    finished.append(finish(ids, kept, lax.ppermute(sent, "frame", last), dq, n_groups))
    proj = add_parts(ids, proj_kept, lax.ppermute(proj_sent, "frame", last), n_groups)
    proj = exchange(proj, n_groups, n_tok, 1)
    grad_proj = join(ids, proj, n_groups).T
    returned = [exchange(sums, n_groups, n_tok, -1) for sums in finished]
    grad_queries, grad_keys, grad_values = unpack(ids, returned, n_groups)
    return (grad_queries, grad_keys, grad_values, grad_proj)


def solution(mesh):
    in_specs = (
        P("frame", "space"),
        P("frame", "space"),
        P("frame", "space"),
        P("frame", "space"),
        P("space", "frame"),
    )
    out_specs = (P("frame", "space"), P("frame", "space"), P("frame", "space"), P("space", "frame"))
    return jax.shard_map(local, mesh=mesh, in_specs=in_specs, out_specs=out_specs, check_vma=False)
```

```python
import functools
import math

import jax
import jax.numpy as jnp
from jax import lax
from jax.experimental import pallas as pl
from jax.experimental.pallas import tpu as pltpu
from jax.sharding import PartitionSpec as P

HD = 128
VMEM_BYTES = 24 * 1024 * 1024
BF16 = jnp.bfloat16
F32 = jnp.float32


def bits_of(count):
    found = []
    bit = 1
    while bit < count:
        found.append(bit)
        bit *= 2
    return found


def relative_of(position, bits):
    total = 0
    for place, bit in enumerate(reversed(bits)):
        if position >> place & 1:
            total |= bit
    return total


def shift_pairs(n_groups, n_tok, step):
    return [
        (g * n_tok + t, (g + step) % n_groups * n_tok + t)
        for g in range(n_groups)
        for t in range(n_tok)
    ]


def xor_pairs(count, bit):
    return [(i, i ^ bit) for i in range(count)]


def gather_blocks(block, axis, count, bits):
    blocks = [block]
    for bit in reversed(bits):
        blocks = blocks + [lax.ppermute(b, axis, xor_pairs(count, bit)) for b in blocks]
    return blocks


def params():
    return pltpu.CompilerParams(vmem_limit_bytes=VMEM_BYTES)


def smem():
    return pl.BlockSpec(memory_space=pltpu.SMEM)


def vmem():
    return pl.BlockSpec(memory_space=pltpu.VMEM)


def aligned(value, unit):
    return pl.multiple_of(value, unit)


def dot(a, b, dims):
    return lax.dot_general(a, b, (dims, ((), ())), preferred_element_type=F32)


def whole_call(body, out_shape, args, name, scratch=(), cost=None):
    single = not isinstance(out_shape, list)
    return pl.pallas_call(
        body,
        out_shape=out_shape,
        in_specs=[smem()] + [vmem()] * (len(args) - 1),
        out_specs=vmem() if single else [vmem()] * len(out_shape),
        scratch_shapes=list(scratch),
        compiler_params=params(),
        cost_estimate=cost,
        name=name,
    )(*args)


def pack_kernel(n_groups, ids, q, k, v, w, *refs):
    outs, sems = refs[:-1], refs[-1]
    rows, depth = q.shape[0], w.shape[0]
    gw = q.shape[1] // n_groups
    copies = []
    for s in range(n_groups):
        cols = pl.ds(aligned(lax.rem(ids[0] + s, n_groups) * gw, HD), gw)
        own = outs[n_groups] if s == 0 else outs[s].at[pl.ds(2 * rows + depth, rows), :]
        for source, target in (
            (k, outs[s].at[pl.ds(0, rows), :]),
            (v, outs[s].at[pl.ds(rows, rows), :]),
            (w, outs[s].at[pl.ds(2 * rows, depth), :]),
            (q, own),
        ):
            copies.append(
                pltpu.make_async_copy(source.at[:, cols], target, sems.at[len(copies)])
            )
    for copy in copies:
        copy.start()
    for copy in copies:
        copy.wait()


def pack(ids, q, k, v, w, n_groups):
    rows, width = q.shape
    gw = width // n_groups
    shared = 2 * rows + w.shape[0]
    shapes = (
        [jax.ShapeDtypeStruct((shared, gw), BF16)]
        + [jax.ShapeDtypeStruct((shared + rows, gw), BF16)] * (n_groups - 1)
        + [jax.ShapeDtypeStruct((rows, gw), BF16)]
    )
    return pl.pallas_call(
        functools.partial(pack_kernel, n_groups),
        out_shape=shapes,
        in_specs=[smem()] + [pl.BlockSpec(memory_space=pltpu.HBM)] * 4,
        out_specs=[vmem()] * len(shapes),
        scratch_shapes=[pltpu.SemaphoreType.DMA((4 * n_groups,))],
        compiler_params=pltpu.CompilerParams(vmem_limit_bytes=60 * 1024 * 1024),
        name="pack",
    )(ids, q, k, v, w)


def stack_kernel(n_groups, rows, ids, *refs):
    pieces, out = refs[:n_groups], refs[n_groups]
    shared = out.shape[0] // n_groups
    depth = shared - 2 * rows
    for s, piece in enumerate(pieces):
        for i in range(2):
            at = (i * n_groups + s) * rows
            out[at : at + rows, :] = piece[i * rows : (i + 1) * rows, :]
        at = 2 * n_groups * rows + s * depth
        out[at : at + depth, :] = piece[2 * rows : shared, :]


def stack(ids, pieces, rows):
    shared, gw = pieces[0].shape
    return whole_call(
        functools.partial(stack_kernel, len(pieces), rows),
        jax.ShapeDtypeStruct((shared * len(pieces), gw), BF16),
        (ids, *pieces),
        "stack",
    )


def stack_queries_kernel(ids, own, *refs):
    pieces, out = refs[:-1], refs[-1]
    rows = own.shape[0]
    out[:rows, :] = own[...]
    for s, piece in enumerate(pieces):
        out[(s + 1) * rows : (s + 2) * rows, :] = piece[piece.shape[0] - rows :, :]


def stack_queries(ids, own, pieces):
    rows, gw = own.shape
    shape = jax.ShapeDtypeStruct((rows * (len(pieces) + 1), gw), BF16)
    return whole_call(stack_queries_kernel, shape, (ids, own, *pieces), "stack_queries")


def forward_kernel(chunk, scale, q_in, *refs):
    blocks, (p_out, o_out, il_out, logits) = refs[:-4], refs[-4:]
    part = blocks[0].shape[0] // 2
    q = q_in[...]
    top = None
    for j, kv in enumerate(blocks):
        for c in range(0, part, chunk):
            at = j * part + c
            block = dot(kv[c : c + chunk, :], q, ((1,), (1,)))
            logits[at : at + chunk, :] = block
            here = jnp.max(block, axis=0, keepdims=True)
            top = here if top is None else jnp.maximum(top, here)
    top = top * scale
    total = jnp.zeros_like(top)
    out = jnp.zeros((HD, q.shape[0]), F32)
    for j, kv in enumerate(blocks):
        for c in range(0, part, chunk):
            at = j * part + c
            prob = jnp.exp2(logits[at : at + chunk, :] * scale - top)
            total = total + jnp.sum(prob, axis=0, keepdims=True)
            low = prob.astype(BF16)
            p_out[0, at : at + chunk, :] = low
            out = out + dot(kv[part + c : part + c + chunk, :], low, ((0,), (0,)))
    inverse = 1.0 / total
    il_out[0] = inverse
    o_out[...] = (out * inverse).T.astype(BF16)


def forward(q, blocks, part):
    n_q, gw = q.shape
    heads = gw // HD
    seq_len = part * len(blocks)
    chunk = part if part <= 640 else math.gcd(part, 512)
    scale = math.log2(math.e) / math.sqrt(HD)
    return pl.pallas_call(
        functools.partial(forward_kernel, chunk, scale),
        grid=(heads,),
        out_shape=[
            jax.ShapeDtypeStruct((heads, seq_len, n_q), BF16),
            jax.ShapeDtypeStruct((n_q, gw), BF16),
            jax.ShapeDtypeStruct((heads, 1, n_q), F32),
        ],
        in_specs=[pl.BlockSpec((n_q, HD), lambda h: (0, h))]
        + [pl.BlockSpec((2 * part, HD), lambda h: (0, h))] * len(blocks),
        out_specs=[
            pl.BlockSpec((1, seq_len, n_q), lambda h: (h, 0, 0)),
            pl.BlockSpec((n_q, HD), lambda h: (0, h)),
            pl.BlockSpec((1, 1, n_q), lambda h: (h, 0, 0)),
        ],
        scratch_shapes=[pltpu.VMEM((seq_len, n_q), F32)],
        compiler_params=params(),
        cost_estimate=pl.CostEstimate(
            flops=4 * heads * seq_len * n_q * HD,
            bytes_accessed=2 * heads * seq_len * n_q,
            transcendentals=heads * seq_len * n_q,
        ),
        name="forward",
    )(q, *blocks)


def backward_kernel(n_groups, chunk, factor, *refs):
    q_in, p_in, o_in, il_in, da_in = refs[:5]
    dq_outs, halves, dq_all = refs[-n_groups - 3 : -3], refs[-3:-1], refs[-1]
    blocks = refs[5 : -n_groups - 3]
    part = blocks[0].shape[0] // 2
    rows = dq_outs[0].shape[0]
    q = q_in[...]
    n_q = q.shape[0]
    inverse = jnp.broadcast_to(il_in[0], (HD, n_q)).T
    da = (da_in[...].astype(F32) * inverse).astype(BF16)
    delta = jnp.sum((da.astype(F32) * o_in[...].astype(F32)).T, axis=0, keepdims=True)
    dq = jnp.zeros((HD, n_q), F32)
    per_half = max(1, len(blocks) // 2)
    for j, kv in enumerate(blocks):
        out = halves[j // per_half]
        base = j % per_half * 2 * part
        for c in range(0, part, chunk):
            at = j * part + c
            low = p_in[0, at : at + chunk, :]
            dp = dot(kv[part + c : part + c + chunk, :], da, ((1,), (1,)))
            ds = (low.astype(F32) * (dp - delta)).astype(BF16)
            dk = (factor * dot(ds, q, ((1,), (0,)))).astype(BF16)
            out[base + c : base + c + chunk, :] = dk
            dv = dot(low, da, ((1,), (0,))).astype(BF16)
            out[base + part + c : base + part + c + chunk, :] = dv
            dq = dq + dot(kv[c : c + chunk, :], ds, ((0,), (0,)))
    dq_all[...] = (factor * dq).T.astype(BF16)
    for s in range(n_groups):
        dq_outs[s][...] = dq_all[s * rows : (s + 1) * rows, :]


def backward(head, count, q, blocks, part, probs, out, inverse, grad_attn, n_groups):
    n_q = q.shape[0]
    rows = n_q // n_groups
    seq_len = part * len(blocks)
    chunk = part if part <= 640 else math.gcd(part, 512)
    per_half = max(1, len(blocks) // 2)
    column = pl.BlockSpec((n_q, HD), lambda i: (0, head + i))
    results = pl.pallas_call(
        functools.partial(backward_kernel, n_groups, chunk, 1.0 / math.sqrt(HD)),
        grid=(count,),
        out_shape=[jax.ShapeDtypeStruct((rows, count * HD), BF16)] * n_groups
        + [jax.ShapeDtypeStruct((per_half * 2 * part, count * HD), BF16)] * 2,
        in_specs=[
            column,
            pl.BlockSpec((1, seq_len, n_q), lambda i: (head + i, 0, 0)),
            column,
            pl.BlockSpec((1, 1, n_q), lambda i: (head + i, 0, 0)),
            column,
        ]
        + [pl.BlockSpec((2 * part, HD), lambda i: (0, head + i))] * len(blocks),
        out_specs=[pl.BlockSpec((rows, HD), lambda i: (0, i))] * n_groups
        + [pl.BlockSpec((per_half * 2 * part, HD), lambda i: (0, i))] * 2,
        scratch_shapes=[pltpu.VMEM((n_q, HD), BF16)],
        compiler_params=params(),
        cost_estimate=pl.CostEstimate(
            flops=n_q * HD,
            bytes_accessed=2 * n_q * HD,
            transcendentals=0,
        ),
        name="backward",
    )(q, probs, out, inverse, grad_attn, *blocks)
    return results[:n_groups], results[n_groups:]


def frame_block(ids, sign, s, position, n_groups, n_tok):
    group = lax.rem(ids[0] + sign * s + n_groups, n_groups)
    return group * n_tok + jnp.bitwise_xor(ids[1], relative_of(position, bits_of(n_tok)))


def project_kernel(n_groups, n_tok, n_space, ids, attn, *refs):
    blocks, grads = refs[:n_tok], refs[n_tok : n_tok + n_groups * n_space]
    grad_attn, kept, sent, weight, whole, tokens = refs[n_tok + n_groups * n_space :]
    rows, part = grads[0].shape
    depth = weight.shape[0] // (n_groups * n_tok)
    first = blocks[0].shape[0] - n_groups * depth
    for j in range(n_tok):
        for s in range(n_groups):
            place = frame_block(ids, -1, s, j, n_groups, n_tok) * depth
            at = first + s * depth
            weight[pl.ds(aligned(place, 16), depth), :] = blocks[j][at : at + depth, :]
    total = None
    for r in range(n_space):
        for s in range(n_groups):
            tokens[s * rows : (s + 1) * rows, :] = grads[r * n_groups + s][...]
        start = jnp.bitwise_xor(ids[2], relative_of(r, bits_of(n_space))) * part
        block = tokens[...]
        here = pl.ds(aligned(start, 16), part)
        term = dot(block, weight[here, :], ((1,), (0,)))
        total = term if total is None else total + term
        whole[here, :] = dot(block, attn[...], ((0,), (0,))).astype(BF16)
    grad_attn[...] = total.astype(BF16)
    per_half = max(1, n_tok // 2)
    for j in range(n_tok):
        half = sent if j >= per_half else kept
        for s in range(n_groups):
            place = frame_block(ids, 1, s, j, n_groups, n_tok) * depth
            at = (j % per_half * n_groups + s) * depth
            half[at : at + depth, :] = whole[pl.ds(aligned(place, 16), depth), :]


def project(ids, attn, blocks, grads, depth, n_groups, n_tok, n_space):
    n_q, gw = attn.shape
    part = grads[0].shape[1]
    half = n_groups * depth * max(1, n_tok // 2)
    total = n_groups * n_tok * depth
    return whole_call(
        functools.partial(project_kernel, n_groups, n_tok, n_space),
        [jax.ShapeDtypeStruct((n_q, gw), BF16)] + [jax.ShapeDtypeStruct((half, gw), BF16)] * 2,
        (ids, attn, *blocks, *grads),
        "project",
        [
            pltpu.VMEM((total, gw), BF16),
            pltpu.VMEM((total, gw), BF16),
            pltpu.VMEM((n_q, part), BF16),
        ],
        pl.CostEstimate(
            flops=4 * n_q * total * gw,
            bytes_accessed=2 * (n_q * total + 2 * total * gw + 2 * n_q * gw),
            transcendentals=0,
        ),
    )


def add_kernel(ids, kept, other, *outs):
    rows = outs[0].shape[0]
    for i, out in enumerate(outs):
        total = kept[i * rows : (i + 1) * rows, :].astype(F32)
        total = total + other[i * rows : (i + 1) * rows, :].astype(F32)
        out[...] = total.astype(BF16)


def add_parts(ids, kept, other, count):
    rows, gw = kept.shape
    shape = jax.ShapeDtypeStruct((rows // count, gw), BF16)
    return whole_call(add_kernel, [shape] * count, (ids, kept, other), "add_parts")


def halve(ids, kept, sent, n_frame, bits):
    for bit in bits[:-1]:
        other = lax.ppermute(sent, "frame", xor_pairs(n_frame, bit))
        kept, sent = add_parts(ids, kept, other, 2)
    return kept, sent


def finish_kernel(n_groups, ids, kept, other, *refs):
    dq, outs = refs[:n_groups], refs[n_groups:]
    rows = dq[0].shape[0]
    for s in range(n_groups):
        outs[s][:rows, :] = dq[s][...]
        for i in range(2):
            at = (i * n_groups + s) * rows
            total = kept[at : at + rows, :].astype(F32) + other[at : at + rows, :].astype(F32)
            outs[s][(i + 1) * rows : (i + 2) * rows, :] = total.astype(BF16)


def finish(ids, kept, other, dq, n_groups):
    rows, cols = dq[0].shape
    return whole_call(
        functools.partial(finish_kernel, n_groups),
        [jax.ShapeDtypeStruct((3 * rows, cols), BF16)] * n_groups,
        (ids, kept, other, *dq),
        "finish",
    )


def unpack_kernel(n_groups, ids, *refs):
    pieces, outs = refs[:-3], refs[-3:]
    rows, gw = outs[0].shape[0], outs[0].shape[1] // n_groups
    before = 0
    for c in range(0, len(pieces), n_groups):
        cols = pieces[c].shape[1]
        for s in range(n_groups):
            start = lax.rem(ids[0] + s, n_groups) * gw + before
            for i, out in enumerate(outs):
                piece = pieces[c + s][i * rows : (i + 1) * rows, :]
                out[:, pl.ds(aligned(start, HD), cols)] = piece
        before += cols


def unpack(ids, chunks, n_groups):
    rows = chunks[0][0].shape[0] // 3
    gw = sum(pieces[0].shape[1] for pieces in chunks)
    return whole_call(
        functools.partial(unpack_kernel, n_groups),
        [jax.ShapeDtypeStruct((rows, gw * n_groups), BF16)] * 3,
        (ids, *[piece for pieces in chunks for piece in pieces]),
        "unpack",
    )


def join_kernel(n_groups, ids, *refs):
    pieces, out = refs[:n_groups], refs[n_groups]
    gw = pieces[0].shape[1]
    for s in range(n_groups):
        start = lax.rem(ids[0] - s + n_groups, n_groups) * gw
        out[:, pl.ds(aligned(start, HD), gw)] = pieces[s][...].astype(F32)


def join(ids, pieces, n_groups):
    rows, gw = pieces[0].shape
    return whole_call(
        functools.partial(join_kernel, n_groups),
        jax.ShapeDtypeStruct((rows, gw * n_groups), F32),
        (ids, *pieces),
        "join",
    )


def exchange(pieces, n_groups, n_tok, sign):
    return [pieces[0]] + [
        lax.ppermute(pieces[s], "frame", shift_pairs(n_groups, n_tok, sign * s))
        for s in range(1, n_groups)
    ]


def local(queries, keys, values, grad_out, proj_weight):
    n_frame = lax.axis_size("frame")
    n_space = lax.axis_size("space")
    rows, width = queries.shape
    depth = proj_weight.shape[1]
    n_groups = math.gcd(width // HD, n_frame)
    n_tok = n_frame // n_groups
    tok_bits = bits_of(n_tok)
    space_bits = bits_of(n_space)
    heads = width // n_groups // HD
    shared = 2 * rows + depth
    frame = lax.axis_index("frame")
    ids = jnp.stack([frame // n_tok, frame % n_tok, lax.axis_index("space")]).astype(jnp.int32)

    tie = lax.optimization_barrier
    last = xor_pairs(n_frame, tok_bits[-1])

    *pieces, own_q = pack(ids, queries, keys, values, proj_weight.T, n_groups)
    pieces = exchange(pieces, n_groups, n_tok, 1)
    q_pieces = pieces[1:]
    own, others = [pieces[0]], [lax.ppermute(pieces[0], "frame", last)]
    ring = [grad_out]
    across = [gather_blocks(grad_out, "space", n_space, space_bits)]
    for s in range(1, n_groups):
        piece = pieces[s][:shared]
        if s == 1:
            ring[0], piece, others[0], *across[0] = tie((ring[0], piece, others[0], *across[0]))
            ring.append(lax.ppermute(ring[0], "frame", shift_pairs(n_groups, n_tok, 1)))
        own.append(piece)
        others.append(lax.ppermute(piece, "frame", last))
        if s == 1 and n_groups > 2:
            ring[1], others[1], *pieces[2:] = tie((ring[1], others[1], *pieces[2:]))

    for s in range(1, n_groups):
        across.append(gather_blocks(ring[s], "space", n_space, space_bits))
        if s + 1 < n_groups:
            arriving = lax.ppermute(ring[s], "frame", shift_pairs(n_groups, n_tok, 1))
            count = n_groups if s == 1 else 0
            tied = tie((arriving, *across[s], *others[:count]))
            arriving, across[s] = tied[0], list(tied[1 : 1 + n_space])
            others[:count] = tied[1 + n_space :]
            ring.append(arriving)

    q = stack_queries(ids, own_q, q_pieces)
    blocks = [stack(ids, own, rows), stack(ids, others, rows)]
    for bit in reversed(tok_bits[:-1]):
        blocks = blocks + [lax.ppermute(b, "frame", xor_pairs(n_frame, bit)) for b in blocks]
    part = n_groups * rows
    probs, out, inverse = forward(q, blocks, part)
    grads = [across[s][r] for r in range(n_space) for s in range(n_groups)]
    grad_attn, kept, sent = project(ids, out, blocks, grads, depth, n_groups, n_tok, n_space)

    def attention_chunk(head, count, q, *before):
        dq, halves = backward(
            head, count, q, blocks, part, probs, out, inverse, grad_attn, n_groups
        )
        kept, sent, *before = tie((*halves, *before))
        return dq, halve(ids, kept, sent, n_frame, tok_bits), *before

    proj_kept, proj_sent = halve(ids, kept, sent, n_frame, tok_bits)
    dq, (kept, sent) = attention_chunk(0, 1, q)
    returned = []
    if heads > 1:
        q, kept, sent, proj_kept, proj_sent = tie((q, kept, sent, proj_kept, proj_sent))
        other = lax.ppermute(sent, "frame", last)
        next_dq, (next_kept, sent), other = attention_chunk(1, heads - 1, q, other)
        sums = finish(ids, kept, other, dq, n_groups)
        proj_sent, *sums = tie((proj_sent, *sums))
        returned.append(exchange(sums, n_groups, n_tok, -1))
        dq, kept = next_dq, next_kept
    other = lax.ppermute(proj_sent, "frame", last)
    proj = exchange(add_parts(ids, proj_kept, other, n_groups), n_groups, n_tok, 1)
    other = lax.ppermute(sent, "frame", last)
    if returned:
        other, *returned[0][1:-1] = tie((other, *returned[0][1:-1]))
    returned.append(exchange(finish(ids, kept, other, dq, n_groups), n_groups, n_tok, -1))
    grad_proj = join(ids, proj, n_groups).T
    grad_queries, grad_keys, grad_values = unpack(ids, returned, n_groups)
    return (grad_queries, grad_keys, grad_values, grad_proj)


def solution(mesh):
    in_specs = (
        P("frame", "space"),
        P("frame", "space"),
        P("frame", "space"),
        P("frame", "space"),
        P("space", "frame"),
    )
    out_specs = (P("frame", "space"), P("frame", "space"), P("frame", "space"), P("space", "frame"))
    return jax.shard_map(local, mesh=mesh, in_specs=in_specs, out_specs=out_specs, check_vma=False)
```

```python
import functools
import math

import jax
import jax.numpy as jnp
from jax import lax
from jax.experimental import pallas as pl
from jax.experimental.pallas import tpu as pltpu
from jax.sharding import PartitionSpec as P

HD = 128
VMEM_BYTES = 24 * 1024 * 1024
BF16 = jnp.bfloat16
F32 = jnp.float32


def bits_of(count):
    found = []
    bit = 1
    while bit < count:
        found.append(bit)
        bit *= 2
    return found


def relative_of(position, bits):
    total = 0
    for place, bit in enumerate(reversed(bits)):
        if position >> place & 1:
            total |= bit
    return total


def shift_pairs(n_groups, n_tok, step):
    return [
        (g * n_tok + t, (g + step) % n_groups * n_tok + t)
        for g in range(n_groups)
        for t in range(n_tok)
    ]


def xor_pairs(count, bit):
    return [(i, i ^ bit) for i in range(count)]


def gather_blocks(block, axis, count, bits):
    blocks = [block]
    for bit in reversed(bits):
        blocks = blocks + [lax.ppermute(b, axis, xor_pairs(count, bit)) for b in blocks]
    return blocks


def params():
    return pltpu.CompilerParams(vmem_limit_bytes=VMEM_BYTES)


def smem():
    return pl.BlockSpec(memory_space=pltpu.SMEM)


def vmem():
    return pl.BlockSpec(memory_space=pltpu.VMEM)


def aligned(value, unit):
    return pl.multiple_of(value, unit)


def dot(a, b, dims):
    return lax.dot_general(a, b, (dims, ((), ())), preferred_element_type=F32)


def whole_call(body, out_shape, args, name, scratch=(), cost=None):
    single = not isinstance(out_shape, list)
    return pl.pallas_call(
        body,
        out_shape=out_shape,
        in_specs=[smem()] + [vmem()] * (len(args) - 1),
        out_specs=vmem() if single else [vmem()] * len(out_shape),
        scratch_shapes=list(scratch),
        compiler_params=params(),
        cost_estimate=cost,
        name=name,
    )(*args)


def pack_kernel(n_groups, ids, q, k, v, w, *refs):
    outs, sems = refs[:-1], refs[-1]
    rows, depth = q.shape[0], w.shape[0]
    gw = q.shape[1] // n_groups
    copies = []
    for s in range(n_groups):
        cols = pl.ds(aligned(lax.rem(ids[0] + s, n_groups) * gw, HD), gw)
        own = outs[n_groups] if s == 0 else outs[s].at[pl.ds(2 * rows + depth, rows), :]
        for source, target in (
            (k, outs[s].at[pl.ds(0, rows), :]),
            (v, outs[s].at[pl.ds(rows, rows), :]),
            (w, outs[s].at[pl.ds(2 * rows, depth), :]),
            (q, own),
        ):
            copies.append(
                pltpu.make_async_copy(source.at[:, cols], target, sems.at[len(copies)])
            )
    for copy in copies:
        copy.start()
    for copy in copies:
        copy.wait()


def pack(ids, q, k, v, w, n_groups):
    rows, width = q.shape
    gw = width // n_groups
    shared = 2 * rows + w.shape[0]
    shapes = (
        [jax.ShapeDtypeStruct((shared, gw), BF16)]
        + [jax.ShapeDtypeStruct((shared + rows, gw), BF16)] * (n_groups - 1)
        + [jax.ShapeDtypeStruct((rows, gw), BF16)]
    )
    return pl.pallas_call(
        functools.partial(pack_kernel, n_groups),
        out_shape=shapes,
        in_specs=[smem()] + [pl.BlockSpec(memory_space=pltpu.HBM)] * 4,
        out_specs=[vmem()] * len(shapes),
        scratch_shapes=[pltpu.SemaphoreType.DMA((4 * n_groups,))],
        compiler_params=pltpu.CompilerParams(vmem_limit_bytes=60 * 1024 * 1024),
        name="pack",
    )(ids, q, k, v, w)


def stack_kernel(n_groups, rows, ids, *refs):
    pieces, out = refs[:n_groups], refs[n_groups]
    shared = out.shape[0] // n_groups
    depth = shared - 2 * rows
    for s, piece in enumerate(pieces):
        for i in range(2):
            at = (i * n_groups + s) * rows
            out[at : at + rows, :] = piece[i * rows : (i + 1) * rows, :]
        at = 2 * n_groups * rows + s * depth
        out[at : at + depth, :] = piece[2 * rows : shared, :]


def stack(ids, pieces, rows):
    shared, gw = pieces[0].shape
    return whole_call(
        functools.partial(stack_kernel, len(pieces), rows),
        jax.ShapeDtypeStruct((shared * len(pieces), gw), BF16),
        (ids, *pieces),
        "stack",
    )


def stack_queries_kernel(ids, own, *refs):
    pieces, out = refs[:-1], refs[-1]
    rows = own.shape[0]
    out[:rows, :] = own[...]
    for s, piece in enumerate(pieces):
        out[(s + 1) * rows : (s + 2) * rows, :] = piece[piece.shape[0] - rows :, :]


def stack_queries(ids, own, pieces):
    rows, gw = own.shape
    shape = jax.ShapeDtypeStruct((rows * (len(pieces) + 1), gw), BF16)
    return whole_call(stack_queries_kernel, shape, (ids, own, *pieces), "stack_queries")


def forward_kernel(chunk, scale, q_in, *refs):
    blocks, (p_out, o_out, il_out, logits) = refs[:-4], refs[-4:]
    part = blocks[0].shape[0] // 2
    q = q_in[...]
    top = None
    for j, kv in enumerate(blocks):
        for c in range(0, part, chunk):
            at = j * part + c
            block = dot(kv[c : c + chunk, :], q, ((1,), (1,)))
            logits[at : at + chunk, :] = block
            here = jnp.max(block, axis=0, keepdims=True)
            top = here if top is None else jnp.maximum(top, here)
    top = top * scale
    total = jnp.zeros_like(top)
    out = jnp.zeros((HD, q.shape[0]), F32)
    for j, kv in enumerate(blocks):
        for c in range(0, part, chunk):
            at = j * part + c
            prob = jnp.exp2(logits[at : at + chunk, :] * scale - top)
            total = total + jnp.sum(prob, axis=0, keepdims=True)
            low = prob.astype(BF16)
            p_out[0, at : at + chunk, :] = low
            out = out + dot(kv[part + c : part + c + chunk, :], low, ((0,), (0,)))
    inverse = 1.0 / total
    il_out[0] = inverse
    o_out[...] = (out * inverse).T.astype(BF16)


def forward(q, blocks, part):
    n_q, gw = q.shape
    heads = gw // HD
    seq_len = part * len(blocks)
    chunk = part if part <= 640 else math.gcd(part, 512)
    scale = math.log2(math.e) / math.sqrt(HD)
    return pl.pallas_call(
        functools.partial(forward_kernel, chunk, scale),
        grid=(heads,),
        out_shape=[
            jax.ShapeDtypeStruct((heads, seq_len, n_q), BF16),
            jax.ShapeDtypeStruct((n_q, gw), BF16),
            jax.ShapeDtypeStruct((heads, 1, n_q), F32),
        ],
        in_specs=[pl.BlockSpec((n_q, HD), lambda h: (0, h))]
        + [pl.BlockSpec((2 * part, HD), lambda h: (0, h))] * len(blocks),
        out_specs=[
            pl.BlockSpec((1, seq_len, n_q), lambda h: (h, 0, 0)),
            pl.BlockSpec((n_q, HD), lambda h: (0, h)),
            pl.BlockSpec((1, 1, n_q), lambda h: (h, 0, 0)),
        ],
        scratch_shapes=[pltpu.VMEM((seq_len, n_q), F32)],
        compiler_params=params(),
        cost_estimate=pl.CostEstimate(
            flops=4 * heads * seq_len * n_q * HD,
            bytes_accessed=2 * heads * seq_len * n_q,
            transcendentals=heads * seq_len * n_q,
        ),
        name="forward",
    )(q, *blocks)


def backward_kernel(n_groups, chunk, factor, *refs):
    q_in, p_in, o_in, il_in, da_in = refs[:5]
    dq_outs, halves, dq_all = refs[-n_groups - 3 : -3], refs[-3:-1], refs[-1]
    blocks = refs[5 : -n_groups - 3]
    part = blocks[0].shape[0] // 2
    rows = dq_outs[0].shape[0]
    q = q_in[...]
    n_q = q.shape[0]
    inverse = jnp.broadcast_to(il_in[0], (HD, n_q)).T
    da = (da_in[...].astype(F32) * inverse).astype(BF16)
    delta = jnp.sum((da.astype(F32) * o_in[...].astype(F32)).T, axis=0, keepdims=True)
    dq = jnp.zeros((HD, n_q), F32)
    per_half = max(1, len(blocks) // 2)
    for j, kv in enumerate(blocks):
        out = halves[j // per_half]
        base = j % per_half * 2 * part
        for c in range(0, part, chunk):
            at = j * part + c
            low = p_in[0, at : at + chunk, :]
            dp = dot(kv[part + c : part + c + chunk, :], da, ((1,), (1,)))
            ds = (low.astype(F32) * (dp - delta)).astype(BF16)
            dk = (factor * dot(ds, q, ((1,), (0,)))).astype(BF16)
            out[base + c : base + c + chunk, :] = dk
            dv = dot(low, da, ((1,), (0,))).astype(BF16)
            out[base + part + c : base + part + c + chunk, :] = dv
            dq = dq + dot(kv[c : c + chunk, :], ds, ((0,), (0,)))
    dq_all[...] = (factor * dq).T.astype(BF16)
    for s in range(n_groups):
        dq_outs[s][...] = dq_all[s * rows : (s + 1) * rows, :]


def backward(head, count, q, blocks, part, probs, out, inverse, grad_attn, n_groups):
    n_q = q.shape[0]
    rows = n_q // n_groups
    seq_len = part * len(blocks)
    chunk = part if part <= 640 else math.gcd(part, 512)
    per_half = max(1, len(blocks) // 2)
    column = pl.BlockSpec((n_q, HD), lambda i: (0, head + i))
    results = pl.pallas_call(
        functools.partial(backward_kernel, n_groups, chunk, 1.0 / math.sqrt(HD)),
        grid=(count,),
        out_shape=[jax.ShapeDtypeStruct((rows, count * HD), BF16)] * n_groups
        + [jax.ShapeDtypeStruct((per_half * 2 * part, count * HD), BF16)] * 2,
        in_specs=[
            column,
            pl.BlockSpec((1, seq_len, n_q), lambda i: (head + i, 0, 0)),
            column,
            pl.BlockSpec((1, 1, n_q), lambda i: (head + i, 0, 0)),
            column,
        ]
        + [pl.BlockSpec((2 * part, HD), lambda i: (0, head + i))] * len(blocks),
        out_specs=[pl.BlockSpec((rows, HD), lambda i: (0, i))] * n_groups
        + [pl.BlockSpec((per_half * 2 * part, HD), lambda i: (0, i))] * 2,
        scratch_shapes=[pltpu.VMEM((n_q, HD), BF16)],
        compiler_params=params(),
        cost_estimate=pl.CostEstimate(
            flops=n_q * HD,
            bytes_accessed=2 * n_q * HD,
            transcendentals=0,
        ),
        name="backward",
    )(q, probs, out, inverse, grad_attn, *blocks)
    return results[:n_groups], results[n_groups:]


def frame_block(ids, sign, s, position, n_groups, n_tok):
    group = lax.rem(ids[0] + sign * s + n_groups, n_groups)
    return group * n_tok + jnp.bitwise_xor(ids[1], relative_of(position, bits_of(n_tok)))


def project_kernel(n_groups, n_tok, n_space, ids, attn, *refs):
    blocks, grads = refs[:n_tok], refs[n_tok : n_tok + n_groups * n_space]
    grad_attn, kept, sent, weight, whole, tokens = refs[n_tok + n_groups * n_space :]
    rows, part = grads[0].shape
    depth = weight.shape[0] // (n_groups * n_tok)
    first = blocks[0].shape[0] - n_groups * depth
    for j in range(n_tok):
        for s in range(n_groups):
            place = frame_block(ids, -1, s, j, n_groups, n_tok) * depth
            at = first + s * depth
            weight[pl.ds(aligned(place, 16), depth), :] = blocks[j][at : at + depth, :]
    total = None
    for r in range(n_space):
        for s in range(n_groups):
            tokens[s * rows : (s + 1) * rows, :] = grads[r * n_groups + s][...]
        start = jnp.bitwise_xor(ids[2], relative_of(r, bits_of(n_space))) * part
        block = tokens[...]
        here = pl.ds(aligned(start, 16), part)
        term = dot(block, weight[here, :], ((1,), (0,)))
        total = term if total is None else total + term
        whole[here, :] = dot(block, attn[...], ((0,), (0,))).astype(BF16)
    grad_attn[...] = total.astype(BF16)
    per_half = max(1, n_tok // 2)
    for j in range(n_tok):
        half = sent if j >= per_half else kept
        for s in range(n_groups):
            place = frame_block(ids, 1, s, j, n_groups, n_tok) * depth
            at = (j % per_half * n_groups + s) * depth
            half[at : at + depth, :] = whole[pl.ds(aligned(place, 16), depth), :]


def project(ids, attn, blocks, grads, depth, n_groups, n_tok, n_space):
    n_q, gw = attn.shape
    part = grads[0].shape[1]
    half = n_groups * depth * max(1, n_tok // 2)
    total = n_groups * n_tok * depth
    return whole_call(
        functools.partial(project_kernel, n_groups, n_tok, n_space),
        [jax.ShapeDtypeStruct((n_q, gw), BF16)] + [jax.ShapeDtypeStruct((half, gw), BF16)] * 2,
        (ids, attn, *blocks, *grads),
        "project",
        [
            pltpu.VMEM((total, gw), BF16),
            pltpu.VMEM((total, gw), BF16),
            pltpu.VMEM((n_q, part), BF16),
        ],
        pl.CostEstimate(
            flops=4 * n_q * total * gw,
            bytes_accessed=2 * (n_q * total + 2 * total * gw + 2 * n_q * gw),
            transcendentals=0,
        ),
    )


def add_kernel(ids, kept, other, *outs):
    rows = outs[0].shape[0]
    for i, out in enumerate(outs):
        total = kept[i * rows : (i + 1) * rows, :].astype(F32)
        total = total + other[i * rows : (i + 1) * rows, :].astype(F32)
        out[...] = total.astype(BF16)


def add_parts(ids, kept, other, count):
    rows, gw = kept.shape
    shape = jax.ShapeDtypeStruct((rows // count, gw), BF16)
    return whole_call(add_kernel, [shape] * count, (ids, kept, other), "add_parts")


def halve(ids, kept, sent, n_frame, bits):
    for bit in bits[:-1]:
        other = lax.ppermute(sent, "frame", xor_pairs(n_frame, bit))
        kept, sent = add_parts(ids, kept, other, 2)
    return kept, sent


def finish_kernel(n_groups, ids, kept, other, *refs):
    dq, outs = refs[:n_groups], refs[-n_groups:]
    rows, cols = dq[0].shape
    for s in range(n_groups):
        outs[s][:rows, :cols] = dq[s][...]
        for i in range(2):
            at = (i * n_groups + s) * rows
            total = kept[at : at + rows, :].astype(F32) + other[at : at + rows, :].astype(F32)
            outs[s][:rows, (i + 1) * cols : (i + 2) * cols] = total.astype(BF16)
    if len(refs) > 2 * n_groups:
        proj_kept, proj_other = refs[n_groups : n_groups + 2]
        depth = proj_kept.shape[0] // n_groups
        wide = proj_kept.shape[1]
        for s in range(n_groups):
            here = pl.ds(((n_groups - s) % n_groups) * depth, depth)
            total = proj_kept[here, :].astype(F32) + proj_other[here, :].astype(F32)
            outs[s][rows:, :wide] = total.astype(BF16)


def finish(ids, kept, other, dq, n_groups, *proj):
    rows, cols = dq[0].shape
    wide = 3 * cols
    if proj:
        wide = max(wide, proj[0].shape[1])
        rows = rows + proj[0].shape[0] // n_groups
    return whole_call(
        functools.partial(finish_kernel, n_groups),
        [jax.ShapeDtypeStruct((rows, wide), BF16)] * n_groups,
        (ids, kept, other, *dq, *proj),
        "finish",
    )


def unpack_kernel(n_groups, widths, ids, *refs):
    pieces, outs = refs[:-3], refs[-3:]
    rows, gw = outs[0].shape[0], outs[0].shape[1] // n_groups
    before = 0
    for c, cols in enumerate(widths):
        for s in range(n_groups):
            start = lax.rem(ids[0] + s, n_groups) * gw + before
            for i, out in enumerate(outs):
                piece = pieces[c * n_groups + s][:rows, i * cols : (i + 1) * cols]
                out[:, pl.ds(aligned(start, HD), cols)] = piece
        before += cols


def unpack(ids, chunks, rows, gw, n_groups):
    widths = [HD, gw - HD][: len(chunks)]
    return whole_call(
        functools.partial(unpack_kernel, n_groups, widths),
        [jax.ShapeDtypeStruct((rows, gw * n_groups), BF16)] * 3,
        (ids, *[piece for pieces in chunks for piece in pieces]),
        "unpack",
    )


def join_kernel(n_groups, rows, gw, ids, *refs):
    pieces, out = refs[:n_groups], refs[n_groups]
    for s in range(n_groups):
        start = lax.rem(ids[0] + s, n_groups) * gw
        out[:, pl.ds(aligned(start, HD), gw)] = pieces[s][rows:, :gw].astype(F32)


def join(ids, pieces, rows, gw, n_groups):
    depth = pieces[0].shape[0] - rows
    return whole_call(
        functools.partial(join_kernel, n_groups, rows, gw),
        jax.ShapeDtypeStruct((depth, gw * n_groups), F32),
        (ids, *pieces),
        "join",
    )


def exchange(pieces, n_groups, n_tok, sign):
    return [pieces[0]] + [
        lax.ppermute(pieces[s], "frame", shift_pairs(n_groups, n_tok, sign * s))
        for s in range(1, n_groups)
    ]


def local(queries, keys, values, grad_out, proj_weight):
    n_frame = lax.axis_size("frame")
    n_space = lax.axis_size("space")
    rows, width = queries.shape
    gw = width // math.gcd(width // HD, n_frame)
    depth = proj_weight.shape[1]
    n_groups = math.gcd(width // HD, n_frame)
    n_tok = n_frame // n_groups
    tok_bits = bits_of(n_tok)
    space_bits = bits_of(n_space)
    heads = width // n_groups // HD
    shared = 2 * rows + depth
    frame = lax.axis_index("frame")
    ids = jnp.stack([frame // n_tok, frame % n_tok, lax.axis_index("space")]).astype(jnp.int32)

    tie = lax.optimization_barrier
    last = xor_pairs(n_frame, tok_bits[-1])

    *pieces, own_q = pack(ids, queries, keys, values, proj_weight.T, n_groups)
    pieces = exchange(pieces, n_groups, n_tok, 1)
    q_pieces = pieces[1:]
    own, others, ring, across = [pieces[0]], [], grad_out, []
    for s in range(n_groups):
        others.append(lax.ppermute(own[s], "frame", last))
        across.append(gather_blocks(ring, "space", n_space, space_bits))
        if s + 1 < n_groups:
            ring = lax.ppermute(ring, "frame", shift_pairs(n_groups, n_tok, 1))
            step = (ring, pieces[s + 1][:shared], others[s], *across[s])
            ring, piece, others[s], *across[s] = tie(step)
            own.append(piece)

    q = stack_queries(ids, own_q, q_pieces)
    blocks = [stack(ids, own, rows), stack(ids, others, rows)]
    for bit in reversed(tok_bits[:-1]):
        blocks = blocks + [lax.ppermute(b, "frame", xor_pairs(n_frame, bit)) for b in blocks]
    part = n_groups * rows
    probs, out, inverse = forward(q, blocks, part)
    grads = [across[s][r] for r in range(n_space) for s in range(n_groups)]
    grad_attn, kept, sent = project(ids, out, blocks, grads, depth, n_groups, n_tok, n_space)

    def attention_chunk(head, count, q, *before):
        dq, halves = backward(
            head, count, q, blocks, part, probs, out, inverse, grad_attn, n_groups
        )
        kept, sent, *before = tie((*halves, *before))
        return dq, halve(ids, kept, sent, n_frame, tok_bits), *before

    proj_kept, proj_sent = halve(ids, kept, sent, n_frame, tok_bits)
    dq, (kept, sent) = attention_chunk(0, 1, q)
    q, kept, sent, proj_kept, proj_sent = tie((q, kept, sent, proj_kept, proj_sent))
    other = lax.ppermute(sent, "frame", last)
    proj_other = lax.ppermute(proj_sent, "frame", last)
    if heads > 1:
        dq_rest, (kept_rest, sent_rest), other, proj_other = attention_chunk(
            1, heads - 1, q, other, proj_other
        )
    sums = finish(ids, kept, other, dq, n_groups, proj_kept, proj_other)
    first = exchange(sums, n_groups, n_tok, -1)
    returned = [first]
    if heads > 1:
        other = lax.ppermute(sent_rest, "frame", last)
        sums = finish(ids, kept_rest, other, dq_rest, n_groups)
        returned.append(exchange(sums, n_groups, n_tok, -1))
    grad_proj = join(ids, first, rows, gw, n_groups).T
    grad_queries, grad_keys, grad_values = unpack(ids, returned, rows, gw, n_groups)
    return (grad_queries, grad_keys, grad_values, grad_proj)


def solution(mesh):
    in_specs = (
        P("frame", "space"),
        P("frame", "space"),
        P("frame", "space"),
        P("frame", "space"),
        P("space", "frame"),
    )
    out_specs = (P("frame", "space"), P("frame", "space"), P("frame", "space"), P("space", "frame"))
    return jax.shard_map(local, mesh=mesh, in_specs=in_specs, out_specs=out_specs, check_vma=False)
```

```python
import functools
import math

import jax
import jax.numpy as jnp
from jax import lax
from jax.experimental import pallas as pl
from jax.experimental.pallas import tpu as pltpu
from jax.sharding import PartitionSpec as P

HD = 128
VMEM_BYTES = 24 * 1024 * 1024
BF16 = jnp.bfloat16
F32 = jnp.float32


def bits_of(count):
    found = []
    bit = 1
    while bit < count:
        found.append(bit)
        bit *= 2
    return found


def relative_of(position, bits):
    total = 0
    for place, bit in enumerate(reversed(bits)):
        if position >> place & 1:
            total |= bit
    return total


def shift_pairs(n_groups, n_tok, step):
    return [
        (g * n_tok + t, (g + step) % n_groups * n_tok + t)
        for g in range(n_groups)
        for t in range(n_tok)
    ]


def xor_pairs(count, bit):
    return [(i, i ^ bit) for i in range(count)]


def gather_blocks(block, axis, count, bits):
    blocks = [block]
    for bit in reversed(bits):
        blocks = blocks + [lax.ppermute(b, axis, xor_pairs(count, bit)) for b in blocks]
    return blocks


def params():
    return pltpu.CompilerParams(vmem_limit_bytes=VMEM_BYTES)


def smem():
    return pl.BlockSpec(memory_space=pltpu.SMEM)


def vmem():
    return pl.BlockSpec(memory_space=pltpu.VMEM)


def aligned(value, unit):
    return pl.multiple_of(value, unit)


def dot(a, b, dims):
    return lax.dot_general(a, b, (dims, ((), ())), preferred_element_type=F32)


def whole_call(body, out_shape, args, name, scratch=(), cost=None):
    single = not isinstance(out_shape, list)
    return pl.pallas_call(
        body,
        out_shape=out_shape,
        in_specs=[smem()] + [vmem()] * (len(args) - 1),
        out_specs=vmem() if single else [vmem()] * len(out_shape),
        scratch_shapes=list(scratch),
        compiler_params=params(),
        cost_estimate=cost,
        name=name,
    )(*args)


def pack_kernel(n_groups, ids, q, k, v, w, *refs):
    outs, sems = refs[:-1], refs[-1]
    rows, depth = q.shape[0], w.shape[0]
    gw = q.shape[1] // n_groups
    copies = []
    for s in range(n_groups):
        cols = pl.ds(aligned(lax.rem(ids[0] + s, n_groups) * gw, HD), gw)
        own = outs[n_groups] if s == 0 else outs[s].at[pl.ds(2 * rows + depth, rows), :]
        for source, target in (
            (k, outs[s].at[pl.ds(0, rows), :]),
            (v, outs[s].at[pl.ds(rows, rows), :]),
            (w, outs[s].at[pl.ds(2 * rows, depth), :]),
            (q, own),
        ):
            copies.append(
                pltpu.make_async_copy(source.at[:, cols], target, sems.at[len(copies)])
            )
    for copy in copies:
        copy.start()
    for copy in copies:
        copy.wait()


def pack(ids, q, k, v, w, n_groups):
    rows, width = q.shape
    gw = width // n_groups
    shared = 2 * rows + w.shape[0]
    shapes = (
        [jax.ShapeDtypeStruct((shared, gw), BF16)]
        + [jax.ShapeDtypeStruct((shared + rows, gw), BF16)] * (n_groups - 1)
        + [jax.ShapeDtypeStruct((rows, gw), BF16)]
    )
    return pl.pallas_call(
        functools.partial(pack_kernel, n_groups),
        out_shape=shapes,
        in_specs=[smem()] + [pl.BlockSpec(memory_space=pltpu.HBM)] * 4,
        out_specs=[vmem()] * len(shapes),
        scratch_shapes=[pltpu.SemaphoreType.DMA((4 * n_groups,))],
        compiler_params=pltpu.CompilerParams(vmem_limit_bytes=60 * 1024 * 1024),
        name="pack",
    )(ids, q, k, v, w)


def stack_kernel(n_groups, rows, ids, *refs):
    pieces, out = refs[:n_groups], refs[n_groups]
    shared = out.shape[0] // n_groups
    depth = shared - 2 * rows
    for s, piece in enumerate(pieces):
        for i in range(2):
            at = (i * n_groups + s) * rows
            out[at : at + rows, :] = piece[i * rows : (i + 1) * rows, :]
        at = 2 * n_groups * rows + s * depth
        out[at : at + depth, :] = piece[2 * rows : shared, :]


def stack(ids, pieces, rows):
    shared, gw = pieces[0].shape
    return whole_call(
        functools.partial(stack_kernel, len(pieces), rows),
        jax.ShapeDtypeStruct((shared * len(pieces), gw), BF16),
        (ids, *pieces),
        "stack",
    )


def stack_queries_kernel(ids, own, *refs):
    pieces, out = refs[:-1], refs[-1]
    rows = own.shape[0]
    out[:rows, :] = own[...]
    for s, piece in enumerate(pieces):
        out[(s + 1) * rows : (s + 2) * rows, :] = piece[piece.shape[0] - rows :, :]


def stack_queries(ids, own, pieces):
    rows, gw = own.shape
    shape = jax.ShapeDtypeStruct((rows * (len(pieces) + 1), gw), BF16)
    return whole_call(stack_queries_kernel, shape, (ids, own, *pieces), "stack_queries")


def forward_kernel(chunk, scale, q_in, *refs):
    blocks, (p_out, o_out, il_out, logits) = refs[:-4], refs[-4:]
    part = blocks[0].shape[0] // 2
    q = q_in[...]
    top = None
    for j, kv in enumerate(blocks):
        for c in range(0, part, chunk):
            at = j * part + c
            block = dot(kv[c : c + chunk, :], q, ((1,), (1,)))
            logits[at : at + chunk, :] = block
            here = jnp.max(block, axis=0, keepdims=True)
            top = here if top is None else jnp.maximum(top, here)
    top = top * scale
    total = jnp.zeros_like(top)
    out = jnp.zeros((HD, q.shape[0]), F32)
    for j, kv in enumerate(blocks):
        for c in range(0, part, chunk):
            at = j * part + c
            prob = jnp.exp2(logits[at : at + chunk, :] * scale - top)
            total = total + jnp.sum(prob, axis=0, keepdims=True)
            low = prob.astype(BF16)
            p_out[0, at : at + chunk, :] = low
            out = out + dot(kv[part + c : part + c + chunk, :], low, ((0,), (0,)))
    inverse = 1.0 / total
    il_out[0] = inverse
    o_out[...] = (out * inverse).T.astype(BF16)


def forward(q, blocks, part):
    n_q, gw = q.shape
    heads = gw // HD
    seq_len = part * len(blocks)
    chunk = part if part <= 640 else math.gcd(part, 512)
    scale = math.log2(math.e) / math.sqrt(HD)
    return pl.pallas_call(
        functools.partial(forward_kernel, chunk, scale),
        grid=(heads,),
        out_shape=[
            jax.ShapeDtypeStruct((heads, seq_len, n_q), BF16),
            jax.ShapeDtypeStruct((n_q, gw), BF16),
            jax.ShapeDtypeStruct((heads, 1, n_q), F32),
        ],
        in_specs=[pl.BlockSpec((n_q, HD), lambda h: (0, h))]
        + [pl.BlockSpec((2 * part, HD), lambda h: (0, h))] * len(blocks),
        out_specs=[
            pl.BlockSpec((1, seq_len, n_q), lambda h: (h, 0, 0)),
            pl.BlockSpec((n_q, HD), lambda h: (0, h)),
            pl.BlockSpec((1, 1, n_q), lambda h: (h, 0, 0)),
        ],
        scratch_shapes=[pltpu.VMEM((seq_len, n_q), F32)],
        compiler_params=params(),
        cost_estimate=pl.CostEstimate(
            flops=4 * heads * seq_len * n_q * HD,
            bytes_accessed=2 * heads * seq_len * n_q,
            transcendentals=heads * seq_len * n_q,
        ),
        name="forward",
    )(q, *blocks)


def backward_kernel(n_groups, chunk, factor, *refs):
    q_in, p_in, o_in, il_in, da_in = refs[:5]
    dq_outs, halves, dq_all = refs[-n_groups - 3 : -3], refs[-3:-1], refs[-1]
    blocks = refs[5 : -n_groups - 3]
    part = blocks[0].shape[0] // 2
    rows = dq_outs[0].shape[0]
    q = q_in[...]
    n_q = q.shape[0]
    inverse = jnp.broadcast_to(il_in[0], (HD, n_q)).T
    da = (da_in[...].astype(F32) * inverse).astype(BF16)
    delta = jnp.sum((da.astype(F32) * o_in[...].astype(F32)).T, axis=0, keepdims=True)
    dq = jnp.zeros((HD, n_q), F32)
    per_half = max(1, len(blocks) // 2)
    for j, kv in enumerate(blocks):
        out = halves[j // per_half]
        base = j % per_half * 2 * part
        for c in range(0, part, chunk):
            at = j * part + c
            low = p_in[0, at : at + chunk, :]
            dp = dot(kv[part + c : part + c + chunk, :], da, ((1,), (1,)))
            ds = (low.astype(F32) * (dp - delta)).astype(BF16)
            dk = (factor * dot(ds, q, ((1,), (0,)))).astype(BF16)
            out[base + c : base + c + chunk, :] = dk
            dv = dot(low, da, ((1,), (0,))).astype(BF16)
            out[base + part + c : base + part + c + chunk, :] = dv
            dq = dq + dot(kv[c : c + chunk, :], ds, ((0,), (0,)))
    dq_all[...] = (factor * dq).T.astype(BF16)
    for s in range(n_groups):
        dq_outs[s][...] = dq_all[s * rows : (s + 1) * rows, :]


def backward(head, count, q, blocks, part, probs, out, inverse, grad_attn, n_groups):
    n_q = q.shape[0]
    rows = n_q // n_groups
    seq_len = part * len(blocks)
    chunk = part if part <= 640 else math.gcd(part, 512)
    per_half = max(1, len(blocks) // 2)
    column = pl.BlockSpec((n_q, HD), lambda i: (0, head + i))
    results = pl.pallas_call(
        functools.partial(backward_kernel, n_groups, chunk, 1.0 / math.sqrt(HD)),
        grid=(count,),
        out_shape=[jax.ShapeDtypeStruct((rows, count * HD), BF16)] * n_groups
        + [jax.ShapeDtypeStruct((per_half * 2 * part, count * HD), BF16)] * 2,
        in_specs=[
            column,
            pl.BlockSpec((1, seq_len, n_q), lambda i: (head + i, 0, 0)),
            column,
            pl.BlockSpec((1, 1, n_q), lambda i: (head + i, 0, 0)),
            column,
        ]
        + [pl.BlockSpec((2 * part, HD), lambda i: (0, head + i))] * len(blocks),
        out_specs=[pl.BlockSpec((rows, HD), lambda i: (0, i))] * n_groups
        + [pl.BlockSpec((per_half * 2 * part, HD), lambda i: (0, i))] * 2,
        scratch_shapes=[pltpu.VMEM((n_q, HD), BF16)],
        compiler_params=params(),
        cost_estimate=pl.CostEstimate(
            flops=n_q * HD,
            bytes_accessed=2 * n_q * HD,
            transcendentals=0,
        ),
        name="backward",
    )(q, probs, out, inverse, grad_attn, *blocks)
    return results[:n_groups], results[n_groups:]


def frame_block(ids, sign, s, position, n_groups, n_tok):
    group = lax.rem(ids[0] + sign * s + n_groups, n_groups)
    return group * n_tok + jnp.bitwise_xor(ids[1], relative_of(position, bits_of(n_tok)))


def tokens_of(ids, tokens, grads, n_groups, n_space):
    rows, part = grads[0].shape
    for r in range(n_space):
        for s in range(n_groups):
            tokens[s * rows : (s + 1) * rows, :] = grads[r * n_groups + s][...]
        start = jnp.bitwise_xor(ids[2], relative_of(r, bits_of(n_space))) * part
        yield tokens[...], pl.ds(aligned(start, 16), part)


def attn_kernel(n_groups, n_tok, n_space, ids, *refs):
    blocks, grads = refs[:n_tok], refs[n_tok : n_tok + n_groups * n_space]
    grad_attn, weight, tokens = refs[n_tok + n_groups * n_space :]
    depth = weight.shape[0] // (n_groups * n_tok)
    first = blocks[0].shape[0] - n_groups * depth
    for j in range(n_tok):
        for s in range(n_groups):
            place = frame_block(ids, -1, s, j, n_groups, n_tok) * depth
            at = first + s * depth
            weight[pl.ds(aligned(place, 16), depth), :] = blocks[j][at : at + depth, :]
    total = None
    for block, here in tokens_of(ids, tokens, grads, n_groups, n_space):
        term = dot(block, weight[here, :], ((1,), (0,)))
        total = term if total is None else total + term
    grad_attn[...] = total.astype(BF16)


def projection_cost(n_q, total, gw):
    return pl.CostEstimate(
        flops=2 * n_q * total * gw,
        bytes_accessed=2 * (n_q * total + total * gw + n_q * gw),
        transcendentals=0,
    )


def attn_gradient(ids, blocks, grads, depth, n_groups, n_tok, n_space):
    rows, part = grads[0].shape
    n_q, gw = rows * n_groups, blocks[0].shape[1]
    total = n_groups * n_tok * depth
    return whole_call(
        functools.partial(attn_kernel, n_groups, n_tok, n_space),
        jax.ShapeDtypeStruct((n_q, gw), BF16),
        (ids, *blocks, *grads),
        "attn_gradient",
        [pltpu.VMEM((total, gw), BF16), pltpu.VMEM((n_q, part), BF16)],
        projection_cost(n_q, total, gw),
    )


def proj_kernel(n_groups, n_tok, n_space, ids, attn, *refs):
    grads, (kept, sent, whole, tokens) = refs[: n_groups * n_space], refs[n_groups * n_space :]
    depth = whole.shape[0] // (n_groups * n_tok)
    for block, here in tokens_of(ids, tokens, grads, n_groups, n_space):
        whole[here, :] = dot(block, attn[...], ((0,), (0,))).astype(BF16)
    per_half = max(1, n_tok // 2)
    for j in range(n_tok):
        half = sent if j >= per_half else kept
        for s in range(n_groups):
            place = frame_block(ids, 1, s, j, n_groups, n_tok) * depth
            at = (j % per_half * n_groups + s) * depth
            half[at : at + depth, :] = whole[pl.ds(aligned(place, 16), depth), :]


def proj_gradient(ids, attn, grads, depth, n_groups, n_tok, n_space):
    n_q, gw = attn.shape
    part = grads[0].shape[1]
    half = n_groups * depth * max(1, n_tok // 2)
    total = n_groups * n_tok * depth
    return whole_call(
        functools.partial(proj_kernel, n_groups, n_tok, n_space),
        [jax.ShapeDtypeStruct((half, gw), BF16)] * 2,
        (ids, attn, *grads),
        "proj_gradient",
        [pltpu.VMEM((total, gw), BF16), pltpu.VMEM((n_q, part), BF16)],
        projection_cost(n_q, total, gw),
    )


def add_kernel(ids, kept, other, *outs):
    rows = outs[0].shape[0]
    for i, out in enumerate(outs):
        total = kept[i * rows : (i + 1) * rows, :].astype(F32)
        total = total + other[i * rows : (i + 1) * rows, :].astype(F32)
        out[...] = total.astype(BF16)


def add_parts(ids, kept, other, count):
    rows, gw = kept.shape
    shape = jax.ShapeDtypeStruct((rows // count, gw), BF16)
    return whole_call(add_kernel, [shape] * count, (ids, kept, other), "add_parts")


def halve(ids, kept, sent, n_frame, bits):
    for bit in bits[:-1]:
        other = lax.ppermute(sent, "frame", xor_pairs(n_frame, bit))
        kept, sent = add_parts(ids, kept, other, 2)
    return kept, sent


def finish_kernel(n_groups, ids, kept, other, *refs):
    dq, outs = refs[:n_groups], refs[n_groups:]
    rows = dq[0].shape[0]
    for s in range(n_groups):
        outs[s][:rows, :] = dq[s][...]
        for i in range(2):
            at = (i * n_groups + s) * rows
            total = kept[at : at + rows, :].astype(F32) + other[at : at + rows, :].astype(F32)
            outs[s][(i + 1) * rows : (i + 2) * rows, :] = total.astype(BF16)


def finish(ids, kept, other, dq, n_groups):
    rows, cols = dq[0].shape
    return whole_call(
        functools.partial(finish_kernel, n_groups),
        [jax.ShapeDtypeStruct((3 * rows, cols), BF16)] * n_groups,
        (ids, kept, other, *dq),
        "finish",
    )


def unpack_kernel(n_groups, widths, ids, *refs):
    pieces, outs = refs[:-3], refs[-3:]
    rows, gw = outs[0].shape[0], outs[0].shape[1] // n_groups
    before = 0
    for c, cols in enumerate(widths):
        for s in range(n_groups):
            start = lax.rem(ids[0] + s, n_groups) * gw + before
            for i, out in enumerate(outs):
                piece = pieces[c * n_groups + s][i * rows : (i + 1) * rows, :]
                out[:, pl.ds(aligned(start, HD), cols)] = piece
        before += cols


def unpack(ids, chunks, rows, gw, n_groups):
    widths = [HD, gw - HD][: len(chunks)]
    return whole_call(
        functools.partial(unpack_kernel, n_groups, widths),
        [jax.ShapeDtypeStruct((rows, gw * n_groups), BF16)] * 3,
        (ids, *[piece for pieces in chunks for piece in pieces]),
        "unpack",
    )


def join_kernel(n_groups, ids, *refs):
    pieces, out = refs[:n_groups], refs[n_groups]
    gw = pieces[0].shape[1]
    for s in range(n_groups):
        start = lax.rem(ids[0] - s + n_groups, n_groups) * gw
        out[:, pl.ds(aligned(start, HD), gw)] = pieces[s][...].astype(F32)


def join(ids, pieces, n_groups):
    rows, gw = pieces[0].shape
    return whole_call(
        functools.partial(join_kernel, n_groups),
        jax.ShapeDtypeStruct((rows, gw * n_groups), F32),
        (ids, *pieces),
        "join",
    )


def exchange(pieces, n_groups, n_tok, sign):
    return [pieces[0]] + [
        lax.ppermute(pieces[s], "frame", shift_pairs(n_groups, n_tok, sign * s))
        for s in range(1, n_groups)
    ]


def local(queries, keys, values, grad_out, proj_weight):
    n_frame = lax.axis_size("frame")
    n_space = lax.axis_size("space")
    rows, width = queries.shape
    gw = width // math.gcd(width // HD, n_frame)
    depth = proj_weight.shape[1]
    n_groups = math.gcd(width // HD, n_frame)
    n_tok = n_frame // n_groups
    tok_bits = bits_of(n_tok)
    space_bits = bits_of(n_space)
    heads = width // n_groups // HD
    shared = 2 * rows + depth
    frame = lax.axis_index("frame")
    ids = jnp.stack([frame // n_tok, frame % n_tok, lax.axis_index("space")]).astype(jnp.int32)

    tie = lax.optimization_barrier
    last = xor_pairs(n_frame, tok_bits[-1])

    *pieces, own_q = pack(ids, queries, keys, values, proj_weight.T, n_groups)
    pieces = exchange(pieces, n_groups, n_tok, 1)
    q_pieces = pieces[1:]
    middle = n_groups // 2
    plan = [[middle], [s for s in range(1, n_groups) if s != middle]]
    others, ring, across, here = [None] * n_groups, grad_out, [], [0]
    for step in range(n_groups):
        for s in here:
            pieces[s] = pieces[s][:shared]
            others[s] = lax.ppermute(pieces[s], "frame", last)
        across.append(gather_blocks(ring, "space", n_space, space_bits))
        if step + 1 < n_groups:
            ring = lax.ppermute(ring, "frame", shift_pairs(n_groups, n_tok, 1))
            coming = plan[step] if step < len(plan) else []
            sent = here if coming else []
            values_of = [ring, *across[step]]
            values_of += [pieces[s] for s in coming] + [others[s] for s in sent]
            ring, *tied = tie(tuple(values_of))
            across[step] = tied[:n_space]
            for s, piece in zip(coming, tied[n_space:]):
                pieces[s] = piece
            for s, piece in zip(sent, tied[n_space + len(coming) :]):
                others[s] = piece
            here = coming
    own = pieces

    q = stack_queries(ids, own_q, q_pieces)
    blocks = [stack(ids, own, rows), stack(ids, others, rows)]
    for bit in reversed(tok_bits[:-1]):
        blocks = blocks + [lax.ppermute(b, "frame", xor_pairs(n_frame, bit)) for b in blocks]
    part = n_groups * rows
    probs, out, inverse = forward(q, blocks, part)
    grads = [across[s][r] for r in range(n_space) for s in range(n_groups)]
    grad_attn = attn_gradient(ids, blocks, grads, depth, n_groups, n_tok, n_space)

    def attention_halves(head, count, q):
        return backward(head, count, q, blocks, part, probs, out, inverse, grad_attn, n_groups)

    def across_x(piece):
        return lax.ppermute(piece, "frame", last)

    dq, (kept, sent) = attention_halves(0, 1, q)
    out_after, kept, sent = tie((out, kept, sent))
    kept, sent = halve(ids, kept, sent, n_frame, tok_bits)
    proj = proj_gradient(ids, out_after, grads, depth, n_groups, n_tok, n_space)
    q, kept, sent, *proj = tie((q, kept, sent, *proj))
    other = across_x(sent)
    proj_kept, proj_sent = halve(ids, *proj, n_frame, tok_bits)
    if heads > 1:
        dq_rest, halves = attention_halves(1, heads - 1, q)
        other, proj_sent, *halves = tie((other, proj_sent, *halves))
    sums = finish(ids, kept, other, dq, n_groups)
    proj_sent, *sums = tie((proj_sent, *sums))
    returned = [exchange(sums, n_groups, n_tok, -1)]
    proj_other = across_x(proj_sent)
    if heads > 1:
        kept, sent = halve(ids, *halves, n_frame, tok_bits)
        proj_other, sent, *returned[0][1:] = tie((proj_other, sent, *returned[0][1:]))
    proj_pieces = exchange(add_parts(ids, proj_kept, proj_other, n_groups), n_groups, n_tok, 1)
    if heads > 1:
        other, *proj_pieces[1:] = tie((across_x(sent), *proj_pieces[1:]))
        sums = finish(ids, kept, other, dq_rest, n_groups)
        returned.append(exchange(sums, n_groups, n_tok, -1))
    grad_proj = join(ids, proj_pieces, n_groups).T
    grad_queries, grad_keys, grad_values = unpack(ids, returned, rows, gw, n_groups)
    return (grad_queries, grad_keys, grad_values, grad_proj)


def solution(mesh):
    in_specs = (
        P("frame", "space"),
        P("frame", "space"),
        P("frame", "space"),
        P("frame", "space"),
        P("space", "frame"),
    )
    out_specs = (P("frame", "space"), P("frame", "space"), P("frame", "space"), P("space", "frame"))
    return jax.shard_map(local, mesh=mesh, in_specs=in_specs, out_specs=out_specs, check_vma=False)
```

```python
import functools
import math

import jax
import jax.numpy as jnp
from jax import lax
from jax.experimental import pallas as pl
from jax.experimental.pallas import tpu as pltpu
from jax.sharding import PartitionSpec as P

HD = 128
VMEM_BYTES = 24 * 1024 * 1024
BF16 = jnp.bfloat16
F32 = jnp.float32


def bits_of(count):
    found = []
    bit = 1
    while bit < count:
        found.append(bit)
        bit *= 2
    return found


def relative_of(position, bits):
    total = 0
    for place, bit in enumerate(reversed(bits)):
        if position >> place & 1:
            total |= bit
    return total


def shift_pairs(n_groups, n_tok, step):
    return [
        (g * n_tok + t, (g + step) % n_groups * n_tok + t)
        for g in range(n_groups)
        for t in range(n_tok)
    ]


def xor_pairs(count, bit):
    return [(i, i ^ bit) for i in range(count)]


def gather_blocks(block, axis, count, bits):
    blocks = [block]
    for bit in reversed(bits):
        blocks = blocks + [lax.ppermute(b, axis, xor_pairs(count, bit)) for b in blocks]
    return blocks


def params():
    return pltpu.CompilerParams(vmem_limit_bytes=VMEM_BYTES)


def smem():
    return pl.BlockSpec(memory_space=pltpu.SMEM)


def vmem():
    return pl.BlockSpec(memory_space=pltpu.VMEM)


def aligned(value, unit):
    return pl.multiple_of(value, unit)


def dot(a, b, dims):
    return lax.dot_general(a, b, (dims, ((), ())), preferred_element_type=F32)


def whole_call(body, out_shape, args, name, scratch=(), cost=None):
    single = not isinstance(out_shape, list)
    return pl.pallas_call(
        body,
        out_shape=out_shape,
        in_specs=[smem()] + [vmem()] * (len(args) - 1),
        out_specs=vmem() if single else [vmem()] * len(out_shape),
        scratch_shapes=list(scratch),
        compiler_params=params(),
        cost_estimate=cost,
        name=name,
    )(*args)


def pack_kernel(n_groups, ids, q, k, v, w, *refs):
    outs, sems = refs[:-1], refs[-1]
    rows, depth = q.shape[0], w.shape[0]
    gw = q.shape[1] // n_groups
    copies = []
    for s in range(n_groups):
        cols = pl.ds(aligned(lax.rem(ids[0] + s, n_groups) * gw, HD), gw)
        own = outs[n_groups] if s == 0 else outs[s].at[pl.ds(2 * rows + depth, rows), :]
        for source, target in (
            (k, outs[s].at[pl.ds(0, rows), :]),
            (v, outs[s].at[pl.ds(rows, rows), :]),
            (w, outs[s].at[pl.ds(2 * rows, depth), :]),
            (q, own),
        ):
            copies.append(
                pltpu.make_async_copy(source.at[:, cols], target, sems.at[len(copies)])
            )
    for copy in copies:
        copy.start()
    for copy in copies:
        copy.wait()


def pack(ids, q, k, v, w, n_groups):
    rows, width = q.shape
    gw = width // n_groups
    shared = 2 * rows + w.shape[0]
    shapes = (
        [jax.ShapeDtypeStruct((shared, gw), BF16)]
        + [jax.ShapeDtypeStruct((shared + rows, gw), BF16)] * (n_groups - 1)
        + [jax.ShapeDtypeStruct((rows, gw), BF16)]
    )
    return pl.pallas_call(
        functools.partial(pack_kernel, n_groups),
        out_shape=shapes,
        in_specs=[smem()] + [pl.BlockSpec(memory_space=pltpu.HBM)] * 4,
        out_specs=[vmem()] * len(shapes),
        scratch_shapes=[pltpu.SemaphoreType.DMA((4 * n_groups,))],
        compiler_params=pltpu.CompilerParams(vmem_limit_bytes=60 * 1024 * 1024),
        name="pack",
    )(ids, q, k, v, w)


def stack_kernel(n_groups, rows, ids, *refs):
    pieces, out = refs[:n_groups], refs[n_groups]
    shared = out.shape[0] // n_groups
    depth = shared - 2 * rows
    for s, piece in enumerate(pieces):
        for i in range(2):
            at = (i * n_groups + s) * rows
            out[at : at + rows, :] = piece[i * rows : (i + 1) * rows, :]
        at = 2 * n_groups * rows + s * depth
        out[at : at + depth, :] = piece[2 * rows : shared, :]


def stack(ids, pieces, rows):
    shared, gw = pieces[0].shape
    return whole_call(
        functools.partial(stack_kernel, len(pieces), rows),
        jax.ShapeDtypeStruct((shared * len(pieces), gw), BF16),
        (ids, *pieces),
        "stack",
    )


def stack_queries_kernel(ids, own, *refs):
    pieces, out = refs[:-1], refs[-1]
    rows = own.shape[0]
    out[:rows, :] = own[...]
    for s, piece in enumerate(pieces):
        out[(s + 1) * rows : (s + 2) * rows, :] = piece[piece.shape[0] - rows :, :]


def stack_queries(ids, own, pieces):
    rows, gw = own.shape
    shape = jax.ShapeDtypeStruct((rows * (len(pieces) + 1), gw), BF16)
    return whole_call(stack_queries_kernel, shape, (ids, own, *pieces), "stack_queries")


def forward_kernel(chunk, scale, q_in, *refs):
    blocks, (p_out, o_out, il_out, logits) = refs[:-4], refs[-4:]
    part = blocks[0].shape[0] // 2
    q = q_in[...]
    top = None
    for j, kv in enumerate(blocks):
        for c in range(0, part, chunk):
            at = j * part + c
            block = dot(kv[c : c + chunk, :], q, ((1,), (1,)))
            logits[at : at + chunk, :] = block
            here = jnp.max(block, axis=0, keepdims=True)
            top = here if top is None else jnp.maximum(top, here)
    top = top * scale
    total = jnp.zeros_like(top)
    out = jnp.zeros((HD, q.shape[0]), F32)
    for j, kv in enumerate(blocks):
        for c in range(0, part, chunk):
            at = j * part + c
            prob = jnp.exp2(logits[at : at + chunk, :] * scale - top)
            total = total + jnp.sum(prob, axis=0, keepdims=True)
            low = prob.astype(BF16)
            p_out[0, at : at + chunk, :] = low
            out = out + dot(kv[part + c : part + c + chunk, :], low, ((0,), (0,)))
    inverse = 1.0 / total
    il_out[0] = inverse
    o_out[...] = (out * inverse).T.astype(BF16)


def forward(q, blocks, part):
    n_q, gw = q.shape
    heads = gw // HD
    seq_len = part * len(blocks)
    chunk = part if part <= 640 else math.gcd(part, 512)
    scale = math.log2(math.e) / math.sqrt(HD)
    return pl.pallas_call(
        functools.partial(forward_kernel, chunk, scale),
        grid=(heads,),
        out_shape=[
            jax.ShapeDtypeStruct((heads, seq_len, n_q), BF16),
            jax.ShapeDtypeStruct((n_q, gw), BF16),
            jax.ShapeDtypeStruct((heads, 1, n_q), F32),
        ],
        in_specs=[pl.BlockSpec((n_q, HD), lambda h: (0, h))]
        + [pl.BlockSpec((2 * part, HD), lambda h: (0, h))] * len(blocks),
        out_specs=[
            pl.BlockSpec((1, seq_len, n_q), lambda h: (h, 0, 0)),
            pl.BlockSpec((n_q, HD), lambda h: (0, h)),
            pl.BlockSpec((1, 1, n_q), lambda h: (h, 0, 0)),
        ],
        scratch_shapes=[pltpu.VMEM((seq_len, n_q), F32)],
        compiler_params=params(),
        cost_estimate=pl.CostEstimate(
            flops=4 * heads * seq_len * n_q * HD,
            bytes_accessed=2 * heads * seq_len * n_q,
            transcendentals=heads * seq_len * n_q,
        ),
        name="forward",
    )(q, *blocks)


def backward_kernel(n_groups, chunk, factor, *refs):
    q_in, p_in, o_in, il_in, da_in = refs[:5]
    dq_outs, halves, dq_all = refs[-n_groups - 3 : -3], refs[-3:-1], refs[-1]
    blocks = refs[5 : -n_groups - 3]
    part = blocks[0].shape[0] // 2
    rows = dq_outs[0].shape[0]
    q = q_in[...]
    n_q = q.shape[0]
    inverse = jnp.broadcast_to(il_in[0], (HD, n_q)).T
    da = (da_in[...].astype(F32) * inverse).astype(BF16)
    delta = jnp.sum((da.astype(F32) * o_in[...].astype(F32)).T, axis=0, keepdims=True)
    dq = jnp.zeros((HD, n_q), F32)
    per_half = max(1, len(blocks) // 2)
    for j, kv in enumerate(blocks):
        out = halves[j // per_half]
        base = j % per_half * 2 * part
        for c in range(0, part, chunk):
            at = j * part + c
            low = p_in[0, at : at + chunk, :]
            dp = dot(kv[part + c : part + c + chunk, :], da, ((1,), (1,)))
            ds = (low.astype(F32) * (dp - delta)).astype(BF16)
            dk = (factor * dot(ds, q, ((1,), (0,)))).astype(BF16)
            out[base + c : base + c + chunk, :] = dk
            dv = dot(low, da, ((1,), (0,))).astype(BF16)
            out[base + part + c : base + part + c + chunk, :] = dv
            dq = dq + dot(kv[c : c + chunk, :], ds, ((0,), (0,)))
    dq_all[...] = (factor * dq).T.astype(BF16)
    for s in range(n_groups):
        dq_outs[s][...] = dq_all[s * rows : (s + 1) * rows, :]


def backward(head, count, q, blocks, part, probs, out, inverse, grad_attn, n_groups):
    n_q = q.shape[0]
    rows = n_q // n_groups
    seq_len = part * len(blocks)
    chunk = part if part <= 640 else math.gcd(part, 512)
    per_half = max(1, len(blocks) // 2)
    column = pl.BlockSpec((n_q, HD), lambda i: (0, head + i))
    results = pl.pallas_call(
        functools.partial(backward_kernel, n_groups, chunk, 1.0 / math.sqrt(HD)),
        grid=(count,),
        out_shape=[jax.ShapeDtypeStruct((rows, count * HD), BF16)] * n_groups
        + [jax.ShapeDtypeStruct((per_half * 2 * part, count * HD), BF16)] * 2,
        in_specs=[
            column,
            pl.BlockSpec((1, seq_len, n_q), lambda i: (head + i, 0, 0)),
            column,
            pl.BlockSpec((1, 1, n_q), lambda i: (head + i, 0, 0)),
            column,
        ]
        + [pl.BlockSpec((2 * part, HD), lambda i: (0, head + i))] * len(blocks),
        out_specs=[pl.BlockSpec((rows, HD), lambda i: (0, i))] * n_groups
        + [pl.BlockSpec((per_half * 2 * part, HD), lambda i: (0, i))] * 2,
        scratch_shapes=[pltpu.VMEM((n_q, HD), BF16)],
        compiler_params=params(),
        cost_estimate=pl.CostEstimate(
            flops=n_q * HD,
            bytes_accessed=2 * n_q * HD,
            transcendentals=0,
        ),
        name="backward",
    )(q, probs, out, inverse, grad_attn, *blocks)
    return results[:n_groups], results[n_groups:]


def frame_block(ids, sign, s, position, n_groups, n_tok):
    group = lax.rem(ids[0] + sign * s + n_groups, n_groups)
    return group * n_tok + jnp.bitwise_xor(ids[1], relative_of(position, bits_of(n_tok)))


def tokens_of(ids, tokens, grads, n_groups, n_space):
    rows, part = grads[0].shape
    for r in range(n_space):
        for s in range(n_groups):
            tokens[s * rows : (s + 1) * rows, :] = grads[r * n_groups + s][...]
        start = jnp.bitwise_xor(ids[2], relative_of(r, bits_of(n_space))) * part
        yield tokens[...], pl.ds(aligned(start, 16), part)


def attn_kernel(n_groups, n_tok, n_space, ids, *refs):
    blocks, grads = refs[:n_tok], refs[n_tok : n_tok + n_groups * n_space]
    grad_attn, weight, tokens = refs[n_tok + n_groups * n_space :]
    depth = weight.shape[0] // (n_groups * n_tok)
    first = blocks[0].shape[0] - n_groups * depth
    for j in range(n_tok):
        for s in range(n_groups):
            place = frame_block(ids, -1, s, j, n_groups, n_tok) * depth
            at = first + s * depth
            weight[pl.ds(aligned(place, 16), depth), :] = blocks[j][at : at + depth, :]
    total = None
    for block, here in tokens_of(ids, tokens, grads, n_groups, n_space):
        term = dot(block, weight[here, :], ((1,), (0,)))
        total = term if total is None else total + term
    grad_attn[...] = total.astype(BF16)


def projection_cost(n_q, gw):
    return pl.CostEstimate(
        flops=n_q * gw,
        bytes_accessed=2 * n_q * gw,
        transcendentals=0,
    )


def attn_gradient(ids, blocks, grads, depth, n_groups, n_tok, n_space):
    rows, part = grads[0].shape
    n_q, gw = rows * n_groups, blocks[0].shape[1]
    total = n_groups * n_tok * depth
    return whole_call(
        functools.partial(attn_kernel, n_groups, n_tok, n_space),
        jax.ShapeDtypeStruct((n_q, gw), BF16),
        (ids, *blocks, *grads),
        "attn_gradient",
        [pltpu.VMEM((total, gw), BF16), pltpu.VMEM((n_q, part), BF16)],
        projection_cost(n_q, gw),
    )


def proj_kernel(n_groups, n_tok, n_space, ids, attn, *refs):
    grads, (kept, sent, whole, tokens) = refs[: n_groups * n_space], refs[n_groups * n_space :]
    depth = whole.shape[0] // (n_groups * n_tok)
    for block, here in tokens_of(ids, tokens, grads, n_groups, n_space):
        whole[here, :] = dot(block, attn[...], ((0,), (0,))).astype(BF16)
    per_half = max(1, n_tok // 2)
    for j in range(n_tok):
        half = sent if j >= per_half else kept
        for s in range(n_groups):
            place = frame_block(ids, 1, s, j, n_groups, n_tok) * depth
            at = (j % per_half * n_groups + s) * depth
            half[at : at + depth, :] = whole[pl.ds(aligned(place, 16), depth), :]


def proj_gradient(ids, attn, grads, depth, n_groups, n_tok, n_space):
    n_q, gw = attn.shape
    part = grads[0].shape[1]
    half = n_groups * depth * max(1, n_tok // 2)
    total = n_groups * n_tok * depth
    return whole_call(
        functools.partial(proj_kernel, n_groups, n_tok, n_space),
        [jax.ShapeDtypeStruct((half, gw), BF16)] * 2,
        (ids, attn, *grads),
        "proj_gradient",
        [pltpu.VMEM((total, gw), BF16), pltpu.VMEM((n_q, part), BF16)],
        projection_cost(n_q, gw),
    )


def add_kernel(ids, kept, other, *outs):
    rows = outs[0].shape[0]
    for i, out in enumerate(outs):
        total = kept[i * rows : (i + 1) * rows, :].astype(F32)
        total = total + other[i * rows : (i + 1) * rows, :].astype(F32)
        out[...] = total.astype(BF16)


def add_parts(ids, kept, other, count):
    rows, gw = kept.shape
    shape = jax.ShapeDtypeStruct((rows // count, gw), BF16)
    return whole_call(add_kernel, [shape] * count, (ids, kept, other), "add_parts")


def halve(ids, kept, sent, n_frame, bits):
    for bit in bits[:-1]:
        other = lax.ppermute(sent, "frame", xor_pairs(n_frame, bit))
        kept, sent = add_parts(ids, kept, other, 2)
    return kept, sent


def finish_kernel(n_groups, ids, kept, other, *refs):
    dq, outs = refs[:n_groups], refs[n_groups:]
    rows = dq[0].shape[0]
    for s in range(n_groups):
        outs[s][:rows, :] = dq[s][...]
        for i in range(2):
            at = (i * n_groups + s) * rows
            total = kept[at : at + rows, :].astype(F32) + other[at : at + rows, :].astype(F32)
            outs[s][(i + 1) * rows : (i + 2) * rows, :] = total.astype(BF16)


def finish(ids, kept, other, dq, n_groups):
    rows, cols = dq[0].shape
    return whole_call(
        functools.partial(finish_kernel, n_groups),
        [jax.ShapeDtypeStruct((3 * rows, cols), BF16)] * n_groups,
        (ids, kept, other, *dq),
        "finish",
    )


def unpack_kernel(n_groups, widths, ids, *refs):
    pieces, outs = refs[:-3], refs[-3:]
    rows, gw = outs[0].shape[0], outs[0].shape[1] // n_groups
    before = 0
    for c, cols in enumerate(widths):
        for s in range(n_groups):
            start = lax.rem(ids[0] + s, n_groups) * gw + before
            for i, out in enumerate(outs):
                piece = pieces[c * n_groups + s][i * rows : (i + 1) * rows, :]
                out[:, pl.ds(aligned(start, HD), cols)] = piece
        before += cols


def unpack(ids, chunks, rows, gw, n_groups):
    widths = [HD, gw - HD][: len(chunks)]
    return whole_call(
        functools.partial(unpack_kernel, n_groups, widths),
        [jax.ShapeDtypeStruct((rows, gw * n_groups), BF16)] * 3,
        (ids, *[piece for pieces in chunks for piece in pieces]),
        "unpack",
    )


def join_kernel(n_groups, ids, *refs):
    pieces, out = refs[:n_groups], refs[n_groups]
    gw = pieces[0].shape[1]
    for s in range(n_groups):
        start = lax.rem(ids[0] - s + n_groups, n_groups) * gw
        out[:, pl.ds(aligned(start, HD), gw)] = pieces[s][...].astype(F32)


def join(ids, pieces, n_groups):
    rows, gw = pieces[0].shape
    return whole_call(
        functools.partial(join_kernel, n_groups),
        jax.ShapeDtypeStruct((rows, gw * n_groups), F32),
        (ids, *pieces),
        "join",
    )


def exchange(pieces, n_groups, n_tok, sign):
    return [pieces[0]] + [
        lax.ppermute(pieces[s], "frame", shift_pairs(n_groups, n_tok, sign * s))
        for s in range(1, n_groups)
    ]


def local(queries, keys, values, grad_out, proj_weight):
    n_frame = lax.axis_size("frame")
    n_space = lax.axis_size("space")
    rows, width = queries.shape
    gw = width // math.gcd(width // HD, n_frame)
    depth = proj_weight.shape[1]
    n_groups = math.gcd(width // HD, n_frame)
    n_tok = n_frame // n_groups
    tok_bits = bits_of(n_tok)
    space_bits = bits_of(n_space)
    heads = width // n_groups // HD
    shared = 2 * rows + depth
    frame = lax.axis_index("frame")
    ids = jnp.stack([frame // n_tok, frame % n_tok, lax.axis_index("space")]).astype(jnp.int32)

    tie = lax.optimization_barrier
    last = xor_pairs(n_frame, tok_bits[-1])

    *pieces, own_q = pack(ids, queries, keys, values, proj_weight.T, n_groups)
    pieces = exchange(pieces, n_groups, n_tok, 1)
    q_pieces = pieces[1:]
    own, others, ring, across = [pieces[0]], [], grad_out, []
    for s in range(n_groups):
        others.append(lax.ppermute(own[s], "frame", last))
        across.append(gather_blocks(ring, "space", n_space, space_bits))
        if s + 1 < n_groups:
            ring = lax.ppermute(ring, "frame", shift_pairs(n_groups, n_tok, 1))
            step = (ring, pieces[s + 1][:shared], others[s], *across[s])
            ring, piece, others[s], *across[s] = tie(step)
            own.append(piece)

    q = stack_queries(ids, own_q, q_pieces)
    blocks = [stack(ids, own, rows), stack(ids, others, rows)]
    for bit in reversed(tok_bits[:-1]):
        blocks = blocks + [lax.ppermute(b, "frame", xor_pairs(n_frame, bit)) for b in blocks]
    part = n_groups * rows
    probs, out, inverse = forward(q, blocks, part)
    grads = [across[s][r] for r in range(n_space) for s in range(n_groups)]
    grad_attn = attn_gradient(ids, blocks, grads, depth, n_groups, n_tok, n_space)

    def attention_halves(head, count, q):
        return backward(head, count, q, blocks, part, probs, out, inverse, grad_attn, n_groups)

    def across_x(piece):
        return lax.ppermute(piece, "frame", last)

    dq, halves = attention_halves(0, 1, q)
    kept, sent = halve(ids, *halves, n_frame, tok_bits)
    other = across_x(sent)
    out_after, kept = tie((out, kept))
    proj = proj_gradient(ids, out_after, grads, depth, n_groups, n_tok, n_space)
    other, *proj = tie((other, *proj))
    proj_kept, proj_sent = halve(ids, *proj, n_frame, tok_bits)
    sums = finish(ids, kept, other, dq, n_groups)
    proj_sent, q, *sums = tie((proj_sent, q, *sums))
    returned = [exchange(sums, n_groups, n_tok, -1)]
    proj_other = across_x(proj_sent)
    if heads > 1:
        dq_rest, halves = attention_halves(1, heads - 1, q)
        step = (proj_other, *halves, *returned[0][1:])
        proj_other, kept, sent, *returned[0][1:] = tie(step)
        kept, sent = halve(ids, kept, sent, n_frame, tok_bits)
    proj_pieces = exchange(add_parts(ids, proj_kept, proj_other, n_groups), n_groups, n_tok, 1)
    if heads > 1:
        other, *proj_pieces[1:] = tie((across_x(sent), *proj_pieces[1:]))
        sums = finish(ids, kept, other, dq_rest, n_groups)
        returned.append(exchange(sums, n_groups, n_tok, -1))
    grad_proj = join(ids, proj_pieces, n_groups).T
    grad_queries, grad_keys, grad_values = unpack(ids, returned, rows, gw, n_groups)
    return (grad_queries, grad_keys, grad_values, grad_proj)


def solution(mesh):
    in_specs = (
        P("frame", "space"),
        P("frame", "space"),
        P("frame", "space"),
        P("frame", "space"),
        P("space", "frame"),
    )
    out_specs = (P("frame", "space"), P("frame", "space"), P("frame", "space"), P("space", "frame"))
    return jax.shard_map(local, mesh=mesh, in_specs=in_specs, out_specs=out_specs, check_vma=False)
```

```python
import functools
import math

import jax
import jax.numpy as jnp
from jax import lax
from jax.experimental import pallas as pl
from jax.experimental.pallas import tpu as pltpu
from jax.sharding import PartitionSpec as P

HD = 128
VMEM_BYTES = 24 * 1024 * 1024
BF16 = jnp.bfloat16
F32 = jnp.float32


def bits_of(count):
    found = []
    bit = 1
    while bit < count:
        found.append(bit)
        bit *= 2
    return found


def relative_of(position, bits):
    total = 0
    for place, bit in enumerate(reversed(bits)):
        if position >> place & 1:
            total |= bit
    return total


def shift_pairs(n_groups, n_tok, step):
    return [
        (g * n_tok + t, (g + step) % n_groups * n_tok + t)
        for g in range(n_groups)
        for t in range(n_tok)
    ]


def xor_pairs(count, bit):
    return [(i, i ^ bit) for i in range(count)]


def gather_blocks(block, axis, count, bits):
    blocks = [block]
    for bit in reversed(bits):
        blocks = blocks + [lax.ppermute(b, axis, xor_pairs(count, bit)) for b in blocks]
    return blocks


def params():
    return pltpu.CompilerParams(vmem_limit_bytes=VMEM_BYTES)


def smem():
    return pl.BlockSpec(memory_space=pltpu.SMEM)


def vmem():
    return pl.BlockSpec(memory_space=pltpu.VMEM)


def aligned(value, unit):
    return pl.multiple_of(value, unit)


def dot(a, b, dims):
    return lax.dot_general(a, b, (dims, ((), ())), preferred_element_type=F32)


def whole_call(body, out_shape, args, name, scratch=(), cost=None):
    single = not isinstance(out_shape, list)
    return pl.pallas_call(
        body,
        out_shape=out_shape,
        in_specs=[smem()] + [vmem()] * (len(args) - 1),
        out_specs=vmem() if single else [vmem()] * len(out_shape),
        scratch_shapes=list(scratch),
        compiler_params=params(),
        cost_estimate=cost,
        name=name,
    )(*args)


def pack_kernel(n_groups, ids, q, k, v, w, *refs):
    outs, sems = refs[:-1], refs[-1]
    rows, depth = q.shape[0], w.shape[0]
    gw = q.shape[1] // n_groups
    copies = []
    for s in range(n_groups):
        cols = pl.ds(aligned(lax.rem(ids[0] + s, n_groups) * gw, HD), gw)
        own = outs[n_groups] if s == 0 else outs[s].at[pl.ds(2 * rows + depth, rows), :]
        for source, target in (
            (k, outs[s].at[pl.ds(0, rows), :]),
            (v, outs[s].at[pl.ds(rows, rows), :]),
            (w, outs[s].at[pl.ds(2 * rows, depth), :]),
            (q, own),
        ):
            copies.append(
                pltpu.make_async_copy(source.at[:, cols], target, sems.at[len(copies)])
            )
    for copy in copies:
        copy.start()
    for copy in copies:
        copy.wait()


def pack(ids, q, k, v, w, n_groups):
    rows, width = q.shape
    gw = width // n_groups
    shared = 2 * rows + w.shape[0]
    shapes = (
        [jax.ShapeDtypeStruct((shared, gw), BF16)]
        + [jax.ShapeDtypeStruct((shared + rows, gw), BF16)] * (n_groups - 1)
        + [jax.ShapeDtypeStruct((rows, gw), BF16)]
    )
    return pl.pallas_call(
        functools.partial(pack_kernel, n_groups),
        out_shape=shapes,
        in_specs=[smem()] + [pl.BlockSpec(memory_space=pltpu.HBM)] * 4,
        out_specs=[pl.BlockSpec(memory_space=pltpu.HBM)] * len(shapes),
        scratch_shapes=[pltpu.SemaphoreType.DMA((4 * n_groups,))],
        compiler_params=pltpu.CompilerParams(vmem_limit_bytes=60 * 1024 * 1024),
        name="pack",
    )(ids, q, k, v, w)


def stack_kernel(n_groups, rows, ids, *refs):
    pieces, out = refs[:n_groups], refs[n_groups]
    shared = out.shape[0] // n_groups
    depth = shared - 2 * rows
    for s, piece in enumerate(pieces):
        for i in range(2):
            at = (i * n_groups + s) * rows
            out[at : at + rows, :] = piece[i * rows : (i + 1) * rows, :]
        at = 2 * n_groups * rows + s * depth
        out[at : at + depth, :] = piece[2 * rows : shared, :]


def stack(ids, pieces, rows):
    shared, gw = pieces[0].shape
    return whole_call(
        functools.partial(stack_kernel, len(pieces), rows),
        jax.ShapeDtypeStruct((shared * len(pieces), gw), BF16),
        (ids, *pieces),
        "stack",
    )


def stack_queries_kernel(ids, own, *refs):
    pieces, out = refs[:-1], refs[-1]
    rows = own.shape[0]
    out[:rows, :] = own[...]
    for s, piece in enumerate(pieces):
        out[(s + 1) * rows : (s + 2) * rows, :] = piece[piece.shape[0] - rows :, :]


def stack_queries(ids, own, pieces):
    rows, gw = own.shape
    shape = jax.ShapeDtypeStruct((rows * (len(pieces) + 1), gw), BF16)
    return whole_call(stack_queries_kernel, shape, (ids, own, *pieces), "stack_queries")


def forward_kernel(chunk, scale, q_in, *refs):
    blocks, (p_out, o_out, il_out, logits) = refs[:-4], refs[-4:]
    part = blocks[0].shape[0] // 2
    q = q_in[...]
    top = None
    for j, kv in enumerate(blocks):
        for c in range(0, part, chunk):
            at = j * part + c
            block = dot(kv[c : c + chunk, :], q, ((1,), (1,)))
            logits[at : at + chunk, :] = block
            here = jnp.max(block, axis=0, keepdims=True)
            top = here if top is None else jnp.maximum(top, here)
    top = top * scale
    total = jnp.zeros_like(top)
    out = jnp.zeros((HD, q.shape[0]), F32)
    for j, kv in enumerate(blocks):
        for c in range(0, part, chunk):
            at = j * part + c
            prob = jnp.exp2(logits[at : at + chunk, :] * scale - top)
            total = total + jnp.sum(prob, axis=0, keepdims=True)
            low = prob.astype(BF16)
            p_out[0, at : at + chunk, :] = low
            out = out + dot(kv[part + c : part + c + chunk, :], low, ((0,), (0,)))
    inverse = 1.0 / total
    il_out[0] = inverse
    o_out[...] = (out * inverse).T.astype(BF16)


def forward(q, blocks, part):
    n_q, gw = q.shape
    heads = gw // HD
    seq_len = part * len(blocks)
    chunk = part if part <= 640 else math.gcd(part, 512)
    scale = math.log2(math.e) / math.sqrt(HD)
    return pl.pallas_call(
        functools.partial(forward_kernel, chunk, scale),
        grid=(heads,),
        out_shape=[
            jax.ShapeDtypeStruct((heads, seq_len, n_q), BF16),
            jax.ShapeDtypeStruct((n_q, gw), BF16),
            jax.ShapeDtypeStruct((heads, 1, n_q), F32),
        ],
        in_specs=[pl.BlockSpec((n_q, HD), lambda h: (0, h))]
        + [pl.BlockSpec((2 * part, HD), lambda h: (0, h))] * len(blocks),
        out_specs=[
            pl.BlockSpec((1, seq_len, n_q), lambda h: (h, 0, 0)),
            pl.BlockSpec((n_q, HD), lambda h: (0, h)),
            pl.BlockSpec((1, 1, n_q), lambda h: (h, 0, 0)),
        ],
        scratch_shapes=[pltpu.VMEM((seq_len, n_q), F32)],
        compiler_params=params(),
        cost_estimate=pl.CostEstimate(
            flops=4 * heads * seq_len * n_q * HD,
            bytes_accessed=2 * heads * seq_len * n_q,
            transcendentals=heads * seq_len * n_q,
        ),
        name="forward",
    )(q, *blocks)


def backward_kernel(n_groups, chunk, factor, *refs):
    q_in, p_in, o_in, il_in, da_in = refs[:5]
    dq_outs, halves, dq_all = refs[-n_groups - 3 : -3], refs[-3:-1], refs[-1]
    blocks = refs[5 : -n_groups - 3]
    part = blocks[0].shape[0] // 2
    rows = dq_outs[0].shape[0]
    q = q_in[...]
    n_q = q.shape[0]
    inverse = jnp.broadcast_to(il_in[0], (HD, n_q)).T
    da = (da_in[...].astype(F32) * inverse).astype(BF16)
    delta = jnp.sum((da.astype(F32) * o_in[...].astype(F32)).T, axis=0, keepdims=True)
    dq = jnp.zeros((HD, n_q), F32)
    per_half = max(1, len(blocks) // 2)
    for j, kv in enumerate(blocks):
        out = halves[j // per_half]
        base = j % per_half * 2 * part
        for c in range(0, part, chunk):
            at = j * part + c
            low = p_in[0, at : at + chunk, :]
            dp = dot(kv[part + c : part + c + chunk, :], da, ((1,), (1,)))
            ds = (low.astype(F32) * (dp - delta)).astype(BF16)
            dk = (factor * dot(ds, q, ((1,), (0,)))).astype(BF16)
            out[base + c : base + c + chunk, :] = dk
            dv = dot(low, da, ((1,), (0,))).astype(BF16)
            out[base + part + c : base + part + c + chunk, :] = dv
            dq = dq + dot(kv[c : c + chunk, :], ds, ((0,), (0,)))
    dq_all[...] = (factor * dq).T.astype(BF16)
    for s in range(n_groups):
        dq_outs[s][...] = dq_all[s * rows : (s + 1) * rows, :]


def backward(head, count, q, blocks, part, probs, out, inverse, grad_attn, n_groups):
    n_q = q.shape[0]
    rows = n_q // n_groups
    seq_len = part * len(blocks)
    chunk = part if part <= 640 else math.gcd(part, 512)
    per_half = max(1, len(blocks) // 2)
    column = pl.BlockSpec((n_q, HD), lambda i: (0, head + i))
    results = pl.pallas_call(
        functools.partial(backward_kernel, n_groups, chunk, 1.0 / math.sqrt(HD)),
        grid=(count,),
        out_shape=[jax.ShapeDtypeStruct((rows, count * HD), BF16)] * n_groups
        + [jax.ShapeDtypeStruct((per_half * 2 * part, count * HD), BF16)] * 2,
        in_specs=[
            column,
            pl.BlockSpec((1, seq_len, n_q), lambda i: (head + i, 0, 0)),
            column,
            pl.BlockSpec((1, 1, n_q), lambda i: (head + i, 0, 0)),
            column,
        ]
        + [pl.BlockSpec((2 * part, HD), lambda i: (0, head + i))] * len(blocks),
        out_specs=[pl.BlockSpec((rows, HD), lambda i: (0, i))] * n_groups
        + [pl.BlockSpec((per_half * 2 * part, HD), lambda i: (0, i))] * 2,
        scratch_shapes=[pltpu.VMEM((n_q, HD), BF16)],
        compiler_params=params(),
        cost_estimate=pl.CostEstimate(
            flops=n_q * HD,
            bytes_accessed=2 * n_q * HD,
            transcendentals=0,
        ),
        name="backward",
    )(q, probs, out, inverse, grad_attn, *blocks)
    return results[:n_groups], results[n_groups:]


def frame_block(ids, sign, s, position, n_groups, n_tok):
    group = lax.rem(ids[0] + sign * s + n_groups, n_groups)
    return group * n_tok + jnp.bitwise_xor(ids[1], relative_of(position, bits_of(n_tok)))


def tokens_of(ids, tokens, grads, n_groups, n_space):
    rows, part = grads[0].shape
    for r in range(n_space):
        for s in range(n_groups):
            tokens[s * rows : (s + 1) * rows, :] = grads[r * n_groups + s][...]
        start = jnp.bitwise_xor(ids[2], relative_of(r, bits_of(n_space))) * part
        yield tokens[...], pl.ds(aligned(start, 16), part)


def attn_kernel(n_groups, n_tok, n_space, ids, *refs):
    blocks, grads = refs[:n_tok], refs[n_tok : n_tok + n_groups * n_space]
    grad_attn, weight, tokens = refs[n_tok + n_groups * n_space :]
    depth = weight.shape[0] // (n_groups * n_tok)
    first = blocks[0].shape[0] - n_groups * depth
    for j in range(n_tok):
        for s in range(n_groups):
            place = frame_block(ids, -1, s, j, n_groups, n_tok) * depth
            at = first + s * depth
            weight[pl.ds(aligned(place, 16), depth), :] = blocks[j][at : at + depth, :]
    total = None
    for block, here in tokens_of(ids, tokens, grads, n_groups, n_space):
        term = dot(block, weight[here, :], ((1,), (0,)))
        total = term if total is None else total + term
    grad_attn[...] = total.astype(BF16)


def projection_cost(n_q, gw):
    return pl.CostEstimate(
        flops=n_q * gw,
        bytes_accessed=2 * n_q * gw,
        transcendentals=0,
    )


def attn_gradient(ids, blocks, grads, depth, n_groups, n_tok, n_space):
    rows, part = grads[0].shape
    n_q, gw = rows * n_groups, blocks[0].shape[1]
    total = n_groups * n_tok * depth
    return whole_call(
        functools.partial(attn_kernel, n_groups, n_tok, n_space),
        jax.ShapeDtypeStruct((n_q, gw), BF16),
        (ids, *blocks, *grads),
        "attn_gradient",
        [pltpu.VMEM((total, gw), BF16), pltpu.VMEM((n_q, part), BF16)],
        projection_cost(n_q, gw),
    )


def proj_kernel(n_groups, n_tok, n_space, ids, attn, *refs):
    grads, (kept, sent, whole, tokens) = refs[: n_groups * n_space], refs[n_groups * n_space :]
    depth = whole.shape[0] // (n_groups * n_tok)
    for block, here in tokens_of(ids, tokens, grads, n_groups, n_space):
        whole[here, :] = dot(block, attn[...], ((0,), (0,))).astype(BF16)
    per_half = max(1, n_tok // 2)
    for j in range(n_tok):
        half = sent if j >= per_half else kept
        for s in range(n_groups):
            place = frame_block(ids, 1, s, j, n_groups, n_tok) * depth
            at = (j % per_half * n_groups + s) * depth
            half[at : at + depth, :] = whole[pl.ds(aligned(place, 16), depth), :]


def proj_gradient(ids, attn, grads, depth, n_groups, n_tok, n_space):
    n_q, gw = attn.shape
    part = grads[0].shape[1]
    half = n_groups * depth * max(1, n_tok // 2)
    total = n_groups * n_tok * depth
    return whole_call(
        functools.partial(proj_kernel, n_groups, n_tok, n_space),
        [jax.ShapeDtypeStruct((half, gw), BF16)] * 2,
        (ids, attn, *grads),
        "proj_gradient",
        [pltpu.VMEM((total, gw), BF16), pltpu.VMEM((n_q, part), BF16)],
        projection_cost(n_q, gw),
    )


def add_kernel(ids, kept, other, *outs):
    rows = outs[0].shape[0]
    for i, out in enumerate(outs):
        total = kept[i * rows : (i + 1) * rows, :].astype(F32)
        total = total + other[i * rows : (i + 1) * rows, :].astype(F32)
        out[...] = total.astype(BF16)


def add_parts(ids, kept, other, count):
    rows, gw = kept.shape
    shape = jax.ShapeDtypeStruct((rows // count, gw), BF16)
    return whole_call(add_kernel, [shape] * count, (ids, kept, other), "add_parts")


def halve(ids, kept, sent, n_frame, bits):
    for bit in bits[:-1]:
        other = lax.ppermute(sent, "frame", xor_pairs(n_frame, bit))
        kept, sent = add_parts(ids, kept, other, 2)
    return kept, sent


def finish_kernel(n_groups, ids, kept, other, *refs):
    dq, outs = refs[:n_groups], refs[n_groups:]
    rows = dq[0].shape[0]
    for s in range(n_groups):
        outs[s][:rows, :] = dq[s][...]
        for i in range(2):
            at = (i * n_groups + s) * rows
            total = kept[at : at + rows, :].astype(F32) + other[at : at + rows, :].astype(F32)
            outs[s][(i + 1) * rows : (i + 2) * rows, :] = total.astype(BF16)


def finish(ids, kept, other, dq, n_groups):
    rows, cols = dq[0].shape
    return whole_call(
        functools.partial(finish_kernel, n_groups),
        [jax.ShapeDtypeStruct((3 * rows, cols), BF16)] * n_groups,
        (ids, kept, other, *dq),
        "finish",
    )


def unpack_kernel(n_groups, widths, ids, *refs):
    pieces, outs = refs[:-3], refs[-3:]
    rows, gw = outs[0].shape[0], outs[0].shape[1] // n_groups
    before = 0
    for c, cols in enumerate(widths):
        for s in range(n_groups):
            start = lax.rem(ids[0] + s, n_groups) * gw + before
            for i, out in enumerate(outs):
                piece = pieces[c * n_groups + s][i * rows : (i + 1) * rows, :]
                out[:, pl.ds(aligned(start, HD), cols)] = piece
        before += cols


def unpack(ids, chunks, rows, gw, n_groups):
    widths = [HD, gw - HD][: len(chunks)]
    return whole_call(
        functools.partial(unpack_kernel, n_groups, widths),
        [jax.ShapeDtypeStruct((rows, gw * n_groups), BF16)] * 3,
        (ids, *[piece for pieces in chunks for piece in pieces]),
        "unpack",
    )


def join_kernel(n_groups, ids, *refs):
    pieces, out = refs[:n_groups], refs[n_groups]
    gw = pieces[0].shape[1]
    for s in range(n_groups):
        start = lax.rem(ids[0] - s + n_groups, n_groups) * gw
        out[:, pl.ds(aligned(start, HD), gw)] = pieces[s][...].astype(F32)


def join(ids, pieces, n_groups):
    rows, gw = pieces[0].shape
    return whole_call(
        functools.partial(join_kernel, n_groups),
        jax.ShapeDtypeStruct((rows, gw * n_groups), F32),
        (ids, *pieces),
        "join",
    )


def exchange(pieces, n_groups, n_tok, sign):
    return [pieces[0]] + [
        lax.ppermute(pieces[s], "frame", shift_pairs(n_groups, n_tok, sign * s))
        for s in range(1, n_groups)
    ]


def local(queries, keys, values, grad_out, proj_weight):
    n_frame = lax.axis_size("frame")
    n_space = lax.axis_size("space")
    rows, width = queries.shape
    gw = width // math.gcd(width // HD, n_frame)
    depth = proj_weight.shape[1]
    n_groups = math.gcd(width // HD, n_frame)
    n_tok = n_frame // n_groups
    tok_bits = bits_of(n_tok)
    space_bits = bits_of(n_space)
    heads = width // n_groups // HD
    shared = 2 * rows + depth
    frame = lax.axis_index("frame")
    ids = jnp.stack([frame // n_tok, frame % n_tok, lax.axis_index("space")]).astype(jnp.int32)

    tie = lax.optimization_barrier
    last = xor_pairs(n_frame, tok_bits[-1])

    *pieces, own_q = pack(ids, queries, keys, values, proj_weight.T, n_groups)
    pieces = exchange(pieces, n_groups, n_tok, 1)
    q_pieces = pieces[1:]
    own, others, ring, across = [pieces[0]], [], grad_out, []
    for s in range(n_groups):
        others.append(lax.ppermute(own[s], "frame", last))
        across.append(gather_blocks(ring, "space", n_space, space_bits))
        if s + 1 < n_groups:
            ring = lax.ppermute(ring, "frame", shift_pairs(n_groups, n_tok, 1))
            step = (ring, pieces[s + 1][:shared], others[s], *across[s])
            ring, piece, others[s], *across[s] = tie(step)
            own.append(piece)

    q = stack_queries(ids, own_q, q_pieces)
    blocks = [stack(ids, own, rows), stack(ids, others, rows)]
    for bit in reversed(tok_bits[:-1]):
        blocks = blocks + [lax.ppermute(b, "frame", xor_pairs(n_frame, bit)) for b in blocks]
    part = n_groups * rows
    probs, out, inverse = forward(q, blocks, part)
    grads = [across[s][r] for r in range(n_space) for s in range(n_groups)]
    grad_attn = attn_gradient(ids, blocks, grads, depth, n_groups, n_tok, n_space)

    def attention_halves(head, count, q):
        return backward(head, count, q, blocks, part, probs, out, inverse, grad_attn, n_groups)

    def across_x(piece):
        return lax.ppermute(piece, "frame", last)

    dq, halves = attention_halves(0, 1, q)
    kept, sent = halve(ids, *halves, n_frame, tok_bits)
    q, kept, sent = tie((q, kept, sent))
    other = across_x(sent)
    if heads > 1:
        dq_rest, halves = attention_halves(1, heads - 1, q)
        other, *halves = tie((other, *halves))
    sums = finish(ids, kept, other, dq, n_groups)
    returned = [exchange(sums, n_groups, n_tok, -1)]
    out_after, *_ = tie((out, *sums))
    proj = proj_gradient(ids, out_after, grads, depth, n_groups, n_tok, n_space)
    if heads > 1:
        kept, sent = halve(ids, *halves, n_frame, tok_bits)
        other = across_x(sent)
        other, proj, *returned[0][1:] = tie((other, tuple(proj), *returned[0][1:]))
        sums = finish(ids, kept, other, dq_rest, n_groups)
        returned.append(exchange(sums, n_groups, n_tok, -1))
    proj_kept, proj_sent = halve(ids, *proj, n_frame, tok_bits)
    if heads > 1:
        proj_sent, *_ = tie((proj_sent, *sums))
    proj = add_parts(ids, proj_kept, across_x(proj_sent), n_groups)
    proj_pieces = exchange(proj, n_groups, n_tok, 1)
    grad_proj = join(ids, proj_pieces, n_groups).T
    grad_queries, grad_keys, grad_values = unpack(ids, returned, rows, gw, n_groups)
    return (grad_queries, grad_keys, grad_values, grad_proj)


def solution(mesh):
    in_specs = (
        P("frame", "space"),
        P("frame", "space"),
        P("frame", "space"),
        P("frame", "space"),
        P("space", "frame"),
    )
    out_specs = (P("frame", "space"), P("frame", "space"), P("frame", "space"), P("space", "frame"))
    return jax.shard_map(local, mesh=mesh, in_specs=in_specs, out_specs=out_specs, check_vma=False)
```

```python
import functools
import math

import jax
import jax.numpy as jnp
from jax import lax
from jax.experimental import pallas as pl
from jax.experimental.pallas import tpu as pltpu
from jax.sharding import PartitionSpec as P

HD = 128
VMEM_BYTES = 24 * 1024 * 1024
BF16 = jnp.bfloat16
F32 = jnp.float32


def bits_of(count):
    found = []
    bit = 1
    while bit < count:
        found.append(bit)
        bit *= 2
    return found


def relative_of(position, bits):
    total = 0
    for place, bit in enumerate(reversed(bits)):
        if position >> place & 1:
            total |= bit
    return total


def shift_pairs(n_groups, n_tok, step):
    return [
        (g * n_tok + t, (g + step) % n_groups * n_tok + t)
        for g in range(n_groups)
        for t in range(n_tok)
    ]


def xor_pairs(count, bit):
    return [(i, i ^ bit) for i in range(count)]


def gather_blocks(block, axis, count, bits):
    blocks = [block]
    for bit in reversed(bits):
        blocks = blocks + [lax.ppermute(b, axis, xor_pairs(count, bit)) for b in blocks]
    return blocks


def params():
    return pltpu.CompilerParams(vmem_limit_bytes=VMEM_BYTES)


def smem():
    return pl.BlockSpec(memory_space=pltpu.SMEM)


def vmem():
    return pl.BlockSpec(memory_space=pltpu.VMEM)


def aligned(value, unit):
    return pl.multiple_of(value, unit)


def dot(a, b, dims):
    return lax.dot_general(a, b, (dims, ((), ())), preferred_element_type=F32)


def whole_call(body, out_shape, args, name, scratch=(), cost=None):
    single = not isinstance(out_shape, list)
    return pl.pallas_call(
        body,
        out_shape=out_shape,
        in_specs=[smem()] + [vmem()] * (len(args) - 1),
        out_specs=vmem() if single else [vmem()] * len(out_shape),
        scratch_shapes=list(scratch),
        compiler_params=params(),
        cost_estimate=cost,
        name=name,
    )(*args)


def pack_kernel(n_groups, ids, q, k, v, w, *refs):
    outs, sems = refs[:-1], refs[-1]
    rows, depth = q.shape[0], w.shape[0]
    gw = q.shape[1] // n_groups
    copies = []
    for s in range(n_groups):
        cols = pl.ds(aligned(lax.rem(ids[0] + s, n_groups) * gw, HD), gw)
        own = outs[n_groups] if s == 0 else outs[s].at[pl.ds(2 * rows + depth, rows), :]
        for source, target in (
            (k, outs[s].at[pl.ds(0, rows), :]),
            (v, outs[s].at[pl.ds(rows, rows), :]),
            (w, outs[s].at[pl.ds(2 * rows, depth), :]),
            (q, own),
        ):
            copies.append(
                pltpu.make_async_copy(source.at[:, cols], target, sems.at[len(copies)])
            )
    for copy in copies:
        copy.start()
    for copy in copies:
        copy.wait()


def pack(ids, q, k, v, w, n_groups):
    rows, width = q.shape
    gw = width // n_groups
    shared = 2 * rows + w.shape[0]
    shapes = (
        [jax.ShapeDtypeStruct((shared, gw), BF16)]
        + [jax.ShapeDtypeStruct((shared + rows, gw), BF16)] * (n_groups - 1)
        + [jax.ShapeDtypeStruct((rows, gw), BF16)]
    )
    return pl.pallas_call(
        functools.partial(pack_kernel, n_groups),
        out_shape=shapes,
        in_specs=[smem()] + [pl.BlockSpec(memory_space=pltpu.HBM)] * 4,
        out_specs=[vmem()] * len(shapes),
        scratch_shapes=[pltpu.SemaphoreType.DMA((4 * n_groups,))],
        compiler_params=pltpu.CompilerParams(vmem_limit_bytes=60 * 1024 * 1024),
        name="pack",
    )(ids, q, k, v, w)


def stack_kernel(n_groups, rows, ids, *refs):
    pieces, out = refs[:n_groups], refs[n_groups]
    shared = out.shape[0] // n_groups
    depth = shared - 2 * rows
    for s, piece in enumerate(pieces):
        for i in range(2):
            at = (i * n_groups + s) * rows
            out[at : at + rows, :] = piece[i * rows : (i + 1) * rows, :]
        at = 2 * n_groups * rows + s * depth
        out[at : at + depth, :] = piece[2 * rows : shared, :]


def stack(ids, pieces, rows):
    shared, gw = pieces[0].shape
    return whole_call(
        functools.partial(stack_kernel, len(pieces), rows),
        jax.ShapeDtypeStruct((shared * len(pieces), gw), BF16),
        (ids, *pieces),
        "stack",
    )


def stack_queries_kernel(ids, own, *refs):
    pieces, out = refs[:-1], refs[-1]
    rows = own.shape[0]
    out[:rows, :] = own[...]
    for s, piece in enumerate(pieces):
        out[(s + 1) * rows : (s + 2) * rows, :] = piece[piece.shape[0] - rows :, :]


def stack_queries(ids, own, pieces):
    rows, gw = own.shape
    shape = jax.ShapeDtypeStruct((rows * (len(pieces) + 1), gw), BF16)
    return whole_call(stack_queries_kernel, shape, (ids, own, *pieces), "stack_queries")


def forward_kernel(chunk, scale, q_in, *refs):
    blocks, (p_out, o_out, il_out, logits) = refs[:-4], refs[-4:]
    part = blocks[0].shape[0] // 2
    q = q_in[...]
    top = None
    for j, kv in enumerate(blocks):
        for c in range(0, part, chunk):
            at = j * part + c
            block = dot(kv[c : c + chunk, :], q, ((1,), (1,)))
            logits[at : at + chunk, :] = block
            here = jnp.max(block, axis=0, keepdims=True)
            top = here if top is None else jnp.maximum(top, here)
    top = top * scale
    total = jnp.zeros_like(top)
    out = jnp.zeros((HD, q.shape[0]), F32)
    for j, kv in enumerate(blocks):
        for c in range(0, part, chunk):
            at = j * part + c
            prob = jnp.exp2(logits[at : at + chunk, :] * scale - top)
            total = total + jnp.sum(prob, axis=0, keepdims=True)
            low = prob.astype(BF16)
            p_out[0, at : at + chunk, :] = low
            out = out + dot(kv[part + c : part + c + chunk, :], low, ((0,), (0,)))
    inverse = 1.0 / total
    il_out[0] = inverse
    o_out[...] = (out * inverse).T.astype(BF16)


def forward(q, blocks, part):
    n_q, gw = q.shape
    heads = gw // HD
    seq_len = part * len(blocks)
    chunk = part if part <= 640 else math.gcd(part, 512)
    scale = math.log2(math.e) / math.sqrt(HD)
    return pl.pallas_call(
        functools.partial(forward_kernel, chunk, scale),
        grid=(heads,),
        out_shape=[
            jax.ShapeDtypeStruct((heads, seq_len, n_q), BF16),
            jax.ShapeDtypeStruct((n_q, gw), BF16),
            jax.ShapeDtypeStruct((heads, 1, n_q), F32),
        ],
        in_specs=[pl.BlockSpec((n_q, HD), lambda h: (0, h))]
        + [pl.BlockSpec((2 * part, HD), lambda h: (0, h))] * len(blocks),
        out_specs=[
            pl.BlockSpec((1, seq_len, n_q), lambda h: (h, 0, 0)),
            pl.BlockSpec((n_q, HD), lambda h: (0, h)),
            pl.BlockSpec((1, 1, n_q), lambda h: (h, 0, 0)),
        ],
        scratch_shapes=[pltpu.VMEM((seq_len, n_q), F32)],
        compiler_params=params(),
        cost_estimate=pl.CostEstimate(
            flops=4 * heads * seq_len * n_q * HD,
            bytes_accessed=2 * heads * seq_len * n_q,
            transcendentals=heads * seq_len * n_q,
        ),
        name="forward",
    )(q, *blocks)


def backward_kernel(n_groups, chunk, factor, *refs):
    q_in, p_in, o_in, il_in, da_in = refs[:5]
    dq_outs, halves, dq_all = refs[-n_groups - 3 : -3], refs[-3:-1], refs[-1]
    blocks = refs[5 : -n_groups - 3]
    part = blocks[0].shape[0] // 2
    rows = dq_outs[0].shape[0]
    q = q_in[...]
    n_q = q.shape[0]
    inverse = jnp.broadcast_to(il_in[0], (HD, n_q)).T
    da = (da_in[...].astype(F32) * inverse).astype(BF16)
    delta = jnp.sum((da.astype(F32) * o_in[...].astype(F32)).T, axis=0, keepdims=True)
    dq = jnp.zeros((HD, n_q), F32)
    per_half = max(1, len(blocks) // 2)
    for j, kv in enumerate(blocks):
        out = halves[j // per_half]
        base = j % per_half * 2 * part
        for c in range(0, part, chunk):
            at = j * part + c
            low = p_in[0, at : at + chunk, :]
            dp = dot(kv[part + c : part + c + chunk, :], da, ((1,), (1,)))
            ds = (low.astype(F32) * (dp - delta)).astype(BF16)
            dk = (factor * dot(ds, q, ((1,), (0,)))).astype(BF16)
            out[base + c : base + c + chunk, :] = dk
            dv = dot(low, da, ((1,), (0,))).astype(BF16)
            out[base + part + c : base + part + c + chunk, :] = dv
            dq = dq + dot(kv[c : c + chunk, :], ds, ((0,), (0,)))
    dq_all[...] = (factor * dq).T.astype(BF16)
    for s in range(n_groups):
        dq_outs[s][...] = dq_all[s * rows : (s + 1) * rows, :]


def backward(head, count, q, blocks, part, probs, out, inverse, grad_attn, n_groups):
    n_q = q.shape[0]
    rows = n_q // n_groups
    seq_len = part * len(blocks)
    chunk = part if part <= 640 else math.gcd(part, 512)
    per_half = max(1, len(blocks) // 2)
    column = pl.BlockSpec((n_q, HD), lambda i: (0, head + i))
    results = pl.pallas_call(
        functools.partial(backward_kernel, n_groups, chunk, 1.0 / math.sqrt(HD)),
        grid=(count,),
        out_shape=[jax.ShapeDtypeStruct((rows, count * HD), BF16)] * n_groups
        + [jax.ShapeDtypeStruct((per_half * 2 * part, count * HD), BF16)] * 2,
        in_specs=[
            column,
            pl.BlockSpec((1, seq_len, n_q), lambda i: (head + i, 0, 0)),
            column,
            pl.BlockSpec((1, 1, n_q), lambda i: (head + i, 0, 0)),
            column,
        ]
        + [pl.BlockSpec((2 * part, HD), lambda i: (0, head + i))] * len(blocks),
        out_specs=[pl.BlockSpec((rows, HD), lambda i: (0, i))] * n_groups
        + [pl.BlockSpec((per_half * 2 * part, HD), lambda i: (0, i))] * 2,
        scratch_shapes=[pltpu.VMEM((n_q, HD), BF16)],
        compiler_params=params(),
        cost_estimate=pl.CostEstimate(
            flops=n_q * HD,
            bytes_accessed=2 * n_q * HD,
            transcendentals=0,
        ),
        name="backward",
    )(q, probs, out, inverse, grad_attn, *blocks)
    return results[:n_groups], results[n_groups:]


def frame_block(ids, sign, s, position, n_groups, n_tok):
    group = lax.rem(ids[0] + sign * s + n_groups, n_groups)
    return group * n_tok + jnp.bitwise_xor(ids[1], relative_of(position, bits_of(n_tok)))


def tokens_of(ids, tokens, grads, n_groups, n_space):
    rows, part = grads[0].shape
    for r in range(n_space):
        for s in range(n_groups):
            tokens[s * rows : (s + 1) * rows, :] = grads[r * n_groups + s][...]
        start = jnp.bitwise_xor(ids[2], relative_of(r, bits_of(n_space))) * part
        yield tokens[...], pl.ds(aligned(start, 16), part)


def attn_kernel(n_groups, n_tok, n_space, ids, *refs):
    blocks, grads = refs[:n_tok], refs[n_tok : n_tok + n_groups * n_space]
    grad_attn, weight, tokens = refs[n_tok + n_groups * n_space :]
    depth = weight.shape[0] // (n_groups * n_tok)
    first = blocks[0].shape[0] - n_groups * depth
    for j in range(n_tok):
        for s in range(n_groups):
            place = frame_block(ids, -1, s, j, n_groups, n_tok) * depth
            at = first + s * depth
            weight[pl.ds(aligned(place, 16), depth), :] = blocks[j][at : at + depth, :]
    total = None
    for block, here in tokens_of(ids, tokens, grads, n_groups, n_space):
        term = dot(block, weight[here, :], ((1,), (0,)))
        total = term if total is None else total + term
    grad_attn[...] = total.astype(BF16)


def projection_cost(n_q, gw):
    return pl.CostEstimate(
        flops=n_q * gw,
        bytes_accessed=2 * n_q * gw,
        transcendentals=0,
    )


def attn_gradient(ids, blocks, grads, depth, n_groups, n_tok, n_space):
    rows, part = grads[0].shape
    n_q, gw = rows * n_groups, blocks[0].shape[1]
    total = n_groups * n_tok * depth
    return whole_call(
        functools.partial(attn_kernel, n_groups, n_tok, n_space),
        jax.ShapeDtypeStruct((n_q, gw), BF16),
        (ids, *blocks, *grads),
        "attn_gradient",
        [pltpu.VMEM((total, gw), BF16), pltpu.VMEM((n_q, part), BF16)],
        projection_cost(n_q, gw),
    )


def proj_kernel(n_groups, n_tok, n_space, ids, attn, *refs):
    grads, (kept, sent, whole, tokens) = refs[: n_groups * n_space], refs[n_groups * n_space :]
    depth = whole.shape[0] // (n_groups * n_tok)
    for block, here in tokens_of(ids, tokens, grads, n_groups, n_space):
        whole[here, :] = dot(block, attn[...], ((0,), (0,))).astype(BF16)
    per_half = max(1, n_tok // 2)
    for j in range(n_tok):
        half = sent if j >= per_half else kept
        for s in range(n_groups):
            place = frame_block(ids, 1, s, j, n_groups, n_tok) * depth
            at = (j % per_half * n_groups + s) * depth
            half[at : at + depth, :] = whole[pl.ds(aligned(place, 16), depth), :]


def proj_gradient(ids, attn, grads, depth, n_groups, n_tok, n_space):
    n_q, gw = attn.shape
    part = grads[0].shape[1]
    half = n_groups * depth * max(1, n_tok // 2)
    total = n_groups * n_tok * depth
    return whole_call(
        functools.partial(proj_kernel, n_groups, n_tok, n_space),
        [jax.ShapeDtypeStruct((half, gw), BF16)] * 2,
        (ids, attn, *grads),
        "proj_gradient",
        [pltpu.VMEM((total, gw), BF16), pltpu.VMEM((n_q, part), BF16)],
        projection_cost(n_q, gw),
    )


def add_kernel(ids, kept, other, *outs):
    rows = outs[0].shape[0]
    for i, out in enumerate(outs):
        total = kept[i * rows : (i + 1) * rows, :].astype(F32)
        total = total + other[i * rows : (i + 1) * rows, :].astype(F32)
        out[...] = total.astype(BF16)


def add_parts(ids, kept, other, count):
    rows, gw = kept.shape
    shape = jax.ShapeDtypeStruct((rows // count, gw), BF16)
    return whole_call(add_kernel, [shape] * count, (ids, kept, other), "add_parts")


def halve(ids, kept, sent, n_frame, bits):
    for bit in bits[:-1]:
        other = lax.ppermute(sent, "frame", xor_pairs(n_frame, bit))
        kept, sent = add_parts(ids, kept, other, 2)
    return kept, sent


def finish_kernel(n_groups, ids, kept, other, *refs):
    dq, outs = refs[:n_groups], refs[n_groups:]
    rows = dq[0].shape[0]
    for s in range(n_groups):
        outs[s][:rows, :] = dq[s][...]
        for i in range(2):
            at = (i * n_groups + s) * rows
            total = kept[at : at + rows, :].astype(F32) + other[at : at + rows, :].astype(F32)
            outs[s][(i + 1) * rows : (i + 2) * rows, :] = total.astype(BF16)


def finish(ids, kept, other, dq, n_groups):
    rows, cols = dq[0].shape
    return whole_call(
        functools.partial(finish_kernel, n_groups),
        [jax.ShapeDtypeStruct((3 * rows, cols), BF16)] * n_groups,
        (ids, kept, other, *dq),
        "finish",
    )


def unpack_kernel(n_groups, widths, ids, *refs):
    pieces, outs = refs[:-3], refs[-3:]
    rows, gw = outs[0].shape[0], outs[0].shape[1] // n_groups
    before = 0
    for c, cols in enumerate(widths):
        for s in range(n_groups):
            start = lax.rem(ids[0] + s, n_groups) * gw + before
            for i, out in enumerate(outs):
                piece = pieces[c * n_groups + s][i * rows : (i + 1) * rows, :]
                out[:, pl.ds(aligned(start, HD), cols)] = piece
        before += cols


def unpack(ids, chunks, rows, gw, n_groups):
    widths = [HD, gw - HD][: len(chunks)]
    return whole_call(
        functools.partial(unpack_kernel, n_groups, widths),
        [jax.ShapeDtypeStruct((rows, gw * n_groups), BF16)] * 3,
        (ids, *[piece for pieces in chunks for piece in pieces]),
        "unpack",
    )


def join_kernel(n_groups, ids, *refs):
    pieces, out = refs[:n_groups], refs[n_groups]
    gw = pieces[0].shape[1]
    for s in range(n_groups):
        start = lax.rem(ids[0] - s + n_groups, n_groups) * gw
        out[:, pl.ds(aligned(start, HD), gw)] = pieces[s][...].astype(F32)


def join(ids, pieces, n_groups):
    rows, gw = pieces[0].shape
    return whole_call(
        functools.partial(join_kernel, n_groups),
        jax.ShapeDtypeStruct((rows, gw * n_groups), F32),
        (ids, *pieces),
        "join",
    )


def exchange(pieces, n_groups, n_tok, sign):
    return [pieces[0]] + [
        lax.ppermute(pieces[s], "frame", shift_pairs(n_groups, n_tok, sign * s))
        for s in range(1, n_groups)
    ]


def local(queries, keys, values, grad_out, proj_weight):
    n_frame = lax.axis_size("frame")
    n_space = lax.axis_size("space")
    rows, width = queries.shape
    gw = width // math.gcd(width // HD, n_frame)
    depth = proj_weight.shape[1]
    n_groups = math.gcd(width // HD, n_frame)
    n_tok = n_frame // n_groups
    tok_bits = bits_of(n_tok)
    space_bits = bits_of(n_space)
    heads = width // n_groups // HD
    shared = 2 * rows + depth
    frame = lax.axis_index("frame")
    ids = jnp.stack([frame // n_tok, frame % n_tok, lax.axis_index("space")]).astype(jnp.int32)

    tie = lax.optimization_barrier
    last = xor_pairs(n_frame, tok_bits[-1])

    *pieces, own_q = pack(ids, queries, keys, values, proj_weight.T, n_groups)
    pieces = exchange(pieces, n_groups, n_tok, 1)
    q_pieces = pieces[1:]
    own, others, ring, across = [pieces[0]], [], grad_out, []
    for s in range(n_groups):
        others.append(lax.ppermute(own[s], "frame", last))
        across.append(gather_blocks(ring, "space", n_space, space_bits))
        if s + 1 < n_groups:
            ring = lax.ppermute(ring, "frame", shift_pairs(n_groups, n_tok, 1))
            step = (ring, pieces[s + 1][:shared], others[s], *across[s])
            ring, piece, others[s], *across[s] = tie(step)
            own.append(piece)

    q = stack_queries(ids, own_q, q_pieces)
    blocks = [stack(ids, own, rows), stack(ids, others, rows)]
    for bit in reversed(tok_bits[:-1]):
        blocks = blocks + [lax.ppermute(b, "frame", xor_pairs(n_frame, bit)) for b in blocks]
    part = n_groups * rows
    probs, out, inverse = forward(q, blocks, part)
    grads = [across[s][r] for r in range(n_space) for s in range(n_groups)]
    grad_attn = attn_gradient(ids, blocks, grads, depth, n_groups, n_tok, n_space)

    def attention_halves(head, count, q):
        return backward(head, count, q, blocks, part, probs, out, inverse, grad_attn, n_groups)

    def across_x(piece):
        return lax.ppermute(piece, "frame", last)

    dq, halves = attention_halves(0, 1, q)
    kept, sent = halve(ids, *halves, n_frame, tok_bits)
    q, kept, sent = tie((q, kept, sent))
    other = across_x(sent)
    if heads > 1:
        dq_rest, halves = attention_halves(1, heads - 1, q)
        other, *halves = tie((other, *halves))
    sums = finish(ids, kept, other, dq, n_groups)
    returned = [exchange(sums, n_groups, n_tok, -1)]
    out_after, *_ = tie((out, *sums))
    proj = proj_gradient(ids, out_after, grads, depth, n_groups, n_tok, n_space)
    if heads > 1:
        kept, sent = halve(ids, *halves, n_frame, tok_bits)
        other = across_x(sent)
        other, proj, *returned[0][1:] = tie((other, tuple(proj), *returned[0][1:]))
        sums = finish(ids, kept, other, dq_rest, n_groups)
        returned.append(exchange(sums, n_groups, n_tok, -1))
    proj_kept, proj_sent = halve(ids, *proj, n_frame, tok_bits)
    if heads > 1:
        proj_sent, *_ = tie((proj_sent, *sums))
    proj = add_parts(ids, proj_kept, across_x(proj_sent), n_groups)
    proj_pieces = exchange(proj, n_groups, n_tok, 1)
    grad_proj = join(ids, proj_pieces, n_groups).T
    grad_queries, grad_keys, grad_values = unpack(ids, returned, rows, gw, n_groups)
    return (grad_queries, grad_keys, grad_values, grad_proj)


def solution(mesh):
    in_specs = (
        P("frame", "space"),
        P("frame", "space"),
        P("frame", "space"),
        P("frame", "space"),
        P("space", "frame"),
    )
    out_specs = (P("frame", "space"), P("frame", "space"), P("frame", "space"), P("space", "frame"))
    return jax.shard_map(local, mesh=mesh, in_specs=in_specs, out_specs=out_specs, check_vma=False)
```

```python
import functools
import math

import jax
import jax.numpy as jnp
from jax import lax
from jax.experimental import pallas as pl
from jax.experimental.pallas import tpu as pltpu
from jax.sharding import PartitionSpec as P

HD = 128
VMEM_BYTES = 24 * 1024 * 1024
BF16 = jnp.bfloat16
F32 = jnp.float32


def bits_of(count):
    found = []
    bit = 1
    while bit < count:
        found.append(bit)
        bit *= 2
    return found


def relative_of(position, bits):
    total = 0
    for place, bit in enumerate(reversed(bits)):
        if position >> place & 1:
            total |= bit
    return total


def shift_pairs(n_groups, n_tok, step):
    return [
        (g * n_tok + t, (g + step) % n_groups * n_tok + t)
        for g in range(n_groups)
        for t in range(n_tok)
    ]


def xor_pairs(count, bit):
    return [(i, i ^ bit) for i in range(count)]


def gather_blocks(block, axis, count, bits):
    blocks = [block]
    for bit in reversed(bits):
        blocks = blocks + [lax.ppermute(b, axis, xor_pairs(count, bit)) for b in blocks]
    return blocks


def params():
    return pltpu.CompilerParams(vmem_limit_bytes=VMEM_BYTES)


def smem():
    return pl.BlockSpec(memory_space=pltpu.SMEM)


def vmem():
    return pl.BlockSpec(memory_space=pltpu.VMEM)


def aligned(value, unit):
    return pl.multiple_of(value, unit)


def dot(a, b, dims):
    return lax.dot_general(a, b, (dims, ((), ())), preferred_element_type=F32)


def whole_call(body, out_shape, args, name, scratch=(), cost=None):
    single = not isinstance(out_shape, list)
    return pl.pallas_call(
        body,
        out_shape=out_shape,
        in_specs=[smem()] + [vmem()] * (len(args) - 1),
        out_specs=vmem() if single else [vmem()] * len(out_shape),
        scratch_shapes=list(scratch),
        compiler_params=params(),
        cost_estimate=cost,
        name=name,
    )(*args)


def pack_kernel(n_groups, ids, q, k, v, w, *refs):
    outs, sems = refs[:-1], refs[-1]
    rows, depth = q.shape[0], w.shape[0]
    gw = q.shape[1] // n_groups
    copies = []
    for s in range(n_groups):
        cols = pl.ds(aligned(lax.rem(ids[0] + s, n_groups) * gw, HD), gw)
        own = outs[n_groups] if s == 0 else outs[s].at[pl.ds(2 * rows + depth, rows), :]
        for source, target in (
            (k, outs[s].at[pl.ds(0, rows), :]),
            (v, outs[s].at[pl.ds(rows, rows), :]),
            (w, outs[s].at[pl.ds(2 * rows, depth), :]),
            (q, own),
        ):
            copies.append(
                pltpu.make_async_copy(source.at[:, cols], target, sems.at[len(copies)])
            )
    for copy in copies:
        copy.start()
    for copy in copies:
        copy.wait()


def pack(ids, q, k, v, w, n_groups):
    rows, width = q.shape
    gw = width // n_groups
    shared = 2 * rows + w.shape[0]
    shapes = (
        [jax.ShapeDtypeStruct((shared, gw), BF16)]
        + [jax.ShapeDtypeStruct((shared + rows, gw), BF16)] * (n_groups - 1)
        + [jax.ShapeDtypeStruct((rows, gw), BF16)]
    )
    return pl.pallas_call(
        functools.partial(pack_kernel, n_groups),
        out_shape=shapes,
        in_specs=[smem()] + [pl.BlockSpec(memory_space=pltpu.HBM)] * 4,
        out_specs=[vmem()] * len(shapes),
        scratch_shapes=[pltpu.SemaphoreType.DMA((4 * n_groups,))],
        compiler_params=pltpu.CompilerParams(vmem_limit_bytes=60 * 1024 * 1024),
        name="pack",
    )(ids, q, k, v, w)


def stack_kernel(n_groups, rows, ids, *refs):
    pieces, out = refs[:n_groups], refs[n_groups]
    shared = out.shape[0] // n_groups
    depth = shared - 2 * rows
    for s, piece in enumerate(pieces):
        for i in range(2):
            at = (i * n_groups + s) * rows
            out[at : at + rows, :] = piece[i * rows : (i + 1) * rows, :]
        at = 2 * n_groups * rows + s * depth
        out[at : at + depth, :] = piece[2 * rows : shared, :]


def stack(ids, pieces, rows):
    shared, gw = pieces[0].shape
    return whole_call(
        functools.partial(stack_kernel, len(pieces), rows),
        jax.ShapeDtypeStruct((shared * len(pieces), gw), BF16),
        (ids, *pieces),
        "stack",
    )


def stack_queries_kernel(ids, own, *refs):
    pieces, out = refs[:-1], refs[-1]
    rows = own.shape[0]
    out[:rows, :] = own[...]
    for s, piece in enumerate(pieces):
        out[(s + 1) * rows : (s + 2) * rows, :] = piece[piece.shape[0] - rows :, :]


def stack_queries(ids, own, pieces):
    rows, gw = own.shape
    shape = jax.ShapeDtypeStruct((rows * (len(pieces) + 1), gw), BF16)
    return whole_call(stack_queries_kernel, shape, (ids, own, *pieces), "stack_queries")


def forward_kernel(chunk, scale, q_in, *refs):
    blocks, (p_out, o_out, il_out, logits) = refs[:-4], refs[-4:]
    part = blocks[0].shape[0] // 2
    q = q_in[...]
    top = None
    for j, kv in enumerate(blocks):
        for c in range(0, part, chunk):
            at = j * part + c
            block = dot(kv[c : c + chunk, :], q, ((1,), (1,)))
            logits[at : at + chunk, :] = block
            here = jnp.max(block, axis=0, keepdims=True)
            top = here if top is None else jnp.maximum(top, here)
    top = top * scale
    total = jnp.zeros_like(top)
    out = jnp.zeros((HD, q.shape[0]), F32)
    for j, kv in enumerate(blocks):
        for c in range(0, part, chunk):
            at = j * part + c
            prob = jnp.exp2(logits[at : at + chunk, :] * scale - top)
            total = total + jnp.sum(prob, axis=0, keepdims=True)
            low = prob.astype(BF16)
            p_out[0, at : at + chunk, :] = low
            out = out + dot(kv[part + c : part + c + chunk, :], low, ((0,), (0,)))
    inverse = 1.0 / total
    il_out[0] = inverse
    o_out[...] = (out * inverse).T.astype(BF16)


def forward(q, blocks, part):
    n_q, gw = q.shape
    heads = gw // HD
    seq_len = part * len(blocks)
    chunk = part if part <= 640 else math.gcd(part, 512)
    scale = math.log2(math.e) / math.sqrt(HD)
    return pl.pallas_call(
        functools.partial(forward_kernel, chunk, scale),
        grid=(heads,),
        out_shape=[
            jax.ShapeDtypeStruct((heads, seq_len, n_q), BF16),
            jax.ShapeDtypeStruct((n_q, gw), BF16),
            jax.ShapeDtypeStruct((heads, 1, n_q), F32),
        ],
        in_specs=[pl.BlockSpec((n_q, HD), lambda h: (0, h))]
        + [pl.BlockSpec((2 * part, HD), lambda h: (0, h))] * len(blocks),
        out_specs=[
            pl.BlockSpec((1, seq_len, n_q), lambda h: (h, 0, 0)),
            pl.BlockSpec((n_q, HD), lambda h: (0, h)),
            pl.BlockSpec((1, 1, n_q), lambda h: (h, 0, 0)),
        ],
        scratch_shapes=[pltpu.VMEM((seq_len, n_q), F32)],
        compiler_params=params(),
        cost_estimate=pl.CostEstimate(
            flops=4 * heads * seq_len * n_q * HD,
            bytes_accessed=2 * heads * seq_len * n_q,
            transcendentals=heads * seq_len * n_q,
        ),
        name="forward",
    )(q, *blocks)


def backward_kernel(n_groups, chunk, factor, *refs):
    q_in, p_in, o_in, il_in, da_in = refs[:5]
    dq_outs, halves, dq_all = refs[-n_groups - 3 : -3], refs[-3:-1], refs[-1]
    blocks = refs[5 : -n_groups - 3]
    part = blocks[0].shape[0] // 2
    rows = dq_outs[0].shape[0]
    q = q_in[...]
    n_q = q.shape[0]
    inverse = jnp.broadcast_to(il_in[0], (HD, n_q)).T
    da = (da_in[...].astype(F32) * inverse).astype(BF16)
    delta = jnp.sum((da.astype(F32) * o_in[...].astype(F32)).T, axis=0, keepdims=True)
    dq = jnp.zeros((HD, n_q), F32)
    per_half = max(1, len(blocks) // 2)
    for j, kv in enumerate(blocks):
        out = halves[j // per_half]
        base = j % per_half * 2 * part
        for c in range(0, part, chunk):
            at = j * part + c
            low = p_in[0, at : at + chunk, :]
            dp = dot(kv[part + c : part + c + chunk, :], da, ((1,), (1,)))
            ds = (low.astype(F32) * (dp - delta)).astype(BF16)
            dk = (factor * dot(ds, q, ((1,), (0,)))).astype(BF16)
            out[base + c : base + c + chunk, :] = dk
            dv = dot(low, da, ((1,), (0,))).astype(BF16)
            out[base + part + c : base + part + c + chunk, :] = dv
            dq = dq + dot(kv[c : c + chunk, :], ds, ((0,), (0,)))
    dq_all[...] = (factor * dq).T.astype(BF16)
    for s in range(n_groups):
        dq_outs[s][...] = dq_all[s * rows : (s + 1) * rows, :]


def backward(head, count, q, blocks, part, probs, out, inverse, grad_attn, n_groups):
    n_q = q.shape[0]
    rows = n_q // n_groups
    seq_len = part * len(blocks)
    chunk = part if part <= 640 else math.gcd(part, 512)
    per_half = max(1, len(blocks) // 2)
    column = pl.BlockSpec((n_q, HD), lambda i: (0, head + i))
    results = pl.pallas_call(
        functools.partial(backward_kernel, n_groups, chunk, 1.0 / math.sqrt(HD)),
        grid=(count,),
        out_shape=[jax.ShapeDtypeStruct((rows, count * HD), BF16)] * n_groups
        + [jax.ShapeDtypeStruct((per_half * 2 * part, count * HD), BF16)] * 2,
        in_specs=[
            column,
            pl.BlockSpec((1, seq_len, n_q), lambda i: (head + i, 0, 0)),
            column,
            pl.BlockSpec((1, 1, n_q), lambda i: (head + i, 0, 0)),
            column,
        ]
        + [pl.BlockSpec((2 * part, HD), lambda i: (0, head + i))] * len(blocks),
        out_specs=[pl.BlockSpec((rows, HD), lambda i: (0, i))] * n_groups
        + [pl.BlockSpec((per_half * 2 * part, HD), lambda i: (0, i))] * 2,
        scratch_shapes=[pltpu.VMEM((n_q, HD), BF16)],
        compiler_params=params(),
        cost_estimate=pl.CostEstimate(
            flops=n_q * HD,
            bytes_accessed=2 * n_q * HD,
            transcendentals=0,
        ),
        name="backward",
    )(q, probs, out, inverse, grad_attn, *blocks)
    return results[:n_groups], results[n_groups:]


def frame_block(ids, sign, s, position, n_groups, n_tok):
    group = lax.rem(ids[0] + sign * s + n_groups, n_groups)
    return group * n_tok + jnp.bitwise_xor(ids[1], relative_of(position, bits_of(n_tok)))


def tokens_of(ids, tokens, grads, n_groups, n_space):
    rows, part = grads[0].shape
    count = len(grads) // n_space
    for r in range(n_space):
        tokens[:rows, :] = grads[r * count][...]
        for s in range(1, n_groups):
            above, below = grads[r * count + 2 * s - 1 : r * count + 2 * s + 1]
            here = slice(s * rows, (s + 1) * rows)
            tokens[here, :] = jnp.where(ids[0] >= s, above[...], below[...])
        start = jnp.bitwise_xor(ids[2], relative_of(r, bits_of(n_space))) * part
        yield tokens[...], pl.ds(aligned(start, 16), part)


def attn_kernel(n_groups, n_tok, n_space, ids, *refs):
    blocks, grads = refs[:n_tok], refs[n_tok:-3]
    grad_attn, weight, tokens = refs[-3:]
    depth = weight.shape[0] // (n_groups * n_tok)
    first = blocks[0].shape[0] - n_groups * depth
    for j in range(n_tok):
        for s in range(n_groups):
            place = frame_block(ids, -1, s, j, n_groups, n_tok) * depth
            at = first + s * depth
            weight[pl.ds(aligned(place, 16), depth), :] = blocks[j][at : at + depth, :]
    total = None
    for block, here in tokens_of(ids, tokens, grads, n_groups, n_space):
        term = dot(block, weight[here, :], ((1,), (0,)))
        total = term if total is None else total + term
    grad_attn[...] = total.astype(BF16)


def projection_cost(n_q, gw):
    return pl.CostEstimate(
        flops=n_q * gw,
        bytes_accessed=2 * n_q * gw,
        transcendentals=0,
    )


def attn_gradient(ids, blocks, grads, depth, n_groups, n_tok, n_space):
    rows, part = grads[0].shape
    n_q, gw = rows * n_groups, blocks[0].shape[1]
    total = n_groups * n_tok * depth
    return whole_call(
        functools.partial(attn_kernel, n_groups, n_tok, n_space),
        jax.ShapeDtypeStruct((n_q, gw), BF16),
        (ids, *blocks, *grads),
        "attn_gradient",
        [pltpu.VMEM((total, gw), BF16), pltpu.VMEM((n_q, part), BF16)],
        projection_cost(n_q, gw),
    )


def proj_kernel(n_groups, n_tok, n_space, ids, attn, *refs):
    grads, (kept, sent, whole, tokens) = refs[:-4], refs[-4:]
    depth = whole.shape[0] // (n_groups * n_tok)
    for block, here in tokens_of(ids, tokens, grads, n_groups, n_space):
        whole[here, :] = dot(block, attn[...], ((0,), (0,))).astype(BF16)
    per_half = max(1, n_tok // 2)
    for j in range(n_tok):
        half = sent if j >= per_half else kept
        for s in range(n_groups):
            place = frame_block(ids, 1, s, j, n_groups, n_tok) * depth
            at = (j % per_half * n_groups + s) * depth
            half[at : at + depth, :] = whole[pl.ds(aligned(place, 16), depth), :]


def proj_gradient(ids, attn, grads, depth, n_groups, n_tok, n_space):
    n_q, gw = attn.shape
    part = grads[0].shape[1]
    half = n_groups * depth * max(1, n_tok // 2)
    total = n_groups * n_tok * depth
    return whole_call(
        functools.partial(proj_kernel, n_groups, n_tok, n_space),
        [jax.ShapeDtypeStruct((half, gw), BF16)] * 2,
        (ids, attn, *grads),
        "proj_gradient",
        [pltpu.VMEM((total, gw), BF16), pltpu.VMEM((n_q, part), BF16)],
        projection_cost(n_q, gw),
    )


def add_kernel(ids, kept, other, *outs):
    rows = outs[0].shape[0]
    for i, out in enumerate(outs):
        total = kept[i * rows : (i + 1) * rows, :].astype(F32)
        total = total + other[i * rows : (i + 1) * rows, :].astype(F32)
        out[...] = total.astype(BF16)


def add_parts(ids, kept, other, count):
    rows, gw = kept.shape
    shape = jax.ShapeDtypeStruct((rows // count, gw), BF16)
    return whole_call(add_kernel, [shape] * count, (ids, kept, other), "add_parts")


def halve(ids, kept, sent, n_frame, bits):
    for bit in bits[:-1]:
        other = lax.ppermute(sent, "frame", xor_pairs(n_frame, bit))
        kept, sent = add_parts(ids, kept, other, 2)
    return kept, sent


def finish_kernel(n_groups, ids, kept, other, *refs):
    dq, outs = refs[:n_groups], refs[n_groups:]
    rows = dq[0].shape[0]
    for s in range(n_groups):
        outs[s][:rows, :] = dq[s][...]
        for i in range(2):
            at = (i * n_groups + s) * rows
            total = kept[at : at + rows, :].astype(F32) + other[at : at + rows, :].astype(F32)
            outs[s][(i + 1) * rows : (i + 2) * rows, :] = total.astype(BF16)


def finish(ids, kept, other, dq, n_groups):
    rows, cols = dq[0].shape
    return whole_call(
        functools.partial(finish_kernel, n_groups),
        [jax.ShapeDtypeStruct((3 * rows, cols), BF16)] * n_groups,
        (ids, kept, other, *dq),
        "finish",
    )


def unpack_kernel(n_groups, widths, ids, *refs):
    pieces, outs = refs[:-3], refs[-3:]
    rows, gw = outs[0].shape[0], outs[0].shape[1] // n_groups
    before = 0
    for c, cols in enumerate(widths):
        for s in range(n_groups):
            start = lax.rem(ids[0] + s, n_groups) * gw + before
            for i, out in enumerate(outs):
                piece = pieces[c * n_groups + s][i * rows : (i + 1) * rows, :]
                out[:, pl.ds(aligned(start, HD), cols)] = piece
        before += cols


def unpack(ids, chunks, rows, gw, n_groups):
    widths = [HD, gw - HD][: len(chunks)]
    return whole_call(
        functools.partial(unpack_kernel, n_groups, widths),
        [jax.ShapeDtypeStruct((rows, gw * n_groups), BF16)] * 3,
        (ids, *[piece for pieces in chunks for piece in pieces]),
        "unpack",
    )


def join_kernel(n_groups, ids, *refs):
    pieces, out = refs[:n_groups], refs[n_groups]
    gw = pieces[0].shape[1]
    for s in range(n_groups):
        start = lax.rem(ids[0] - s + n_groups, n_groups) * gw
        out[:, pl.ds(aligned(start, HD), gw)] = pieces[s][...].astype(F32)


def join(ids, pieces, n_groups):
    rows, gw = pieces[0].shape
    return whole_call(
        functools.partial(join_kernel, n_groups),
        jax.ShapeDtypeStruct((rows, gw * n_groups), F32),
        (ids, *pieces),
        "join",
    )


def exchange(pieces, n_groups, n_tok, sign):
    return [pieces[0]] + [
        lax.ppermute(pieces[s], "frame", shift_pairs(n_groups, n_tok, sign * s))
        for s in range(1, n_groups)
    ]


def local(queries, keys, values, grad_out, proj_weight):
    n_frame = lax.axis_size("frame")
    n_space = lax.axis_size("space")
    rows, width = queries.shape
    gw = width // math.gcd(width // HD, n_frame)
    depth = proj_weight.shape[1]
    n_groups = math.gcd(width // HD, n_frame)
    n_tok = n_frame // n_groups
    tok_bits = bits_of(n_tok)
    space_bits = bits_of(n_space)
    heads = width // n_groups // HD
    shared = 2 * rows + depth
    frame = lax.axis_index("frame")
    ids = jnp.stack([frame // n_tok, frame % n_tok, lax.axis_index("space")]).astype(jnp.int32)

    tie = lax.optimization_barrier
    last = xor_pairs(n_frame, tok_bits[-1])

    def across_y(piece, first, end):
        groups = range(first * n_tok, end * n_tok)
        blocks = [piece]
        for bit in reversed(space_bits):
            pairs = [(f * n_space + y, f * n_space + (y ^ bit)) for f in groups for y in range(n_space)]
            blocks = blocks + [lax.ppermute(b, ("frame", "space"), pairs) for b in blocks]
        return blocks

    def along_z(piece, first, end, step):
        groups = range(first * n_tok, end * n_tok)
        return lax.ppermute(piece, "frame", [(f, f + step * n_tok) for f in groups])

    *pieces, own_q = pack(ids, queries, keys, values, proj_weight.T, n_groups)
    pieces = exchange(pieces, n_groups, n_tok, 1)
    q_pieces = pieces[1:]
    own, others = [pieces[0]], []
    up, down, across = [grad_out], [grad_out], []
    for s in range(n_groups):
        others.append(lax.ppermute(own[s], "frame", last))
        if s == 0:
            arrived = across_y(grad_out, 0, n_groups)
        else:
            arrived = across_y(up[s], s, n_groups) + across_y(down[s], 0, n_groups - s)
        across.append(arrived)
        if s + 1 < n_groups:
            going_up = along_z(up[s], s, n_groups - 1, 1)
            going_down = along_z(down[s], 1, n_groups - s, -1)
            step = (going_up, going_down, pieces[s + 1][:shared], others[s])
            if s + 2 < n_groups:
                step = (*step, *arrived)
            going_up, going_down, piece, others[s], *arrived = tie(step)
            across[s] = arrived or across[s]
            up.append(going_up)
            down.append(going_down)
            own.append(piece)

    q = stack_queries(ids, own_q, q_pieces)
    blocks = [stack(ids, own, rows), stack(ids, others, rows)]
    for bit in reversed(tok_bits[:-1]):
        blocks = blocks + [lax.ppermute(b, "frame", xor_pairs(n_frame, bit)) for b in blocks]
    part = n_groups * rows
    probs, out, inverse = forward(q, blocks, part)
    grads = []
    for r in range(n_space):
        grads.append(across[0][r])
        for s in range(1, n_groups):
            grads += [across[s][r], across[n_groups - s][n_space + r]]
    grad_attn = attn_gradient(ids, blocks, grads, depth, n_groups, n_tok, n_space)

    def attention_halves(head, count, q):
        return backward(head, count, q, blocks, part, probs, out, inverse, grad_attn, n_groups)

    def across_x(piece):
        return lax.ppermute(piece, "frame", last)

    dq, halves = attention_halves(0, 1, q)
    kept, sent = halve(ids, *halves, n_frame, tok_bits)
    q, kept, sent = tie((q, kept, sent))
    other = across_x(sent)
    if heads > 1:
        dq_rest, halves = attention_halves(1, heads - 1, q)
        other, *halves = tie((other, *halves))
    sums = finish(ids, kept, other, dq, n_groups)
    returned = [exchange(sums, n_groups, n_tok, -1)]
    out_after, *_ = tie((out, *sums))
    proj = proj_gradient(ids, out_after, grads, depth, n_groups, n_tok, n_space)
    if heads > 1:
        kept, sent = halve(ids, *halves, n_frame, tok_bits)
        other = across_x(sent)
        other, proj, *returned[0][1:] = tie((other, tuple(proj), *returned[0][1:]))
        sums = finish(ids, kept, other, dq_rest, n_groups)
        returned.append(exchange(sums, n_groups, n_tok, -1))
    proj_kept, proj_sent = halve(ids, *proj, n_frame, tok_bits)
    if heads > 1:
        proj_sent, *_ = tie((proj_sent, *sums))
    proj = add_parts(ids, proj_kept, across_x(proj_sent), n_groups)
    proj_pieces = exchange(proj, n_groups, n_tok, 1)
    grad_proj = join(ids, proj_pieces, n_groups).T
    grad_queries, grad_keys, grad_values = unpack(ids, returned, rows, gw, n_groups)
    return (grad_queries, grad_keys, grad_values, grad_proj)


def solution(mesh):
    in_specs = (
        P("frame", "space"),
        P("frame", "space"),
        P("frame", "space"),
        P("frame", "space"),
        P("space", "frame"),
    )
    out_specs = (P("frame", "space"), P("frame", "space"), P("frame", "space"), P("space", "frame"))
    return jax.shard_map(local, mesh=mesh, in_specs=in_specs, out_specs=out_specs, check_vma=False)
```

```python
import functools
import math

import jax
import jax.numpy as jnp
from jax import lax
from jax.experimental import pallas as pl
from jax.experimental.pallas import tpu as pltpu
from jax.sharding import PartitionSpec as P

HD = 128
VMEM_BYTES = 24 * 1024 * 1024
BF16 = jnp.bfloat16
F32 = jnp.float32


def bits_of(count):
    found = []
    bit = 1
    while bit < count:
        found.append(bit)
        bit *= 2
    return found


def relative_of(position, bits):
    total = 0
    for place, bit in enumerate(reversed(bits)):
        if position >> place & 1:
            total |= bit
    return total


def shift_pairs(n_groups, n_tok, step):
    return [
        (g * n_tok + t, (g + step) % n_groups * n_tok + t)
        for g in range(n_groups)
        for t in range(n_tok)
    ]


def xor_pairs(count, bit):
    return [(i, i ^ bit) for i in range(count)]


def gather_blocks(block, axis, count, bits):
    blocks = [block]
    for bit in reversed(bits):
        blocks = blocks + [lax.ppermute(b, axis, xor_pairs(count, bit)) for b in blocks]
    return blocks


def params():
    return pltpu.CompilerParams(vmem_limit_bytes=VMEM_BYTES)


def smem():
    return pl.BlockSpec(memory_space=pltpu.SMEM)


def vmem():
    return pl.BlockSpec(memory_space=pltpu.VMEM)


def aligned(value, unit):
    return pl.multiple_of(value, unit)


def dot(a, b, dims):
    return lax.dot_general(a, b, (dims, ((), ())), preferred_element_type=F32)


def whole_call(body, out_shape, args, name, scratch=(), cost=None):
    single = not isinstance(out_shape, list)
    return pl.pallas_call(
        body,
        out_shape=out_shape,
        in_specs=[smem()] + [vmem()] * (len(args) - 1),
        out_specs=vmem() if single else [vmem()] * len(out_shape),
        scratch_shapes=list(scratch),
        compiler_params=params(),
        cost_estimate=cost,
        name=name,
    )(*args)


def pack_kernel(n_groups, ids, q, k, v, w, *refs):
    outs, sems = refs[:-1], refs[-1]
    rows, depth = q.shape[0], w.shape[0]
    gw = q.shape[1] // n_groups
    copies = []
    for s in range(n_groups):
        cols = pl.ds(aligned(lax.rem(ids[0] + s, n_groups) * gw, HD), gw)
        own = outs[n_groups] if s == 0 else outs[s].at[pl.ds(2 * rows + depth, rows), :]
        for source, target in (
            (k, outs[s].at[pl.ds(0, rows), :]),
            (v, outs[s].at[pl.ds(rows, rows), :]),
            (w, outs[s].at[pl.ds(2 * rows, depth), :]),
            (q, own),
        ):
            copies.append(
                pltpu.make_async_copy(source.at[:, cols], target, sems.at[len(copies)])
            )
    for copy in copies:
        copy.start()
    for copy in copies:
        copy.wait()


def pack(ids, q, k, v, w, n_groups):
    rows, width = q.shape
    gw = width // n_groups
    shared = 2 * rows + w.shape[0]
    shapes = (
        [jax.ShapeDtypeStruct((shared, gw), BF16)]
        + [jax.ShapeDtypeStruct((shared + rows, gw), BF16)] * (n_groups - 1)
        + [jax.ShapeDtypeStruct((rows, gw), BF16)]
    )
    return pl.pallas_call(
        functools.partial(pack_kernel, n_groups),
        out_shape=shapes,
        in_specs=[smem()] + [pl.BlockSpec(memory_space=pltpu.HBM)] * 4,
        out_specs=[vmem()] * len(shapes),
        scratch_shapes=[pltpu.SemaphoreType.DMA((4 * n_groups,))],
        compiler_params=pltpu.CompilerParams(vmem_limit_bytes=60 * 1024 * 1024),
        name="pack",
    )(ids, q, k, v, w)


def stack_kernel(n_groups, rows, ids, *refs):
    pieces, out = refs[:n_groups], refs[n_groups]
    shared = out.shape[0] // n_groups
    depth = shared - 2 * rows
    for s, piece in enumerate(pieces):
        for i in range(2):
            at = (i * n_groups + s) * rows
            out[at : at + rows, :] = piece[i * rows : (i + 1) * rows, :]
        at = 2 * n_groups * rows + s * depth
        out[at : at + depth, :] = piece[2 * rows : shared, :]


def stack(ids, pieces, rows):
    shared, gw = pieces[0].shape
    return whole_call(
        functools.partial(stack_kernel, len(pieces), rows),
        jax.ShapeDtypeStruct((shared * len(pieces), gw), BF16),
        (ids, *pieces),
        "stack",
    )


def stack_queries_kernel(ids, own, *refs):
    pieces, out = refs[:-1], refs[-1]
    rows = own.shape[0]
    out[:rows, :] = own[...]
    for s, piece in enumerate(pieces):
        out[(s + 1) * rows : (s + 2) * rows, :] = piece[piece.shape[0] - rows :, :]


def stack_queries(ids, own, pieces):
    rows, gw = own.shape
    shape = jax.ShapeDtypeStruct((rows * (len(pieces) + 1), gw), BF16)
    return whole_call(stack_queries_kernel, shape, (ids, own, *pieces), "stack_queries")


def forward_kernel(chunk, scale, q_in, *refs):
    blocks, (p_out, o_out, il_out, logits) = refs[:-4], refs[-4:]
    part = blocks[0].shape[0] // 2
    q = q_in[...]
    top = None
    for j, kv in enumerate(blocks):
        for c in range(0, part, chunk):
            at = j * part + c
            block = dot(kv[c : c + chunk, :], q, ((1,), (1,)))
            logits[at : at + chunk, :] = block
            here = jnp.max(block, axis=0, keepdims=True)
            top = here if top is None else jnp.maximum(top, here)
    top = top * scale
    total = jnp.zeros_like(top)
    out = jnp.zeros((HD, q.shape[0]), F32)
    for j, kv in enumerate(blocks):
        for c in range(0, part, chunk):
            at = j * part + c
            prob = jnp.exp2(logits[at : at + chunk, :] * scale - top)
            total = total + jnp.sum(prob, axis=0, keepdims=True)
            low = prob.astype(BF16)
            p_out[0, at : at + chunk, :] = low
            out = out + dot(kv[part + c : part + c + chunk, :], low, ((0,), (0,)))
    inverse = 1.0 / total
    il_out[0] = inverse
    o_out[...] = (out * inverse).T.astype(BF16)


def forward(q, blocks, part):
    n_q, gw = q.shape
    heads = gw // HD
    seq_len = part * len(blocks)
    chunk = part if part <= 640 else math.gcd(part, 512)
    scale = math.log2(math.e) / math.sqrt(HD)
    return pl.pallas_call(
        functools.partial(forward_kernel, chunk, scale),
        grid=(heads,),
        out_shape=[
            jax.ShapeDtypeStruct((heads, seq_len, n_q), BF16),
            jax.ShapeDtypeStruct((n_q, gw), BF16),
            jax.ShapeDtypeStruct((heads, 1, n_q), F32),
        ],
        in_specs=[pl.BlockSpec((n_q, HD), lambda h: (0, h))]
        + [pl.BlockSpec((2 * part, HD), lambda h: (0, h))] * len(blocks),
        out_specs=[
            pl.BlockSpec((1, seq_len, n_q), lambda h: (h, 0, 0)),
            pl.BlockSpec((n_q, HD), lambda h: (0, h)),
            pl.BlockSpec((1, 1, n_q), lambda h: (h, 0, 0)),
        ],
        scratch_shapes=[pltpu.VMEM((seq_len, n_q), F32)],
        compiler_params=params(),
        cost_estimate=pl.CostEstimate(
            flops=4 * heads * seq_len * n_q * HD,
            bytes_accessed=2 * heads * seq_len * n_q,
            transcendentals=heads * seq_len * n_q,
        ),
        name="forward",
    )(q, *blocks)


def backward_kernel(n_groups, chunk, factor, *refs):
    q_in, p_in, o_in, il_in, da_in = refs[:5]
    dq_outs, halves, dq_all = refs[-n_groups - 3 : -3], refs[-3:-1], refs[-1]
    blocks = refs[5 : -n_groups - 3]
    part = blocks[0].shape[0] // 2
    rows = dq_outs[0].shape[0]
    q = q_in[...]
    n_q = q.shape[0]
    inverse = jnp.broadcast_to(il_in[0], (HD, n_q)).T
    da = (da_in[...].astype(F32) * inverse).astype(BF16)
    delta = jnp.sum((da.astype(F32) * o_in[...].astype(F32)).T, axis=0, keepdims=True)
    dq = jnp.zeros((HD, n_q), F32)
    per_half = max(1, len(blocks) // 2)
    for j, kv in enumerate(blocks):
        out = halves[j // per_half]
        base = j % per_half * 2 * part
        for c in range(0, part, chunk):
            at = j * part + c
            low = p_in[0, at : at + chunk, :]
            dp = dot(kv[part + c : part + c + chunk, :], da, ((1,), (1,)))
            ds = (low.astype(F32) * (dp - delta)).astype(BF16)
            dk = (factor * dot(ds, q, ((1,), (0,)))).astype(BF16)
            out[base + c : base + c + chunk, :] = dk
            dv = dot(low, da, ((1,), (0,))).astype(BF16)
            out[base + part + c : base + part + c + chunk, :] = dv
            dq = dq + dot(kv[c : c + chunk, :], ds, ((0,), (0,)))
    dq_all[...] = (factor * dq).T.astype(BF16)
    for s in range(n_groups):
        dq_outs[s][...] = dq_all[s * rows : (s + 1) * rows, :]


def backward(head, count, q, blocks, part, probs, out, inverse, grad_attn, n_groups):
    n_q = q.shape[0]
    rows = n_q // n_groups
    seq_len = part * len(blocks)
    chunk = part if part <= 640 else math.gcd(part, 512)
    per_half = max(1, len(blocks) // 2)
    column = pl.BlockSpec((n_q, HD), lambda i: (0, head + i))
    results = pl.pallas_call(
        functools.partial(backward_kernel, n_groups, chunk, 1.0 / math.sqrt(HD)),
        grid=(count,),
        out_shape=[jax.ShapeDtypeStruct((rows, count * HD), BF16)] * n_groups
        + [jax.ShapeDtypeStruct((per_half * 2 * part, count * HD), BF16)] * 2,
        in_specs=[
            column,
            pl.BlockSpec((1, seq_len, n_q), lambda i: (head + i, 0, 0)),
            column,
            pl.BlockSpec((1, 1, n_q), lambda i: (head + i, 0, 0)),
            column,
        ]
        + [pl.BlockSpec((2 * part, HD), lambda i: (0, head + i))] * len(blocks),
        out_specs=[pl.BlockSpec((rows, HD), lambda i: (0, i))] * n_groups
        + [pl.BlockSpec((per_half * 2 * part, HD), lambda i: (0, i))] * 2,
        scratch_shapes=[pltpu.VMEM((n_q, HD), BF16)],
        compiler_params=params(),
        cost_estimate=pl.CostEstimate(
            flops=n_q * HD,
            bytes_accessed=2 * n_q * HD,
            transcendentals=0,
        ),
        name="backward",
    )(q, probs, out, inverse, grad_attn, *blocks)
    return results[:n_groups], results[n_groups:]


def frame_block(ids, sign, s, position, n_groups, n_tok):
    group = lax.rem(ids[0] + sign * s + n_groups, n_groups)
    return group * n_tok + jnp.bitwise_xor(ids[1], relative_of(position, bits_of(n_tok)))


def tokens_of(ids, tokens, grads, n_groups, n_space):
    rows, part = grads[0].shape
    for r in range(n_space):
        for s in range(n_groups):
            tokens[s * rows : (s + 1) * rows, :] = grads[r * n_groups + s][...]
        start = jnp.bitwise_xor(ids[2], relative_of(r, bits_of(n_space))) * part
        yield tokens[...], pl.ds(aligned(start, 16), part)


def attn_kernel(n_groups, n_tok, n_space, ids, *refs):
    blocks, grads = refs[:n_tok], refs[n_tok : n_tok + n_groups * n_space]
    grad_attn, weight, tokens = refs[n_tok + n_groups * n_space :]
    depth = weight.shape[0] // (n_groups * n_tok)
    first = blocks[0].shape[0] - n_groups * depth
    for j in range(n_tok):
        for s in range(n_groups):
            place = frame_block(ids, -1, s, j, n_groups, n_tok) * depth
            at = first + s * depth
            weight[pl.ds(aligned(place, 16), depth), :] = blocks[j][at : at + depth, :]
    total = None
    for block, here in tokens_of(ids, tokens, grads, n_groups, n_space):
        term = dot(block, weight[here, :], ((1,), (0,)))
        total = term if total is None else total + term
    grad_attn[...] = total.astype(BF16)


def projection_cost(n_q, gw):
    return pl.CostEstimate(
        flops=n_q * gw,
        bytes_accessed=2 * n_q * gw,
        transcendentals=0,
    )


def attn_gradient(ids, blocks, grads, depth, n_groups, n_tok, n_space):
    rows, part = grads[0].shape
    n_q, gw = rows * n_groups, blocks[0].shape[1]
    total = n_groups * n_tok * depth
    return whole_call(
        functools.partial(attn_kernel, n_groups, n_tok, n_space),
        jax.ShapeDtypeStruct((n_q, gw), BF16),
        (ids, *blocks, *grads),
        "attn_gradient",
        [pltpu.VMEM((total, gw), BF16), pltpu.VMEM((n_q, part), BF16)],
        projection_cost(n_q, gw),
    )


def proj_kernel(n_groups, n_tok, n_space, ids, attn, *refs):
    grads, (kept, sent, whole, tokens) = refs[: n_groups * n_space], refs[n_groups * n_space :]
    depth = whole.shape[0] // (n_groups * n_tok)
    for block, here in tokens_of(ids, tokens, grads, n_groups, n_space):
        whole[here, :] = dot(block, attn[...], ((0,), (0,))).astype(BF16)
    per_half = max(1, n_tok // 2)
    for j in range(n_tok):
        half = sent if j >= per_half else kept
        for s in range(n_groups):
            place = frame_block(ids, 1, s, j, n_groups, n_tok) * depth
            at = (j % per_half * n_groups + s) * depth
            half[at : at + depth, :] = whole[pl.ds(aligned(place, 16), depth), :]


def proj_gradient(ids, attn, grads, depth, n_groups, n_tok, n_space):
    n_q, gw = attn.shape
    part = grads[0].shape[1]
    half = n_groups * depth * max(1, n_tok // 2)
    total = n_groups * n_tok * depth
    return whole_call(
        functools.partial(proj_kernel, n_groups, n_tok, n_space),
        [jax.ShapeDtypeStruct((half, gw), BF16)] * 2,
        (ids, attn, *grads),
        "proj_gradient",
        [pltpu.VMEM((total, gw), BF16), pltpu.VMEM((n_q, part), BF16)],
        projection_cost(n_q, gw),
    )


def add_kernel(ids, kept, other, *outs):
    rows = outs[0].shape[0]
    for i, out in enumerate(outs):
        total = kept[i * rows : (i + 1) * rows, :].astype(F32)
        total = total + other[i * rows : (i + 1) * rows, :].astype(F32)
        out[...] = total.astype(BF16)


def add_parts(ids, kept, other, count):
    rows, gw = kept.shape
    shape = jax.ShapeDtypeStruct((rows // count, gw), BF16)
    return whole_call(add_kernel, [shape] * count, (ids, kept, other), "add_parts")


def halve(ids, kept, sent, n_frame, bits):
    for bit in bits[:-1]:
        other = lax.ppermute(sent, "frame", xor_pairs(n_frame, bit))
        kept, sent = add_parts(ids, kept, other, 2)
    return kept, sent


def finish_kernel(n_groups, ids, kept, other, *refs):
    dq, outs = refs[:n_groups], refs[n_groups:]
    rows = dq[0].shape[0]
    for s in range(n_groups):
        outs[s][:rows, :] = dq[s][...]
        for i in range(2):
            at = (i * n_groups + s) * rows
            total = kept[at : at + rows, :].astype(F32) + other[at : at + rows, :].astype(F32)
            outs[s][(i + 1) * rows : (i + 2) * rows, :] = total.astype(BF16)


def finish(ids, kept, other, dq, n_groups):
    rows, cols = dq[0].shape
    return whole_call(
        functools.partial(finish_kernel, n_groups),
        [jax.ShapeDtypeStruct((3 * rows, cols), BF16)] * n_groups,
        (ids, kept, other, *dq),
        "finish",
    )


def unpack_kernel(n_groups, widths, ids, *refs):
    pieces, outs = refs[:-3], refs[-3:]
    rows, gw = outs[0].shape[0], outs[0].shape[1] // n_groups
    before = 0
    for c, cols in enumerate(widths):
        for s in range(n_groups):
            start = lax.rem(ids[0] + s, n_groups) * gw + before
            for i, out in enumerate(outs):
                piece = pieces[c * n_groups + s][i * rows : (i + 1) * rows, :]
                out[:, pl.ds(aligned(start, HD), cols)] = piece
        before += cols


def unpack(ids, chunks, rows, gw, n_groups):
    widths = [HD, gw - HD][: len(chunks)]
    return whole_call(
        functools.partial(unpack_kernel, n_groups, widths),
        [jax.ShapeDtypeStruct((rows, gw * n_groups), BF16)] * 3,
        (ids, *[piece for pieces in chunks for piece in pieces]),
        "unpack",
    )


def join_kernel(n_groups, ids, *refs):
    pieces, out = refs[:n_groups], refs[n_groups]
    gw = pieces[0].shape[1]
    for s in range(n_groups):
        start = lax.rem(ids[0] - s + n_groups, n_groups) * gw
        out[:, pl.ds(aligned(start, HD), gw)] = pieces[s][...].astype(F32)


def join(ids, pieces, n_groups):
    rows, gw = pieces[0].shape
    return whole_call(
        functools.partial(join_kernel, n_groups),
        jax.ShapeDtypeStruct((rows, gw * n_groups), F32),
        (ids, *pieces),
        "join",
    )


def exchange(pieces, n_groups, n_tok, sign):
    return [pieces[0]] + [
        lax.ppermute(pieces[s], "frame", shift_pairs(n_groups, n_tok, sign * s))
        for s in range(1, n_groups)
    ]


def local(queries, keys, values, grad_out, proj_weight):
    n_frame = lax.axis_size("frame")
    n_space = lax.axis_size("space")
    rows, width = queries.shape
    gw = width // math.gcd(width // HD, n_frame)
    depth = proj_weight.shape[1]
    n_groups = math.gcd(width // HD, n_frame)
    n_tok = n_frame // n_groups
    tok_bits = bits_of(n_tok)
    space_bits = bits_of(n_space)
    heads = width // n_groups // HD
    shared = 2 * rows + depth
    frame = lax.axis_index("frame")
    ids = jnp.stack([frame // n_tok, frame % n_tok, lax.axis_index("space")]).astype(jnp.int32)

    tie = lax.optimization_barrier
    last = xor_pairs(n_frame, tok_bits[-1])

    *pieces, own_q = pack(ids, queries, keys, values, proj_weight.T, n_groups)
    pieces = exchange(pieces, n_groups, n_tok, 1)
    q_pieces = pieces[1:]
    own, others, ring, across = [pieces[0]], [], grad_out, []
    for s in range(n_groups):
        others.append(lax.ppermute(own[s], "frame", last))
        across.append(gather_blocks(ring, "space", n_space, space_bits))
        if s + 1 < n_groups:
            ring = lax.ppermute(ring, "frame", shift_pairs(n_groups, n_tok, 1))
            step = (ring, pieces[s + 1][:shared], others[s], *across[s])
            ring, piece, others[s], *across[s] = tie(step)
            own.append(piece)

    q = stack_queries(ids, own_q, q_pieces)
    blocks = [stack(ids, own, rows), stack(ids, others, rows)]
    for bit in reversed(tok_bits[:-1]):
        blocks = blocks + [lax.ppermute(b, "frame", xor_pairs(n_frame, bit)) for b in blocks]
    part = n_groups * rows
    probs, out, inverse = forward(q, blocks, part)
    grads = [across[s][r] for r in range(n_space) for s in range(n_groups)]
    grad_attn = attn_gradient(ids, blocks, grads, depth, n_groups, n_tok, n_space)

    def attention_halves(head, count, q):
        return backward(head, count, q, blocks, part, probs, out, inverse, grad_attn, n_groups)

    def across_x(piece):
        return lax.ppermute(piece, "frame", last)

    dq, halves = attention_halves(0, 1, q)
    kept, sent = halve(ids, *halves, n_frame, tok_bits)
    q, kept, sent = tie((q, kept, sent))
    other = across_x(sent)
    if heads > 1:
        dq_rest, halves = attention_halves(1, heads - 1, q)
        other, *halves = tie((other, *halves))
    sums = finish(ids, kept, other, dq, n_groups)
    returned = [exchange(sums, n_groups, n_tok, -1)]
    out_after, *_ = tie((out, *sums))
    proj = proj_gradient(ids, out_after, grads, depth, n_groups, n_tok, n_space)
    if heads > 1:
        kept, sent = halve(ids, *halves, n_frame, tok_bits)
        other = across_x(sent)
    proj_kept, proj_sent = halve(ids, *proj, n_frame, tok_bits)
    if heads > 1:
        step = (other, proj_kept, proj_sent, *returned[0][1:])
        other, proj_kept, proj_sent, *returned[0][1:] = tie(step)
        sums = finish(ids, kept, other, dq_rest, n_groups)
        returned.append(exchange(sums, n_groups, n_tok, -1))
    proj = add_parts(ids, proj_kept, across_x(proj_sent), n_groups)
    proj_pieces = exchange(proj, n_groups, n_tok, 1)
    grad_proj = join(ids, proj_pieces, n_groups).T
    grad_queries, grad_keys, grad_values = unpack(ids, returned, rows, gw, n_groups)
    return (grad_queries, grad_keys, grad_values, grad_proj)


def solution(mesh):
    in_specs = (
        P("frame", "space"),
        P("frame", "space"),
        P("frame", "space"),
        P("frame", "space"),
        P("space", "frame"),
    )
    out_specs = (P("frame", "space"), P("frame", "space"), P("frame", "space"), P("space", "frame"))
    return jax.shard_map(local, mesh=mesh, in_specs=in_specs, out_specs=out_specs, check_vma=False)
```

```python
import functools
import math

import jax
import jax.numpy as jnp
from jax import lax
from jax.experimental import pallas as pl
from jax.experimental.pallas import tpu as pltpu
from jax.sharding import PartitionSpec as P

HD = 128
VMEM_BYTES = 24 * 1024 * 1024
BF16 = jnp.bfloat16
F32 = jnp.float32


def bits_of(count):
    found = []
    bit = 1
    while bit < count:
        found.append(bit)
        bit *= 2
    return found


def relative_of(position, bits):
    total = 0
    for place, bit in enumerate(reversed(bits)):
        if position >> place & 1:
            total |= bit
    return total


def shift_pairs(n_groups, n_tok, step):
    return [
        (g * n_tok + t, (g + step) % n_groups * n_tok + t)
        for g in range(n_groups)
        for t in range(n_tok)
    ]


def xor_pairs(count, bit):
    return [(i, i ^ bit) for i in range(count)]


def gather_blocks(block, axis, count, bits):
    blocks = [block]
    for bit in reversed(bits):
        blocks = blocks + [lax.ppermute(b, axis, xor_pairs(count, bit)) for b in blocks]
    return blocks


def params():
    return pltpu.CompilerParams(vmem_limit_bytes=VMEM_BYTES)


def smem():
    return pl.BlockSpec(memory_space=pltpu.SMEM)


def vmem():
    return pl.BlockSpec(memory_space=pltpu.VMEM)


def aligned(value, unit):
    return pl.multiple_of(value, unit)


def dot(a, b, dims):
    return lax.dot_general(a, b, (dims, ((), ())), preferred_element_type=F32)


def whole_call(body, out_shape, args, name, scratch=(), cost=None):
    single = not isinstance(out_shape, list)
    return pl.pallas_call(
        body,
        out_shape=out_shape,
        in_specs=[smem()] + [vmem()] * (len(args) - 1),
        out_specs=vmem() if single else [vmem()] * len(out_shape),
        scratch_shapes=list(scratch),
        compiler_params=params(),
        cost_estimate=cost,
        name=name,
    )(*args)


def pack_kernel(n_groups, ids, q, k, v, w, *refs):
    outs, sems = refs[:-1], refs[-1]
    rows, depth = q.shape[0], w.shape[0]
    gw = q.shape[1] // n_groups
    copies = []
    for s in range(n_groups):
        cols = pl.ds(aligned(lax.rem(ids[0] + s, n_groups) * gw, HD), gw)
        own = outs[n_groups] if s == 0 else outs[s].at[pl.ds(2 * rows + depth, rows), :]
        for source, target in (
            (k, outs[s].at[pl.ds(0, rows), :]),
            (v, outs[s].at[pl.ds(rows, rows), :]),
            (w, outs[s].at[pl.ds(2 * rows, depth), :]),
            (q, own),
        ):
            copies.append(
                pltpu.make_async_copy(source.at[:, cols], target, sems.at[len(copies)])
            )
    for copy in copies:
        copy.start()
    for copy in copies:
        copy.wait()


def pack(ids, q, k, v, w, n_groups):
    rows, width = q.shape
    gw = width // n_groups
    shared = 2 * rows + w.shape[0]
    shapes = (
        [jax.ShapeDtypeStruct((shared, gw), BF16)]
        + [jax.ShapeDtypeStruct((shared + rows, gw), BF16)] * (n_groups - 1)
        + [jax.ShapeDtypeStruct((rows, gw), BF16)]
    )
    return pl.pallas_call(
        functools.partial(pack_kernel, n_groups),
        out_shape=shapes,
        in_specs=[smem()] + [pl.BlockSpec(memory_space=pltpu.HBM)] * 4,
        out_specs=[vmem()] * len(shapes),
        scratch_shapes=[pltpu.SemaphoreType.DMA((4 * n_groups,))],
        compiler_params=pltpu.CompilerParams(vmem_limit_bytes=60 * 1024 * 1024),
        name="pack",
    )(ids, q, k, v, w)


def stack_kernel(n_groups, rows, ids, *refs):
    pieces, out = refs[:n_groups], refs[n_groups]
    shared = out.shape[0] // n_groups
    depth = shared - 2 * rows
    for s, piece in enumerate(pieces):
        for i in range(2):
            at = (i * n_groups + s) * rows
            out[at : at + rows, :] = piece[i * rows : (i + 1) * rows, :]
        at = 2 * n_groups * rows + s * depth
        out[at : at + depth, :] = piece[2 * rows : shared, :]


def stack(ids, pieces, rows):
    shared, gw = pieces[0].shape
    return whole_call(
        functools.partial(stack_kernel, len(pieces), rows),
        jax.ShapeDtypeStruct((shared * len(pieces), gw), BF16),
        (ids, *pieces),
        "stack",
    )


def stack_queries_kernel(ids, own, *refs):
    pieces, out = refs[:-1], refs[-1]
    rows = own.shape[0]
    out[:rows, :] = own[...]
    for s, piece in enumerate(pieces):
        out[(s + 1) * rows : (s + 2) * rows, :] = piece[piece.shape[0] - rows :, :]


def stack_queries(ids, own, pieces):
    rows, gw = own.shape
    shape = jax.ShapeDtypeStruct((rows * (len(pieces) + 1), gw), BF16)
    return whole_call(stack_queries_kernel, shape, (ids, own, *pieces), "stack_queries")


def forward_kernel(chunk, scale, q_in, *refs):
    blocks, (p_out, o_out, il_out, logits) = refs[:-4], refs[-4:]
    part = blocks[0].shape[0] // 2
    q = q_in[...]
    top = None
    for j, kv in enumerate(blocks):
        for c in range(0, part, chunk):
            at = j * part + c
            block = dot(kv[c : c + chunk, :], q, ((1,), (1,)))
            logits[at : at + chunk, :] = block
            here = jnp.max(block, axis=0, keepdims=True)
            top = here if top is None else jnp.maximum(top, here)
    top = top * scale
    total = jnp.zeros_like(top)
    out = jnp.zeros((HD, q.shape[0]), F32)
    for j, kv in enumerate(blocks):
        for c in range(0, part, chunk):
            at = j * part + c
            prob = jnp.exp2(logits[at : at + chunk, :] * scale - top)
            total = total + jnp.sum(prob, axis=0, keepdims=True)
            low = prob.astype(BF16)
            p_out[0, at : at + chunk, :] = low
            out = out + dot(kv[part + c : part + c + chunk, :], low, ((0,), (0,)))
    inverse = 1.0 / total
    il_out[0] = inverse
    o_out[...] = (out * inverse).T.astype(BF16)


def forward(q, blocks, part):
    n_q, gw = q.shape
    heads = gw // HD
    seq_len = part * len(blocks)
    chunk = part if part <= 640 else math.gcd(part, 512)
    scale = math.log2(math.e) / math.sqrt(HD)
    return pl.pallas_call(
        functools.partial(forward_kernel, chunk, scale),
        grid=(heads,),
        out_shape=[
            jax.ShapeDtypeStruct((heads, seq_len, n_q), BF16),
            jax.ShapeDtypeStruct((n_q, gw), BF16),
            jax.ShapeDtypeStruct((heads, 1, n_q), F32),
        ],
        in_specs=[pl.BlockSpec((n_q, HD), lambda h: (0, h))]
        + [pl.BlockSpec((2 * part, HD), lambda h: (0, h))] * len(blocks),
        out_specs=[
            pl.BlockSpec((1, seq_len, n_q), lambda h: (h, 0, 0)),
            pl.BlockSpec((n_q, HD), lambda h: (0, h)),
            pl.BlockSpec((1, 1, n_q), lambda h: (h, 0, 0)),
        ],
        scratch_shapes=[pltpu.VMEM((seq_len, n_q), F32)],
        compiler_params=params(),
        cost_estimate=pl.CostEstimate(
            flops=4 * heads * seq_len * n_q * HD,
            bytes_accessed=2 * heads * seq_len * n_q,
            transcendentals=heads * seq_len * n_q,
        ),
        name="forward",
    )(q, *blocks)


def backward_kernel(n_groups, chunk, factor, *refs):
    q_in, p_in, o_in, il_in, da_in = refs[:5]
    dq_outs, halves, dq_all = refs[-n_groups - 3 : -3], refs[-3:-1], refs[-1]
    blocks = refs[5 : -n_groups - 3]
    part = blocks[0].shape[0] // 2
    rows = dq_outs[0].shape[0]
    q = q_in[...]
    n_q = q.shape[0]
    inverse = jnp.broadcast_to(il_in[0], (HD, n_q)).T
    da = (da_in[...].astype(F32) * inverse).astype(BF16)
    delta = jnp.sum((da.astype(F32) * o_in[...].astype(F32)).T, axis=0, keepdims=True)
    dq = jnp.zeros((HD, n_q), F32)
    per_half = max(1, len(blocks) // 2)
    for j, kv in enumerate(blocks):
        out = halves[j // per_half]
        base = j % per_half * 2 * part
        for c in range(0, part, chunk):
            at = j * part + c
            low = p_in[0, at : at + chunk, :]
            dp = dot(kv[part + c : part + c + chunk, :], da, ((1,), (1,)))
            ds = (low.astype(F32) * (dp - delta)).astype(BF16)
            dk = (factor * dot(ds, q, ((1,), (0,)))).astype(BF16)
            out[base + c : base + c + chunk, :] = dk
            dv = dot(low, da, ((1,), (0,))).astype(BF16)
            out[base + part + c : base + part + c + chunk, :] = dv
            dq = dq + dot(kv[c : c + chunk, :], ds, ((0,), (0,)))
    dq_all[...] = (factor * dq).T.astype(BF16)
    for s in range(n_groups):
        dq_outs[s][...] = dq_all[s * rows : (s + 1) * rows, :]


def backward(head, count, q, blocks, part, probs, out, inverse, grad_attn, n_groups):
    n_q = q.shape[0]
    rows = n_q // n_groups
    seq_len = part * len(blocks)
    chunk = part if part <= 640 else math.gcd(part, 512)
    per_half = max(1, len(blocks) // 2)
    column = pl.BlockSpec((n_q, HD), lambda i: (0, head + i))
    results = pl.pallas_call(
        functools.partial(backward_kernel, n_groups, chunk, 1.0 / math.sqrt(HD)),
        grid=(count,),
        out_shape=[jax.ShapeDtypeStruct((rows, count * HD), BF16)] * n_groups
        + [jax.ShapeDtypeStruct((per_half * 2 * part, count * HD), BF16)] * 2,
        in_specs=[
            column,
            pl.BlockSpec((1, seq_len, n_q), lambda i: (head + i, 0, 0)),
            column,
            pl.BlockSpec((1, 1, n_q), lambda i: (head + i, 0, 0)),
            column,
        ]
        + [pl.BlockSpec((2 * part, HD), lambda i: (0, head + i))] * len(blocks),
        out_specs=[pl.BlockSpec((rows, HD), lambda i: (0, i))] * n_groups
        + [pl.BlockSpec((per_half * 2 * part, HD), lambda i: (0, i))] * 2,
        scratch_shapes=[pltpu.VMEM((n_q, HD), BF16)],
        compiler_params=params(),
        cost_estimate=pl.CostEstimate(
            flops=n_q * HD,
            bytes_accessed=2 * n_q * HD,
            transcendentals=0,
        ),
        name="backward",
    )(q, probs, out, inverse, grad_attn, *blocks)
    return results[:n_groups], results[n_groups:]


def frame_block(ids, sign, s, position, n_groups, n_tok):
    group = lax.rem(ids[0] + sign * s + n_groups, n_groups)
    return group * n_tok + jnp.bitwise_xor(ids[1], relative_of(position, bits_of(n_tok)))


def tokens_of(ids, tokens, grads, n_groups, n_space):
    rows, part = grads[0].shape
    for r in range(n_space):
        for s in range(n_groups):
            tokens[s * rows : (s + 1) * rows, :] = grads[r * n_groups + s][...]
        start = jnp.bitwise_xor(ids[2], relative_of(r, bits_of(n_space))) * part
        yield tokens[...], pl.ds(aligned(start, 16), part)


def attn_kernel(n_groups, n_tok, n_space, ids, *refs):
    blocks, grads = refs[:n_tok], refs[n_tok : n_tok + n_groups * n_space]
    grad_attn, weight, tokens = refs[n_tok + n_groups * n_space :]
    depth = weight.shape[0] // (n_groups * n_tok)
    first = blocks[0].shape[0] - n_groups * depth
    for j in range(n_tok):
        for s in range(n_groups):
            place = frame_block(ids, -1, s, j, n_groups, n_tok) * depth
            at = first + s * depth
            weight[pl.ds(aligned(place, 16), depth), :] = blocks[j][at : at + depth, :]
    total = None
    for block, here in tokens_of(ids, tokens, grads, n_groups, n_space):
        term = dot(block, weight[here, :], ((1,), (0,)))
        total = term if total is None else total + term
    grad_attn[...] = total.astype(BF16)


def projection_cost(n_q, gw):
    return pl.CostEstimate(
        flops=n_q * gw,
        bytes_accessed=2 * n_q * gw,
        transcendentals=0,
    )


def attn_gradient(ids, blocks, grads, depth, n_groups, n_tok, n_space):
    rows, part = grads[0].shape
    n_q, gw = rows * n_groups, blocks[0].shape[1]
    total = n_groups * n_tok * depth
    return whole_call(
        functools.partial(attn_kernel, n_groups, n_tok, n_space),
        jax.ShapeDtypeStruct((n_q, gw), BF16),
        (ids, *blocks, *grads),
        "attn_gradient",
        [pltpu.VMEM((total, gw), BF16), pltpu.VMEM((n_q, part), BF16)],
        projection_cost(n_q, gw),
    )


def proj_kernel(n_groups, n_tok, n_space, ids, attn, *refs):
    grads, (kept, sent, whole, tokens) = refs[: n_groups * n_space], refs[n_groups * n_space :]
    depth = whole.shape[0] // (n_groups * n_tok)
    for block, here in tokens_of(ids, tokens, grads, n_groups, n_space):
        whole[here, :] = dot(block, attn[...], ((0,), (0,))).astype(BF16)
    per_half = max(1, n_tok // 2)
    for j in range(n_tok):
        half = sent if j >= per_half else kept
        for s in range(n_groups):
            place = frame_block(ids, 1, s, j, n_groups, n_tok) * depth
            at = (j % per_half * n_groups + s) * depth
            half[at : at + depth, :] = whole[pl.ds(aligned(place, 16), depth), :]


def proj_gradient(ids, attn, grads, depth, n_groups, n_tok, n_space):
    n_q, gw = attn.shape
    part = grads[0].shape[1]
    half = n_groups * depth * max(1, n_tok // 2)
    total = n_groups * n_tok * depth
    return whole_call(
        functools.partial(proj_kernel, n_groups, n_tok, n_space),
        [jax.ShapeDtypeStruct((half, gw), BF16)] * 2,
        (ids, attn, *grads),
        "proj_gradient",
        [pltpu.VMEM((total, gw), BF16), pltpu.VMEM((n_q, part), BF16)],
        projection_cost(n_q, gw),
    )


def add_kernel(ids, kept, other, *outs):
    rows = outs[0].shape[0]
    for i, out in enumerate(outs):
        total = kept[i * rows : (i + 1) * rows, :].astype(F32)
        total = total + other[i * rows : (i + 1) * rows, :].astype(F32)
        out[...] = total.astype(BF16)


def add_parts(ids, kept, other, count):
    rows, gw = kept.shape
    shape = jax.ShapeDtypeStruct((rows // count, gw), BF16)
    return whole_call(add_kernel, [shape] * count, (ids, kept, other), "add_parts")


def halve(ids, kept, sent, n_frame, bits):
    for bit in bits[:-1]:
        other = lax.ppermute(sent, "frame", xor_pairs(n_frame, bit))
        kept, sent = add_parts(ids, kept, other, 2)
    return kept, sent


def finish_kernel(n_groups, ids, kept, other, *refs):
    dq, outs = refs[:n_groups], refs[n_groups:]
    rows = dq[0].shape[0]
    for s in range(n_groups):
        outs[s][:rows, :] = dq[s][...]
        for i in range(2):
            at = (i * n_groups + s) * rows
            total = kept[at : at + rows, :].astype(F32) + other[at : at + rows, :].astype(F32)
            outs[s][(i + 1) * rows : (i + 2) * rows, :] = total.astype(BF16)


def finish(ids, kept, other, dq, n_groups):
    rows, cols = dq[0].shape
    return whole_call(
        functools.partial(finish_kernel, n_groups),
        [jax.ShapeDtypeStruct((3 * rows, cols), BF16)] * n_groups,
        (ids, kept, other, *dq),
        "finish",
    )


def unpack_kernel(n_groups, widths, ids, *refs):
    pieces, outs = refs[:-3], refs[-3:]
    rows, gw = outs[0].shape[0], outs[0].shape[1] // n_groups
    before = 0
    for c, cols in enumerate(widths):
        for s in range(n_groups):
            start = lax.rem(ids[0] + s, n_groups) * gw + before
            for i, out in enumerate(outs):
                piece = pieces[c * n_groups + s][i * rows : (i + 1) * rows, :]
                out[:, pl.ds(aligned(start, HD), cols)] = piece
        before += cols


def unpack(ids, chunks, rows, gw, n_groups):
    widths = [max(HD, gw - HD), HD][: len(chunks)]
    return whole_call(
        functools.partial(unpack_kernel, n_groups, widths),
        [jax.ShapeDtypeStruct((rows, gw * n_groups), BF16)] * 3,
        (ids, *[piece for pieces in chunks for piece in pieces]),
        "unpack",
    )


def join_kernel(n_groups, ids, *refs):
    pieces, out = refs[:n_groups], refs[n_groups]
    gw = pieces[0].shape[1]
    for s in range(n_groups):
        start = lax.rem(ids[0] - s + n_groups, n_groups) * gw
        out[:, pl.ds(aligned(start, HD), gw)] = pieces[s][...].astype(F32)


def join(ids, pieces, n_groups):
    rows, gw = pieces[0].shape
    return whole_call(
        functools.partial(join_kernel, n_groups),
        jax.ShapeDtypeStruct((rows, gw * n_groups), F32),
        (ids, *pieces),
        "join",
    )


def exchange(pieces, n_groups, n_tok, sign):
    return [pieces[0]] + [
        lax.ppermute(pieces[s], "frame", shift_pairs(n_groups, n_tok, sign * s))
        for s in range(1, n_groups)
    ]


def local(queries, keys, values, grad_out, proj_weight):
    n_frame = lax.axis_size("frame")
    n_space = lax.axis_size("space")
    rows, width = queries.shape
    gw = width // math.gcd(width // HD, n_frame)
    depth = proj_weight.shape[1]
    n_groups = math.gcd(width // HD, n_frame)
    n_tok = n_frame // n_groups
    tok_bits = bits_of(n_tok)
    space_bits = bits_of(n_space)
    heads = width // n_groups // HD
    shared = 2 * rows + depth
    frame = lax.axis_index("frame")
    ids = jnp.stack([frame // n_tok, frame % n_tok, lax.axis_index("space")]).astype(jnp.int32)

    tie = lax.optimization_barrier
    last = xor_pairs(n_frame, tok_bits[-1])

    *pieces, own_q = pack(ids, queries, keys, values, proj_weight.T, n_groups)
    pieces = exchange(pieces, n_groups, n_tok, 1)
    q_pieces = pieces[1:]
    own, others, ring, across = [pieces[0]], [], grad_out, []
    for s in range(n_groups):
        others.append(lax.ppermute(own[s], "frame", last))
        across.append(gather_blocks(ring, "space", n_space, space_bits))
        if s + 1 < n_groups:
            ring = lax.ppermute(ring, "frame", shift_pairs(n_groups, n_tok, 1))
            step = (ring, pieces[s + 1][:shared], others[s], *across[s])
            ring, piece, others[s], *across[s] = tie(step)
            own.append(piece)

    q = stack_queries(ids, own_q, q_pieces)
    blocks = [stack(ids, own, rows), stack(ids, others, rows)]
    for bit in reversed(tok_bits[:-1]):
        blocks = blocks + [lax.ppermute(b, "frame", xor_pairs(n_frame, bit)) for b in blocks]
    part = n_groups * rows
    probs, out, inverse = forward(q, blocks, part)
    grads = [across[s][r] for r in range(n_space) for s in range(n_groups)]
    grad_attn = attn_gradient(ids, blocks, grads, depth, n_groups, n_tok, n_space)

    def attention_halves(head, count, q):
        return backward(head, count, q, blocks, part, probs, out, inverse, grad_attn, n_groups)

    def across_x(piece):
        return lax.ppermute(piece, "frame", last)

    dq, halves = attention_halves(0, max(1, heads - 1), q)
    kept, sent = halve(ids, *halves, n_frame, tok_bits)
    q, kept, sent = tie((q, kept, sent))
    other = across_x(sent)
    if heads > 1:
        dq_rest, halves = attention_halves(heads - 1, 1, q)
        other, *halves = tie((other, *halves))
    sums = finish(ids, kept, other, dq, n_groups)
    returned = [exchange(sums, n_groups, n_tok, -1)]
    out_after, *_ = tie((out, *sums))
    proj = proj_gradient(ids, out_after, grads, depth, n_groups, n_tok, n_space)
    if heads > 1:
        kept, sent = halve(ids, *halves, n_frame, tok_bits)
        other = across_x(sent)
    proj_kept, proj_sent = halve(ids, *proj, n_frame, tok_bits)
    if heads > 1:
        step = (other, proj_kept, proj_sent, *returned[0][1:])
        other, proj_kept, proj_sent, *returned[0][1:] = tie(step)
        sums = finish(ids, kept, other, dq_rest, n_groups)
        returned.append(exchange(sums, n_groups, n_tok, -1))
    proj = add_parts(ids, proj_kept, across_x(proj_sent), n_groups)
    proj_pieces = exchange(proj, n_groups, n_tok, 1)
    grad_proj = join(ids, proj_pieces, n_groups).T
    grad_queries, grad_keys, grad_values = unpack(ids, returned, rows, gw, n_groups)
    return (grad_queries, grad_keys, grad_values, grad_proj)


def solution(mesh):
    in_specs = (
        P("frame", "space"),
        P("frame", "space"),
        P("frame", "space"),
        P("frame", "space"),
        P("space", "frame"),
    )
    out_specs = (P("frame", "space"), P("frame", "space"), P("frame", "space"), P("space", "frame"))
    return jax.shard_map(local, mesh=mesh, in_specs=in_specs, out_specs=out_specs, check_vma=False)
```
